256 devices in a mesh: gx: 32 (over z, y), gy: 4 (over x), gz: 2 (over core).
Axes of the slice: x: 4, y: 4, z: 8, core: 2. Of those that a mesh axis runs over, the one named last changes fastest.
Arguments:
- adjoint: float32 [22, 512, 32, 256], P(None, 'gx', 'gy', 'gz'), may hold values from -6 to 6
- log_conc: bfloat16 [32, 512, 32, 256], P(None, 'gx', 'gy', 'gz'), may hold values from -3 to 3
- levels: int32 [512, 32, 256], P('gx', 'gy', 'gz'), may hold values from 0 to 3, as said below
- conduct: float32 [512, 32, 256], P('gx', 'gy', 'gz'), may hold values from 6 to 20
- orders_fwd: bfloat16 [206, 32], replicated, may hold values from -1 to 1
- orders_rev: bfloat16 [206, 32], replicated, may hold values from -1 to 1
- stoich: bfloat16 [206, 22], replicated, may hold values from -1.25 to 1.25
- rate_fwd: float32 [206], replicated, may hold values from 0.1 to 1
- rate_rev: float32 [206], replicated, may hold values from 0.1 to 1
- diffusivity: float32 [22], replicated, may hold values from 0.1 to 1
Outputs:
- adjoint_next: float32 [22, 512, 32, 256], P(None, 'gx', 'gy', 'gz')
The draws below stay inside these ranges and needn't reach their ends.
Inputs may be any that keep to these rules, and one draw needn't show every extreme that they name: `levels`: within each aligned block of 4 x-cells by 8 y-rows and all z, some cell holds the block's highest level.
All inputs are finite; a program needn't handle non-finite values.
Results may differ from the reference program's by a relative error of at most 0.0054.
Values sent between devices are 32-bit elements; how exact they have to be, the bound alone decides.
No kernel may reach another device: no remote copies, remote signals or barrier semaphores. Data moves between devices by JAX's collectives and lax.ppermute only.
A program may use at most 128 MiB of HBM per device.

```python
import math
import jax
import jax.numpy as jnp
from jax import lax

CARRIED = 22
SPECIES = 32
REACT = 206
XBAND = 4
YBAND = 8
NX = 512
NY = 32
NZ = 256


def draw_levels(key, part):
    key = jax.random.fold_in(key, 7)
    band_key, cell_key = jax.random.split(key)
    band_top = jax.random.randint(band_key, (NX // XBAND, NY // YBAND, 1), 0, 4)
    band_full = jnp.repeat(jnp.repeat(band_top, XBAND, axis=0), YBAND, axis=1)
    band_full = jnp.broadcast_to(band_full, (NX, NY, NZ))
    cell_levels = jax.random.randint(cell_key, (NX, NY, NZ), 0, band_full + 1)
    x_index = lax.broadcasted_iota(jnp.int32, (NX, NY, NZ), 0)
    y_index = lax.broadcasted_iota(jnp.int32, (NX, NY, NZ), 1)
    z_index = lax.broadcasted_iota(jnp.int32, (NX, NY, NZ), 2)
    corner_mask = (x_index % XBAND == 0) & (y_index % YBAND == 0) & (z_index == 0)
    return jnp.where(corner_mask, band_full, cell_levels).astype(jnp.int32)


def draw_adjoint(key, part):
    key = jax.random.fold_in(key, 11)
    rough_key, line_key, phase_key = jax.random.split(key, 3)
    full_shape = (CARRIED, NX, NY, NZ)
    line_shape = (CARRIED, 1, NY, NZ)
    x_pos = lax.broadcasted_iota(jnp.float32, (1, NX, 1, 1), 1) / NX
    phase = jax.random.uniform(phase_key, line_shape, jnp.float32, 0.0, 2.0 * math.pi)
    wave = jnp.cos(2.0 * math.pi * x_pos + phase)
    rough = jnp.clip(jax.random.normal(rough_key, full_shape, jnp.float32), -5.0, 5.0)
    level = 0.2 * jnp.clip(jax.random.normal(line_key, line_shape, jnp.float32), -3.0, 3.0)
    smooth = level + 0.1 * wave
    return (rough + smooth).astype(jnp.float32)


def steps_of(rng, extent, cuts, least, largest):
    loudness, own = 1.0, jax.random.fold_in(rng, 6)
    for position, blocks in cuts:
        heights = jnp.exp(jax.random.uniform(jax.random.fold_in(own, position), (blocks,), jnp.float32, least / len(cuts), largest / len(cuts)))
        loudness = loudness * jnp.repeat(heights, extent[position] // blocks).reshape([-1 if axis == position else 1 for axis in range(len(extent))])
    return loudness


def gaussian(own_key, dims, spread, most, shards=(), kind=jnp.bfloat16):
    level = steps_of(own_key, dims, shards, -0.22, 0.18) if shards else 1.0
    values = jax.random.normal(own_key, dims, jnp.float32) * spread * level
    return jnp.minimum(jnp.maximum(values, -most), most).astype(kind)


def setup_inputs(seed: int = 0) -> dict:
    arg_keys = jax.random.split(jax.random.key(seed), 11)
    return {
        "adjoint": draw_adjoint(jax.random.fold_in(arg_keys[10], 71), 0),
        "log_conc": gaussian(arg_keys[1], (SPECIES, NX, NY, NZ), 0.5, 3.0, ((1, 32), (2, 4), (3, 2))),
        "levels": draw_levels(jax.random.fold_in(arg_keys[10], 71), 0),
        "conduct": jnp.clip(jnp.exp(math.log(20.0) - 1.2039728 * jax.random.uniform(arg_keys[3], (NX, NY, NZ), jnp.float32) ** steps_of(arg_keys[3], (NX, NY, NZ), ((0, 32), (1, 4), (2, 2)), -0.2, 0.2)), 6.0, 20.0),
        "orders_fwd": gaussian(arg_keys[4], (REACT, SPECIES), SPECIES ** -0.5, 1.0),
        "orders_rev": gaussian(arg_keys[5], (REACT, SPECIES), SPECIES ** -0.5, 1.0),
        "stoich": gaussian(arg_keys[6], (REACT, CARRIED), CARRIED ** -0.5, 1.25),
        "rate_fwd": jnp.clip(jnp.exp(jax.random.uniform(arg_keys[7], (REACT,), jnp.float32, math.log(0.1), math.log(1.0))), 0.1, 1.0),
        "rate_rev": jnp.clip(jnp.exp(jax.random.uniform(arg_keys[8], (REACT,), jnp.float32, math.log(0.1), math.log(1.0))), 0.1, 1.0),
        "diffusivity": jnp.clip(jnp.exp(jax.random.uniform(arg_keys[9], (CARRIED,), jnp.float32, math.log(0.1), math.log(1.0))), 0.1, 1.0),
    }


section_weight = 0.02
step_size = 0.3
mass_weight = 1e-3


def react_terms(operands, react_count):
    lam_flat, conc_flat, level_flat, orders_fwd, orders_rev, stoich, rate_fwd, rate_rev = operands
    carried = lam_flat.shape[0]
    fwd_orders = orders_fwd[:react_count]
    rev_orders = orders_rev[:react_count]
    tier_index = (4 * jnp.arange(react_count, dtype=jnp.int32)) // orders_fwd.shape[0]
    active = tier_index[:, None] <= level_flat[None, :]
    weight = jnp.dot(stoich[:react_count], lam_flat, preferred_element_type=jnp.float32)
    fwd_exp = jnp.dot(fwd_orders, conc_flat, preferred_element_type=jnp.float32)
    rev_exp = jnp.dot(rev_orders, conc_flat, preferred_element_type=jnp.float32)
    act_fwd = jnp.where(active, rate_fwd[:react_count, None] * jnp.exp(fwd_exp) * weight, 0.0).astype(jnp.bfloat16)
    act_rev = jnp.where(active, rate_rev[:react_count, None] * jnp.exp(rev_exp) * weight, 0.0).astype(jnp.bfloat16)
    gained = jnp.dot(fwd_orders[:, :carried].T, act_fwd, preferred_element_type=jnp.float32)
    lost = jnp.dot(rev_orders[:, :carried].T, act_rev, preferred_element_type=jnp.float32)
    return gained - lost


def second_y(padded, y_len):
    inner = padded[:, :, :, 2:-2]
    return (-inner[:, :, 0:y_len] + 16.0 * inner[:, :, 1:y_len + 1] - 30.0 * inner[:, :, 2:y_len + 2]
            + 16.0 * inner[:, :, 3:y_len + 3] - inner[:, :, 4:y_len + 4]) / 12.0


def second_z(padded, z_len):
    inner = padded[:, :, 2:-2, :]
    return (-inner[..., 0:z_len] + 16.0 * inner[..., 1:z_len + 1] - 30.0 * inner[..., 2:z_len + 2]
            + 16.0 * inner[..., 3:z_len + 3] - inner[..., 4:z_len + 4]) / 12.0


def reference(adjoint, log_conc, levels, conduct, orders_fwd, orders_rev, stoich, rate_fwd, rate_rev, diffusivity):
    carried, x_cells, y_cells, z_cells = adjoint.shape
    species = log_conc.shape[0]
    reactions = orders_fwd.shape[0]
    lam_low = adjoint.astype(jnp.bfloat16)

    def plane_terms(inputs):
        lam_plane, conc_plane, level_plane = inputs
        operands = (lam_plane.reshape(carried, y_cells * z_cells), conc_plane.reshape(species, y_cells * z_cells),
                    level_plane.reshape(y_cells * z_cells), orders_fwd, orders_rev, stoich, rate_fwd, rate_rev)
        return react_terms(operands, reactions).reshape(carried, y_cells, z_cells)

    chem = lax.map(plane_terms, (jnp.moveaxis(lam_low, 1, 0), jnp.moveaxis(log_conc, 1, 0), levels))
    chem = jnp.moveaxis(chem, 0, 1)
    padded = jnp.pad(adjoint, ((0, 0), (0, 0), (2, 2), (2, 2)))
    diffusion = diffusivity[:, None, None, None] * (second_y(padded, y_cells) + second_z(padded, z_cells))
    rhs = section_weight * (adjoint + step_size * (chem + diffusion))
    kappa_prev = jnp.concatenate([jnp.zeros((1, y_cells, z_cells), jnp.float32), conduct[:-1]], axis=0)
    lower = mass_weight / 3.0 - kappa_prev
    diag = mass_weight + kappa_prev + conduct
    upper = mass_weight / 3.0 - conduct

    def forward(carry, inputs):
        c_prev, d_prev = carry
        lower_cell, diag_cell, upper_cell, rhs_cell = inputs
        denom = diag_cell - lower_cell * c_prev
        c_next = upper_cell / denom
        d_next = (rhs_cell - lower_cell * d_prev) / denom
        return (c_next, d_next), (c_next, d_next)

    start = (jnp.zeros((y_cells, z_cells), jnp.float32), jnp.zeros((carried, y_cells, z_cells), jnp.float32))
    final_state, sweeps = lax.scan(forward, start, (lower, diag, upper, jnp.moveaxis(rhs, 1, 0)))

    def backward(w_next, inputs):
        c_cell, d_cell = inputs
        w_cell = d_cell - c_cell * w_next
        return w_cell, w_cell

    last_state, solved = lax.scan(backward, jnp.zeros((carried, y_cells, z_cells), jnp.float32), sweeps, reverse=True)
    return jnp.moveaxis(solved, 0, 1)
```

```python
import math

import jax
import jax.numpy as jnp
from jax import lax
from jax.experimental import pallas as pl
from jax.experimental.pallas import tpu as pltpu
from jax.sharding import PartitionSpec as P

SECTION = 0.02
STEP = 0.3
MASS = 0.001
LOG2E = math.log2(math.e)
OFF = -1024.0

K_ROWS = 96
R_PAD = 208
CHUNKS = ((0, 64), (64, 48), (112, 48), (160, 48))
TILE = 256
XB = 2
LIMIT = 12 * 1024 * 1024
F32 = jnp.float32
BF16 = jnp.bfloat16


def iota(shape, dim):
    return lax.broadcasted_iota(jnp.int32, shape, dim)


def dot(a, b):
    return lax.dot_general(a, b, (((1,), (0,)), ((), ())), preferred_element_type=F32)


def dot_nt(a, b):
    return lax.dot_general(a, b, (((1,), (1,)), ((), ())), preferred_element_type=F32)


def one_hot(mask):
    return jnp.where(mask, 1.0, 0.0).astype(BF16)


def build_weights(of_ref, or_ref, st_ref, rf_ref, rr_ref, wide_ref, w_ref, c_ref):
    species, react = of_ref.shape
    carried = st_ref.shape[0]
    eye = one_hot(iota((R_PAD, 256), 0) == iota((R_PAD, 256), 1))
    pick_row, pick_col = iota((32, 32), 0), iota((32, 32), 1)
    pick = one_hot(pick_col == jnp.where(pick_row < 16, pick_row, jnp.where(pick_row < 24, pick_row - 2, -1)))
    sub, tier = iota((8, 256), 0), 4 * iota((8, 256), 1) // react
    full = []
    for index, (orders, rate) in enumerate(((of_ref, rf_ref), (or_ref, rr_ref))):
        wide_ref[...] = jnp.zeros(wide_ref.shape, F32)
        wide_ref[0:species, 0:react] = orders[...].astype(F32)
        plain = wide_ref[0:32, :]
        sign = 1.0 if index == 0 else -1.0
        c_ref[index] = (sign * dot(pick, plain.astype(BF16)))[:, 0:R_PAD].astype(BF16)
        scaled = plain * LOG2E
        hi = scaled.astype(BF16).astype(F32)
        wide_ref[0:32, :] = hi
        wide_ref[32:64, :] = scaled - hi
        wide_ref[88:89, 0:react] = jnp.log(rate[...]) * LOG2E
        r = jnp.broadcast_to(wide_ref[88:89, :], (8, 256))
        r0 = r.astype(BF16).astype(F32)
        r1 = (r - r0).astype(BF16).astype(F32)
        parts = jnp.where(sub == 3, r0, jnp.where(sub == 4, r1, jnp.where(sub == 5, r - r0 - r1, 0.0)))
        wide_ref[88:96, :] = jnp.where(sub < 3, jnp.where(tier > sub, OFF, 0.0), parts)
        full.append(dot_nt(eye, wide_ref[...].astype(BF16)).astype(BF16))
    wide_ref[...] = jnp.zeros(wide_ref.shape, F32)
    wide_ref[64:80, 0:react] = st_ref[0:16, :].astype(F32)
    wide_ref[82 : 66 + carried, 0:react] = st_ref[16:carried, :].astype(F32)
    full.append(dot_nt(eye, wide_ref[...].astype(BF16)).astype(BF16))
    base = 0
    for start, size in CHUNKS:
        for part in full:
            w_ref[base : base + size, :] = part[start : start + size]
            base += size


def chem_kernel(
    adj_ref, conc_ref, lev_ref, of_ref, or_ref, st_ref, rf_ref, rr_ref, out_ref,
    wide_ref, w_ref, c_ref, conc32_ref, x_ref, act_ref,
):
    @pl.when(pl.program_id(0) == 0)
    def _():
        build_weights(of_ref, or_ref, st_ref, rf_ref, rr_ref, wide_ref, w_ref, c_ref)

    carried, xb, ny, nz = adj_ref.shape
    species = conc_ref.shape[0]
    adj_rows = adj_ref.reshape(carried * xb * ny, nz)
    out_rows = out_ref.reshape(carried * xb * ny, nz)
    pitch = xb * ny
    conc32_ref[...] = conc_ref[...].astype(F32).reshape(species * pitch, nz)
    sub = iota((8, nz), 0)
    for x in range(xb):
        for y in range(ny):
            row = x * ny + y
            cols = slice(y * nz, (y + 1) * nz)
            conc = jnp.concatenate(
                [conc32_ref[pl.ds(row + 8 * q * pitch, 8, stride=pitch), :] for q in range(4)], axis=0
            ).astype(BF16)
            x_ref[x, 0:32, cols] = conc
            x_ref[x, 32:64, cols] = conc
            lam = [adj_rows[pl.ds(row + first * pitch, 8, stride=pitch), :] for first in (0, 8, carried - 8)]
            level = jnp.broadcast_to(lev_ref[x, y : y + 1, :], (8, nz))
            marks = jnp.where(level <= sub, 1.0, 0.0)
            x_ref[x, 64:96, cols] = jnp.concatenate(lam + [marks], axis=0).astype(BF16)
    per_tile = TILE // nz
    for x in range(xb):
        for tile in range(ny // per_tile):
            slot = (x * (ny // per_tile) + tile) % act_ref.shape[0]
            data = x_ref[x, :, tile * TILE : (tile + 1) * TILE]
            base = 0
            for start, size in CHUNKS:
                got = dot(w_ref[base : base + 3 * size, :], data)
                base += 3 * size
                weight = got[2 * size :]
                act_ref[slot, 0, start : start + size, :] = (jnp.exp2(got[:size]) * weight).astype(BF16)
                act_ref[slot, 1, start : start + size, :] = (jnp.exp2(got[size : 2 * size]) * weight).astype(BF16)
            chem = dot(c_ref[0], act_ref[slot, 0]) + dot(c_ref[1], act_ref[slot, 1])
            for part in range(per_tile):
                row = x * ny + tile * per_tile + part
                for q, first in enumerate((0, 8, carried - 8)):
                    out_rows[pl.ds(row + first * pitch, 8, stride=pitch), :] = chem[
                        8 * q : 8 * q + 8, part * nz : (part + 1) * nz
                    ]


def chemistry(adjoint, log_conc, levels, orders_fwd, orders_rev, stoich, rate_fwd, rate_rev):
    carried, nx, ny, nz = adjoint.shape
    species, react = log_conc.shape[0], orders_fwd.shape[0]
    whole = lambda a: pl.BlockSpec(a.shape, lambda i: (0,) * len(a.shape))
    small = [orders_fwd.T, orders_rev.T, stoich.T, rate_fwd.reshape(1, react), rate_rev.reshape(1, react)]
    return pl.pallas_call(
        chem_kernel,
        grid=(nx // XB,),
        in_specs=[
            pl.BlockSpec((carried, XB, ny, nz), lambda i: (0, i, 0, 0)),
            pl.BlockSpec((species, XB, ny, nz), lambda i: (0, i, 0, 0)),
            pl.BlockSpec((XB, ny, nz), lambda i: (i, 0, 0)),
        ]
        + [whole(a) for a in small],
        out_specs=pl.BlockSpec((carried, XB, ny, nz), lambda i: (0, i, 0, 0)),
        out_shape=jax.ShapeDtypeStruct(adjoint.shape, F32),
        scratch_shapes=[
            pltpu.VMEM((K_ROWS, 256), F32),
            pltpu.VMEM((3 * R_PAD, K_ROWS), BF16),
            pltpu.VMEM((2, 32, R_PAD), BF16),
            pltpu.VMEM((species * XB * ny, nz), F32),
            pltpu.VMEM((XB, K_ROWS, ny * nz), BF16),
            pltpu.VMEM((4, 2, R_PAD, TILE), BF16),
        ],
        compiler_params=pltpu.CompilerParams(dimension_semantics=("arbitrary",), vmem_limit_bytes=LIMIT),
        cost_estimate=pl.CostEstimate(flops=12 * 10**9, bytes_accessed=4 * 10**6, transcendentals=6_750_000),
        name="chem",
    )(adjoint, log_conc, levels, *small)


GROUP = 6
GROUPS = 4
ROWS = 16
SB = 2
ANY = pl.BlockSpec(memory_space=pl.ANY)
WHOLE = pl.BlockSpec(memory_space=pltpu.VMEM)
SMALL = pltpu.CompilerParams(vmem_limit_bytes=LIMIT)


def place(s):
    return s // GROUP * ROWS + s % GROUP


def edges_kernel(adj_ref, low_ref, high_ref):
    carried, nx, ny, nz = adj_ref.shape

    @pl.loop(0, carried)
    def _(s):
        for x in range(nx):
            low_ref[s, x] = adj_ref[s, x, ny - 2 : ny, :]
            high_ref[s, x] = adj_ref[s, x, 0:2, :]


def edges(adjoint):
    carried, nx, ny, nz = adjoint.shape
    shape = pltpu.VMEM((carried, nx, 2, nz), F32)
    return pl.pallas_call(
        edges_kernel,
        in_specs=[WHOLE],
        out_specs=[WHOLE, WHOLE],
        out_shape=[shape, shape],
        compiler_params=SMALL,
        cost_estimate=pl.CostEstimate(flops=0, bytes_accessed=2 * 10**6, transcendentals=0),
        name="edges",
    )(adjoint)


def local_kernel(
    diff_ref, cond_ref, adj_ref, chem_ref, near_ref, low_ref, high_ref, part_ref, coef_ref, msg_ref, inv_ref
):
    nx, ny, nz = cond_ref.shape
    carried = adj_ref.shape[0]
    stride = GROUPS * ROWS
    third = MASS / 3.0
    body = MASS + 2.0 * third
    mass_first = jnp.where(lax.axis_index("gx") == 0, MASS + third, body) * jnp.ones((ny, nz), F32)
    gap = cond_ref[0] - third
    mass = jnp.full((ny, nz), body, F32)
    for p in range(1, nx - 1):
        after = cond_ref[p] - third
        inv = 1.0 / (gap + after + mass)
        alpha, beta = gap * inv, after * inv
        coef_ref[0, p], coef_ref[1, p], inv_ref[p] = alpha, beta, inv
        mass_first = mass_first + alpha * mass
        mass = body + beta * mass
        gap = alpha * after
    face = cond_ref[nx - 1] - third
    msg_ref[...] = jnp.zeros(msg_ref.shape, F32)
    for group in range(GROUPS):
        for r, value in ((6, gap), (7, mass_first), (14, face), (15, mass)):
            msg_ref[pl.ds(group * ROWS + r, ny, stride=stride), :] = value

    lane, row = iota((ny, nz), 1), iota((ny, nz), 0)
    keep_low = jnp.where(lax.axis_index("gz") == 0, 1.0, 0.0)
    keep_high = 1.0 - keep_low

    @pl.loop(0, carried)
    def _(s):
        scale = diff_ref[s] * (SECTION * STEP / 12.0)
        b_first, carry = None, None
        for p in range(nx):
            own = adj_ref[s, p]
            near = near_ref[s, p]
            from_high = near * keep_low
            from_low = near * keep_high
            z_up1 = pltpu.roll(jnp.where(lane < 1, from_high, own), nz - 1, 1)
            z_up2 = pltpu.roll(jnp.where(lane < 2, from_high, own), nz - 2, 1)
            z_dn1 = pltpu.roll(jnp.where(lane >= nz - 1, from_low, own), 1, 1)
            z_dn2 = pltpu.roll(jnp.where(lane >= nz - 2, from_low, own), 2, 1)
            low0, low1 = low_ref[s, p, 0:1, :], low_ref[s, p, 1:2, :]
            high0, high1 = high_ref[s, p, 0:1, :], high_ref[s, p, 1:2, :]
            y_up1 = jnp.where(row == ny - 1, high0, pltpu.roll(own, ny - 1, 0))
            y_up2 = jnp.where(row == ny - 1, high1, jnp.where(row == ny - 2, high0, pltpu.roll(own, ny - 2, 0)))
            y_dn1 = jnp.where(row == 0, low1, pltpu.roll(own, 1, 0))
            y_dn2 = jnp.where(row == 0, low0, jnp.where(row == 1, low1, pltpu.roll(own, 2, 0)))
            spread = 16.0 * ((z_up1 + z_dn1) + (y_up1 + y_dn1)) - ((z_up2 + z_dn2) + (y_up2 + y_dn2)) - 60.0 * own
            b = SECTION * own + (SECTION * STEP) * chem_ref[s, p] + scale * spread
            if p == 0:
                b_first = b
            elif p < nx - 1:
                full = b if carry is None else b + carry
                part_ref[s, p] = full * inv_ref[p]
                b_first = b_first + coef_ref[0, p] * full
                carry = coef_ref[1, p] * full
            else:
                b_last = b + carry
        msg_ref[pl.ds(place(s), ny, stride=stride), :] = b_first
        msg_ref[pl.ds(place(s) + 8, ny, stride=stride), :] = b_last


def local_part(diffusivity, adjoint, chem, near, low, high, conduct):
    carried, nx, ny, nz = adjoint.shape
    smem = pl.BlockSpec(memory_space=pltpu.SMEM)
    return pl.pallas_call(
        local_kernel,
        in_specs=[smem] + [WHOLE] * 6,
        out_specs=[WHOLE] * 3,
        out_shape=[
            pltpu.VMEM(adjoint.shape, F32),
            pltpu.VMEM((2, nx, ny, nz), F32),
            pltpu.VMEM((GROUPS * ny * ROWS, nz), F32),
        ],
        scratch_shapes=[pltpu.VMEM((nx, ny, nz), F32)],
        compiler_params=SMALL,
        cost_estimate=pl.CostEstimate(flops=20 * 10**6, bytes_accessed=7 * 10**6, transcendentals=0),
        name="local",
    )(diffusivity, conduct, adjoint, chem, near, low, high)


def chain_kernel(in_ref, out_ref):
    count, _, nz = in_ref.shape
    h, mass, rhs, ends = [], [], [], []
    passed_m = passed_b = None
    for i in range(count):
        low, high = in_ref[i, 0:8, :], in_ref[i, 8:16, :]
        g = jnp.broadcast_to(in_ref[i, 6:7, :], (8, nz))
        m_f = jnp.broadcast_to(in_ref[i, 7:8, :], (8, nz))
        face = jnp.broadcast_to(in_ref[i, 14:15, :], (8, nz))
        m_l = jnp.broadcast_to(in_ref[i, 15:16, :], (8, nz))
        inv = 1.0 / (g + face + m_l)
        a, c = g * inv, face * inv
        m, b = m_f + a * m_l, low + a * high
        if i > 0:
            m, b = m + passed_m, b + passed_b
        passed_m, passed_b = c * m_l, c * high
        h.append(a * face)
        mass.append(m)
        rhs.append(b)
        ends.append((a, c, high * inv))
    half = count // 2
    scale, ratio = [None] * count, [None] * count
    for i in range(half - 1):
        inv = 1.0 / (mass[i] + h[i])
        q = h[i] * inv
        scale[i], ratio[i] = rhs[i] * inv, q
        mass[i + 1] = mass[i + 1] + q * mass[i]
        rhs[i + 1] = rhs[i + 1] + q * rhs[i]
    mass[count - 1] = mass[count - 1] + h[count - 1]
    for i in range(count - 1, half, -1):
        inv = 1.0 / (mass[i] + h[i - 1])
        q = h[i - 1] * inv
        scale[i], ratio[i] = rhs[i] * inv, q
        mass[i - 1] = mass[i - 1] + q * mass[i]
        rhs[i - 1] = rhs[i - 1] + q * rhs[i]
    inv = 1.0 / (mass[half - 1] + h[half - 1])
    q = h[half - 1] * inv
    first = [None] * (count + 1)
    first[half] = (rhs[half] + q * rhs[half - 1]) / (mass[half] + q * mass[half - 1])
    first[half - 1] = rhs[half - 1] * inv + q * first[half]
    for i in range(half - 2, -1, -1):
        first[i] = scale[i] + ratio[i] * first[i + 1]
    for i in range(half + 1, count):
        first[i] = scale[i] + ratio[i] * first[i - 1]
    for i in range(count):
        a, c, part = ends[i]
        last = part + a * first[i]
        if i < count - 1:
            last = last + c * first[i + 1]
        out_ref[i, 0:8, :] = first[i]
        out_ref[i, 8:16, :] = last


def chain(message):
    return pl.pallas_call(
        chain_kernel,
        in_specs=[WHOLE],
        out_specs=WHOLE,
        out_shape=pltpu.VMEM(message.shape, F32),
        compiler_params=SMALL,
        cost_estimate=pl.CostEstimate(flops=10**6, bytes_accessed=10**6, transcendentals=0),
        name="chain",
    )(message)


def back_kernel(coef_ref, ends_ref, part_ref, out_hbm, out_ref, out_sem):
    carried, nx, ny, _ = part_ref.shape
    groups = carried // SB

    def put(g):
        return pltpu.make_async_copy(out_ref.at[pl.ds(g * SB, SB)], out_hbm.at[pl.ds(g * SB, SB)], out_sem.at[g])

    @pl.loop(0, groups)
    def _(g):
        for t in range(SB):
            s = g * SB + t
            first = ends_ref[pl.ds(place(s), ny, stride=GROUPS * ROWS), :]
            value = ends_ref[pl.ds(place(s) + 8, ny, stride=GROUPS * ROWS), :]
            out_ref[s, 0] = first
            out_ref[s, nx - 1] = value
            for p in range(nx - 2, 0, -1):
                value = part_ref[s, p] + coef_ref[0, p] * first + coef_ref[1, p] * value
                out_ref[s, p] = value
        put(g).start()

    @pl.loop(0, groups)
    def _(g):
        put(g).wait()


def back(part, coef, ends):
    groups = part.shape[0] // SB
    return pl.pallas_call(
        back_kernel,
        in_specs=[WHOLE, WHOLE, WHOLE],
        out_specs=ANY,
        out_shape=jax.ShapeDtypeStruct(part.shape, F32),
        scratch_shapes=[pltpu.VMEM(part.shape, F32), pltpu.SemaphoreType.DMA((groups,))],
        compiler_params=SMALL,
        cost_estimate=pl.CostEstimate(flops=2 * 10**6, bytes_accessed=3 * 10**6, transcendentals=0),
        name="back",
    )(coef, ends, part)


def resident(value):
    return pltpu.with_memory_space_constraint(value, pltpu.VMEM)


def shards(
    adjoint, log_conc, levels, conduct, orders_fwd, orders_rev, stoich, rate_fwd, rate_rev, diffusivity
):
    carried, nx, ny, nz = adjoint.shape
    rows_y, blocks = lax.axis_size("gy"), lax.axis_size("gx")
    near = lax.ppermute(adjoint, "gz", [(0, 1), (1, 0)])
    tail, head = edges(adjoint)
    low = lax.ppermute(tail, "gy", [(i, i + 1) for i in range(rows_y - 1)])
    high = lax.ppermute(head, "gy", [(i + 1, i) for i in range(rows_y - 1)])
    chem = chemistry(adjoint, log_conc, levels, orders_fwd, orders_rev, stoich, rate_fwd, rate_rev)
    part, coef, message = local_part(diffusivity, adjoint, chem, near, low, high, conduct)
    message = lax.all_to_all(message.reshape(blocks, ROWS, nz), "gx", 0, 0, tiled=True)
    ends = lax.all_to_all(chain(message), "gx", 0, 0, tiled=True)
    return back(part, coef, ends.reshape(blocks * ROWS, nz))


def solution(mesh):
    cells = P(None, "gx", "gy", "gz")
    planes = P("gx", "gy", "gz")
    in_specs = (cells, cells, planes, planes, P(), P(), P(), P(), P(), P())
    return jax.shard_map(shards, mesh=mesh, in_specs=in_specs, out_specs=cells, check_vma=False)
```

```python
import math

import jax
import jax.numpy as jnp
from jax import lax
from jax.experimental import pallas as pl
from jax.experimental.pallas import tpu as pltpu
from jax.sharding import PartitionSpec as P

SECTION = 0.02
STEP = 0.3
MASS = 0.001
LOG2E = math.log2(math.e)
OFF = -1024.0

K_ROWS = 96
R_PAD = 208
STRIP = 16
CHUNKS = tuple((start, STRIP) for start in range(0, R_PAD, STRIP))
TILE = 512
XB = 2
LIMIT = 12 * 1024 * 1024
F32 = jnp.float32
BF16 = jnp.bfloat16


def iota(shape, dim):
    return lax.broadcasted_iota(jnp.int32, shape, dim)


def dot(a, b):
    return lax.dot_general(a, b, (((1,), (0,)), ((), ())), preferred_element_type=F32)


def dot_nt(a, b):
    return lax.dot_general(a, b, (((1,), (1,)), ((), ())), preferred_element_type=F32)


def one_hot(mask):
    return jnp.where(mask, 1.0, 0.0).astype(BF16)


def build_weights(of_ref, or_ref, st_ref, rf_ref, rr_ref, wide_ref, w_ref, c_ref):
    species, react = of_ref.shape
    carried = st_ref.shape[0]
    eye = one_hot(iota((R_PAD, 256), 0) == iota((R_PAD, 256), 1))
    pick_row, pick_col = iota((32, 32), 0), iota((32, 32), 1)
    pick = one_hot(pick_col == jnp.where(pick_row < 16, pick_row, jnp.where(pick_row < 24, pick_row - 2, -1)))
    sub, tier = iota((8, 256), 0), 4 * iota((8, 256), 1) // react
    full = []
    for index, (orders, rate) in enumerate(((of_ref, rf_ref), (or_ref, rr_ref))):
        wide_ref[...] = jnp.zeros(wide_ref.shape, F32)
        wide_ref[0:species, 0:react] = orders[...].astype(F32)
        plain = wide_ref[0:32, :]
        sign = 1.0 if index == 0 else -1.0
        c_ref[index] = (sign * dot(pick, plain.astype(BF16)))[:, 0:R_PAD].astype(BF16)
        scaled = plain * LOG2E
        hi = scaled.astype(BF16).astype(F32)
        wide_ref[0:32, :] = hi
        wide_ref[32:64, :] = scaled - hi
        wide_ref[88:89, 0:react] = jnp.log(rate[...]) * LOG2E
        r = jnp.broadcast_to(wide_ref[88:89, :], (8, 256))
        r0 = r.astype(BF16).astype(F32)
        r1 = (r - r0).astype(BF16).astype(F32)
        parts = jnp.where(sub == 3, r0, jnp.where(sub == 4, r1, jnp.where(sub == 5, r - r0 - r1, 0.0)))
        wide_ref[88:96, :] = jnp.where(sub < 3, jnp.where(tier > sub, OFF, 0.0), parts)
        full.append(dot_nt(eye, wide_ref[...].astype(BF16)).astype(BF16))
    wide_ref[...] = jnp.zeros(wide_ref.shape, F32)
    wide_ref[64:80, 0:react] = st_ref[0:16, :].astype(F32)
    wide_ref[82 : 66 + carried, 0:react] = st_ref[16:carried, :].astype(F32)
    full.append(dot_nt(eye, wide_ref[...].astype(BF16)).astype(BF16))
    base = 0
    for start, size in CHUNKS:
        for part in full:
            w_ref[base : base + size, :] = part[start : start + size]
            base += size


def chem_kernel(
    adj_ref, conc_ref, lev_ref, of_ref, or_ref, st_ref, rf_ref, rr_ref, out_ref,
    wide_ref, w_ref, c_ref, conc32_ref, x_ref, act_ref,
):
    @pl.when(pl.program_id(0) == 0)
    def _():
        build_weights(of_ref, or_ref, st_ref, rf_ref, rr_ref, wide_ref, w_ref, c_ref)

    carried, xb, ny, nz = adj_ref.shape
    species = conc_ref.shape[0]
    adj_rows = adj_ref.reshape(carried * xb * ny, nz)
    out_rows = out_ref.reshape(carried * xb * ny, nz)
    pitch = xb * ny
    conc32_ref[...] = conc_ref[...].astype(F32).reshape(species * pitch, nz)
    sub = iota((8, nz), 0)
    for x in range(xb):
        for y in range(ny):
            row = x * ny + y
            cols = slice(y * nz, (y + 1) * nz)
            conc = jnp.concatenate(
                [conc32_ref[pl.ds(row + 8 * q * pitch, 8, stride=pitch), :] for q in range(4)], axis=0
            ).astype(BF16)
            x_ref[x, 0:32, cols] = conc
            x_ref[x, 32:64, cols] = conc
            lam = [adj_rows[pl.ds(row + first * pitch, 8, stride=pitch), :] for first in (0, 8, carried - 8)]
            level = jnp.broadcast_to(lev_ref[x, y : y + 1, :], (8, nz))
            marks = jnp.where(level <= sub, 1.0, 0.0)
            x_ref[x, 64:96, cols] = jnp.concatenate(lam + [marks], axis=0).astype(BF16)
    per_tile = TILE // nz
    for x in range(xb):
        for tile in range(ny // per_tile):
            slot = (x * (ny // per_tile) + tile) % act_ref.shape[0]
            data = x_ref[x, :, tile * TILE : (tile + 1) * TILE]
            every = dot(w_ref[...], data)
            for start, size in CHUNKS:
                got = every[3 * start : 3 * (start + size)]
                weight = got[2 * size :]
                act_ref[slot, 0, start : start + size, :] = (jnp.exp2(got[:size]) * weight).astype(BF16)
                act_ref[slot, 1, start : start + size, :] = (jnp.exp2(got[size : 2 * size]) * weight).astype(BF16)
            chem = dot(c_ref[0], act_ref[slot, 0]) + dot(c_ref[1], act_ref[slot, 1])
            for part in range(per_tile):
                row = x * ny + tile * per_tile + part
                for q, first in enumerate((0, 8, carried - 8)):
                    out_rows[pl.ds(row + first * pitch, 8, stride=pitch), :] = chem[
                        8 * q : 8 * q + 8, part * nz : (part + 1) * nz
                    ]


def chemistry(adjoint, log_conc, levels, orders_fwd, orders_rev, stoich, rate_fwd, rate_rev):
    carried, nx, ny, nz = adjoint.shape
    species, react = log_conc.shape[0], orders_fwd.shape[0]
    whole = lambda a: pl.BlockSpec(a.shape, lambda i: (0,) * len(a.shape))
    small = [orders_fwd.T, orders_rev.T, stoich.T, rate_fwd.reshape(1, react), rate_rev.reshape(1, react)]
    return pl.pallas_call(
        chem_kernel,
        grid=(nx // XB,),
        in_specs=[
            pl.BlockSpec((carried, XB, ny, nz), lambda i: (0, i, 0, 0)),
            pl.BlockSpec((species, XB, ny, nz), lambda i: (0, i, 0, 0)),
            pl.BlockSpec((XB, ny, nz), lambda i: (i, 0, 0)),
        ]
        + [whole(a) for a in small],
        out_specs=pl.BlockSpec((carried, XB, ny, nz), lambda i: (0, i, 0, 0)),
        out_shape=jax.ShapeDtypeStruct(adjoint.shape, F32),
        scratch_shapes=[
            pltpu.VMEM((K_ROWS, 256), F32),
            pltpu.VMEM((3 * R_PAD, K_ROWS), BF16),
            pltpu.VMEM((2, 32, R_PAD), BF16),
            pltpu.VMEM((species * XB * ny, nz), F32),
            pltpu.VMEM((XB, K_ROWS, ny * nz), BF16),
            pltpu.VMEM((2, 2, R_PAD, TILE), BF16),
        ],
        compiler_params=pltpu.CompilerParams(dimension_semantics=("arbitrary",), vmem_limit_bytes=LIMIT),
        cost_estimate=pl.CostEstimate(flops=12 * 10**9, bytes_accessed=4 * 10**6, transcendentals=6_750_000),
        name="chem",
    )(adjoint, log_conc, levels, *small)


GROUP = 6
GROUPS = 4
ROWS = 16
SB = 2
ANY = pl.BlockSpec(memory_space=pl.ANY)
WHOLE = pl.BlockSpec(memory_space=pltpu.VMEM)
SMALL = pltpu.CompilerParams(vmem_limit_bytes=LIMIT)


def place(s):
    return s // GROUP * ROWS + s % GROUP


PACK = 4


def edges_kernel(adj_ref, low_ref, high_ref, side_ref):
    carried, nx, ny, nz = adj_ref.shape
    lane = iota((ny, nz), 1)
    own_shift = jnp.where(lax.axis_index("gz") == 0, 2, 0)
    side_ref[...] = jnp.zeros(side_ref.shape, F32)

    @pl.loop(0, carried)
    def _(s):
        start = s % PACK * 2 * nx
        packed = side_ref[s // PACK]
        for x in range(nx):
            low_ref[s, x] = adj_ref[s, x, ny - 2 : ny, :]
            high_ref[s, x] = adj_ref[s, x, 0:2, :]
            moved = pltpu.roll(adj_ref[s, x], lax.rem(start + (2 * x + own_shift), nz), 1)
            packed = jnp.where(lane // 2 == start // 2 + x, moved, packed)
        side_ref[s // PACK] = packed


def edges(adjoint):
    carried, nx, ny, nz = adjoint.shape
    shape = pltpu.VMEM((carried, nx, 2, nz), F32)
    return pl.pallas_call(
        edges_kernel,
        in_specs=[WHOLE],
        out_specs=[WHOLE] * 3,
        out_shape=[shape, shape, pltpu.VMEM((-(-carried // PACK), ny, nz), F32)],
        compiler_params=SMALL,
        cost_estimate=pl.CostEstimate(flops=0, bytes_accessed=2 * 10**6, transcendentals=0),
        name="edges",
    )(adjoint)


def local_kernel(
    diff_ref, cond_ref, adj_ref, chem_ref, near_ref, low_ref, high_ref, part_ref, coef_ref, msg_ref, inv_ref
):
    nx, ny, nz = cond_ref.shape
    carried = adj_ref.shape[0]
    stride = GROUPS * ROWS
    third = MASS / 3.0
    body = MASS + 2.0 * third
    mass_first = jnp.where(lax.axis_index("gx") == 0, MASS + third, body) * jnp.ones((ny, nz), F32)
    gap = cond_ref[0] - third
    mass = jnp.full((ny, nz), body, F32)
    for p in range(1, nx - 1):
        after = cond_ref[p] - third
        inv = 1.0 / (gap + after + mass)
        alpha, beta = gap * inv, after * inv
        coef_ref[0, p], coef_ref[1, p], inv_ref[p] = alpha, beta, inv
        mass_first = mass_first + alpha * mass
        mass = body + beta * mass
        gap = alpha * after
    face = cond_ref[nx - 1] - third
    msg_ref[...] = jnp.zeros(msg_ref.shape, F32)
    for group in range(GROUPS):
        for r, value in ((6, gap), (7, mass_first), (14, face), (15, mass)):
            msg_ref[pl.ds(group * ROWS + r, ny, stride=stride), :] = value

    lane, row = iota((ny, nz), 1), iota((ny, nz), 0)
    keep_low = jnp.where(lax.axis_index("gz") == 0, 1.0, 0.0)
    keep_high = 1.0 - keep_low
    near_shift = jnp.where(lax.axis_index("gz") == 0, 0, 2)

    @pl.loop(0, carried // SB)
    def _(g):
        for t in range(SB):
            s = g * SB + t
            scale = diff_ref[s] * (SECTION * STEP / 12.0)
            side = near_ref[s // PACK]
            back_by = nz - s % PACK * 2 * nx - near_shift
            b_first, carry = None, None
            for p in range(nx):
                own = adj_ref[s, p]
                near = pltpu.roll(side, lax.rem(back_by + (nz - 2 * p), nz), 1)
                from_high = near * keep_low
                from_low = near * keep_high
                z_up1 = pltpu.roll(jnp.where(lane < 1, from_high, own), nz - 1, 1)
                z_up2 = pltpu.roll(jnp.where(lane < 2, from_high, own), nz - 2, 1)
                z_dn1 = pltpu.roll(jnp.where(lane >= nz - 1, from_low, own), 1, 1)
                z_dn2 = pltpu.roll(jnp.where(lane >= nz - 2, from_low, own), 2, 1)
                low0, low1 = low_ref[s, p, 0:1, :], low_ref[s, p, 1:2, :]
                high0, high1 = high_ref[s, p, 0:1, :], high_ref[s, p, 1:2, :]
                y_up1 = jnp.where(row == ny - 1, high0, pltpu.roll(own, ny - 1, 0))
                y_up2 = jnp.where(row == ny - 1, high1, jnp.where(row == ny - 2, high0, pltpu.roll(own, ny - 2, 0)))
                y_dn1 = jnp.where(row == 0, low1, pltpu.roll(own, 1, 0))
                y_dn2 = jnp.where(row == 0, low0, jnp.where(row == 1, low1, pltpu.roll(own, 2, 0)))
                spread = 16.0 * ((z_up1 + z_dn1) + (y_up1 + y_dn1)) - ((z_up2 + z_dn2) + (y_up2 + y_dn2)) - 60.0 * own
                b = SECTION * own + (SECTION * STEP) * chem_ref[s, p] + scale * spread
                if p == 0:
                    b_first = b
                elif p < nx - 1:
                    full = b if carry is None else b + carry
                    part_ref[s, p] = full * inv_ref[p]
                    b_first = b_first + coef_ref[0, p] * full
                    carry = coef_ref[1, p] * full
                else:
                    b_last = b + carry
            msg_ref[pl.ds(place(s), ny, stride=stride), :] = b_first
            msg_ref[pl.ds(place(s) + 8, ny, stride=stride), :] = b_last


def local_part(diffusivity, adjoint, chem, near, low, high, conduct):
    carried, nx, ny, nz = adjoint.shape
    smem = pl.BlockSpec(memory_space=pltpu.SMEM)
    return pl.pallas_call(
        local_kernel,
        in_specs=[smem] + [WHOLE] * 6,
        out_specs=[WHOLE] * 3,
        out_shape=[
            pltpu.VMEM(adjoint.shape, F32),
            pltpu.VMEM((2, nx, ny, nz), F32),
            pltpu.VMEM((GROUPS * ny * ROWS, nz), F32),
        ],
        scratch_shapes=[pltpu.VMEM((nx, ny, nz), F32)],
        compiler_params=SMALL,
        cost_estimate=pl.CostEstimate(flops=20 * 10**6, bytes_accessed=7 * 10**6, transcendentals=0),
        name="local",
    )(diffusivity, conduct, adjoint, chem, near, low, high)


def chain_kernel(in_ref, out_ref):
    count, _, nz = in_ref.shape
    h, mass, rhs, ends = [], [], [], []
    passed_m = passed_b = None
    for i in range(count):
        low, high = in_ref[i, 0:8, :], in_ref[i, 8:16, :]
        g = jnp.broadcast_to(in_ref[i, 6:7, :], (8, nz))
        m_f = jnp.broadcast_to(in_ref[i, 7:8, :], (8, nz))
        face = jnp.broadcast_to(in_ref[i, 14:15, :], (8, nz))
        m_l = jnp.broadcast_to(in_ref[i, 15:16, :], (8, nz))
        inv = 1.0 / (g + face + m_l)
        a, c = g * inv, face * inv
        m, b = m_f + a * m_l, low + a * high
        if i > 0:
            m, b = m + passed_m, b + passed_b
        passed_m, passed_b = c * m_l, c * high
        h.append(a * face)
        mass.append(m)
        rhs.append(b)
        ends.append((a, c, high * inv))
    half = count // 2
    scale, ratio = [None] * count, [None] * count
    for i in range(half - 1):
        inv = 1.0 / (mass[i] + h[i])
        q = h[i] * inv
        scale[i], ratio[i] = rhs[i] * inv, q
        mass[i + 1] = mass[i + 1] + q * mass[i]
        rhs[i + 1] = rhs[i + 1] + q * rhs[i]
    mass[count - 1] = mass[count - 1] + h[count - 1]
    for i in range(count - 1, half, -1):
        inv = 1.0 / (mass[i] + h[i - 1])
        q = h[i - 1] * inv
        scale[i], ratio[i] = rhs[i] * inv, q
        mass[i - 1] = mass[i - 1] + q * mass[i]
        rhs[i - 1] = rhs[i - 1] + q * rhs[i]
    inv = 1.0 / (mass[half - 1] + h[half - 1])
    q = h[half - 1] * inv
    first = [None] * (count + 1)
    first[half] = (rhs[half] + q * rhs[half - 1]) / (mass[half] + q * mass[half - 1])
    first[half - 1] = rhs[half - 1] * inv + q * first[half]
    for i in range(half - 2, -1, -1):
        first[i] = scale[i] + ratio[i] * first[i + 1]
    for i in range(half + 1, count):
        first[i] = scale[i] + ratio[i] * first[i - 1]
    for i in range(count):
        a, c, part = ends[i]
        last = part + a * first[i]
        if i < count - 1:
            last = last + c * first[i + 1]
        out_ref[i, 0:8, :] = first[i]
        out_ref[i, 8:16, :] = last


def chain(message):
    return pl.pallas_call(
        chain_kernel,
        in_specs=[WHOLE],
        out_specs=WHOLE,
        out_shape=pltpu.VMEM(message.shape, F32),
        compiler_params=SMALL,
        cost_estimate=pl.CostEstimate(flops=10**6, bytes_accessed=10**6, transcendentals=0),
        name="chain",
    )(message)


def back_kernel(coef_ref, ends_ref, part_ref, out_hbm, out_ref, out_sem):
    carried, nx, ny, _ = part_ref.shape
    groups = carried // SB

    def put(g):
        return pltpu.make_async_copy(out_ref.at[pl.ds(g * SB, SB)], out_hbm.at[pl.ds(g * SB, SB)], out_sem.at[g])

    @pl.loop(0, groups)
    def _(g):
        for t in range(SB):
            s = g * SB + t
            first = ends_ref[pl.ds(place(s), ny, stride=GROUPS * ROWS), :]
            value = ends_ref[pl.ds(place(s) + 8, ny, stride=GROUPS * ROWS), :]
            out_ref[s, 0] = first
            out_ref[s, nx - 1] = value
            for p in range(nx - 2, 0, -1):
                value = part_ref[s, p] + coef_ref[0, p] * first + coef_ref[1, p] * value
                out_ref[s, p] = value
        put(g).start()

    @pl.loop(0, groups)
    def _(g):
        put(g).wait()


def back(part, coef, ends):
    groups = part.shape[0] // SB
    return pl.pallas_call(
        back_kernel,
        in_specs=[WHOLE, WHOLE, WHOLE],
        out_specs=ANY,
        out_shape=jax.ShapeDtypeStruct(part.shape, F32),
        scratch_shapes=[pltpu.VMEM(part.shape, F32), pltpu.SemaphoreType.DMA((groups,))],
        compiler_params=SMALL,
        cost_estimate=pl.CostEstimate(flops=2 * 10**6, bytes_accessed=3 * 10**6, transcendentals=0),
        name="back",
    )(coef, ends, part)


def resident(value):
    return pltpu.with_memory_space_constraint(value, pltpu.VMEM)


def shards(
    adjoint, log_conc, levels, conduct, orders_fwd, orders_rev, stoich, rate_fwd, rate_rev, diffusivity
):
    carried, nx, ny, nz = adjoint.shape
    rows_y, blocks = lax.axis_size("gy"), lax.axis_size("gx")
    tail, head, side = edges(adjoint)
    low = lax.ppermute(tail, "gy", [(i, i + 1) for i in range(rows_y - 1)])
    high = lax.ppermute(head, "gy", [(i + 1, i) for i in range(rows_y - 1)])
    near = lax.ppermute(side, "gz", [(0, 1), (1, 0)])
    chem = chemistry(adjoint, log_conc, levels, orders_fwd, orders_rev, stoich, rate_fwd, rate_rev)
    part, coef, message = local_part(diffusivity, adjoint, chem, near, low, high, conduct)
    message = lax.all_to_all(message.reshape(blocks, ROWS, nz), "gx", 0, 0, tiled=True)
    ends = lax.all_to_all(chain(message), "gx", 0, 0, tiled=True)
    return back(part, coef, ends.reshape(blocks * ROWS, nz))


def solution(mesh):
    cells = P(None, "gx", "gy", "gz")
    planes = P("gx", "gy", "gz")
    in_specs = (cells, cells, planes, planes, P(), P(), P(), P(), P(), P())
    return jax.shard_map(shards, mesh=mesh, in_specs=in_specs, out_specs=cells, check_vma=False)
```

```python
import math

import jax
import jax.numpy as jnp
from jax import lax
from jax.experimental import pallas as pl
from jax.experimental.pallas import tpu as pltpu
from jax.sharding import PartitionSpec as P

SECTION = 0.02
STEP = 0.3
MASS = 0.001
THIRD = MASS / 3.0
BODY = MASS + 2.0 * THIRD
LOG2E = math.log2(math.e)
OFF = -1024.0

K_ROWS = 96
R_PAD = 208
STRIP = 16
CHUNKS = tuple((start, STRIP) for start in range(0, R_PAD, STRIP))
TILE = 1024
XB = 2
LIMIT = 12 * 1024 * 1024
F32 = jnp.float32
BF16 = jnp.bfloat16


def iota(shape, dim):
    return lax.broadcasted_iota(jnp.int32, shape, dim)


def dot(a, b):
    return lax.dot_general(a, b, (((1,), (0,)), ((), ())), preferred_element_type=F32)


def dot_nt(a, b):
    return lax.dot_general(a, b, (((1,), (1,)), ((), ())), preferred_element_type=F32)


def one_hot(mask):
    return jnp.where(mask, 1.0, 0.0).astype(BF16)


def build_weights(of_ref, or_ref, st_ref, rf_ref, rr_ref, wide_ref, w_ref, c_ref):
    species, react = of_ref.shape
    carried = st_ref.shape[0]
    eye = one_hot(iota((R_PAD, 256), 0) == iota((R_PAD, 256), 1))
    pick_row, pick_col = iota((32, 32), 0), iota((32, 32), 1)
    pick = one_hot(pick_col == jnp.where(pick_row < 16, pick_row, jnp.where(pick_row < 24, pick_row - 2, -1)))
    sub, tier = iota((8, 256), 0), 4 * iota((8, 256), 1) // react
    full = []
    for index, (orders, rate) in enumerate(((of_ref, rf_ref), (or_ref, rr_ref))):
        wide_ref[...] = jnp.zeros(wide_ref.shape, F32)
        wide_ref[0:species, 0:react] = orders[...].astype(F32)
        plain = wide_ref[0:32, :]
        sign = 1.0 if index == 0 else -1.0
        c_ref[index] = (sign * dot(pick, plain.astype(BF16)))[:, 0:R_PAD].astype(BF16)
        scaled = plain * LOG2E
        hi = scaled.astype(BF16).astype(F32)
        wide_ref[0:32, :] = hi
        wide_ref[32:64, :] = scaled - hi
        wide_ref[88:89, 0:react] = jnp.log(rate[...]) * LOG2E
        r = jnp.broadcast_to(wide_ref[88:89, :], (8, 256))
        r0 = r.astype(BF16).astype(F32)
        r1 = (r - r0).astype(BF16).astype(F32)
        parts = jnp.where(sub == 3, r0, jnp.where(sub == 4, r1, jnp.where(sub == 5, r - r0 - r1, 0.0)))
        wide_ref[88:96, :] = jnp.where(sub < 3, jnp.where(tier > sub, OFF, 0.0), parts)
        full.append(dot_nt(eye, wide_ref[...].astype(BF16)).astype(BF16))
    wide_ref[...] = jnp.zeros(wide_ref.shape, F32)
    wide_ref[64:80, 0:react] = st_ref[0:16, :].astype(F32)
    wide_ref[82 : 66 + carried, 0:react] = st_ref[16:carried, :].astype(F32)
    full.append(dot_nt(eye, wide_ref[...].astype(BF16)).astype(BF16))
    base = 0
    for start, size in CHUNKS:
        for part in full:
            w_ref[base : base + size, :] = part[start : start + size]
            base += size


def chem_kernel(
    adj_ref, conc_ref, lev_ref, cond_ref, of_ref, or_ref, st_ref, rf_ref, rr_ref,
    out_ref, coef_ref, tail_ref,
    wide_ref, w_ref, c_ref, conc32_ref, x_ref, act_ref, run_ref,
):
    step = pl.program_id(0)

    @pl.when(step == 0)
    def _():
        run_ref[0] = cond_ref[0] - THIRD
        run_ref[1] = jnp.where(lax.axis_index("gx") == 0, MASS + THIRD, BODY) * jnp.ones(run_ref.shape[1:], F32)
        run_ref[2] = jnp.full(run_ref.shape[1:], BODY, F32)
        build_weights(of_ref, or_ref, st_ref, rf_ref, rr_ref, wide_ref, w_ref, c_ref)

    gap, mass_first, mass = run_ref[0], run_ref[1], run_ref[2]
    for q in range(1, XB + 1):
        p = step * XB + q
        after = cond_ref[jnp.minimum(p, cond_ref.shape[0] - 1)] - THIRD
        inv = 1.0 / (gap + after + mass)
        alpha, beta = gap * inv, after * inv
        coef_ref[0, p], coef_ref[1, p], coef_ref[2, p] = alpha, beta, inv
        mass_first = mass_first + alpha * mass
        mass = BODY + beta * mass
        gap = alpha * after
    run_ref[0], run_ref[1], run_ref[2] = gap, mass_first, mass
    tail_ref[step, 0], tail_ref[step, 1], tail_ref[step, 2] = gap, mass_first, mass

    carried, xb, ny, nz = adj_ref.shape
    species = conc_ref.shape[0]
    adj_rows = adj_ref.reshape(carried * xb * ny, nz)
    out_rows = out_ref.reshape(carried * xb * ny, nz)
    pitch = xb * ny
    conc32_ref[...] = conc_ref[...].astype(F32).reshape(species * pitch, nz)
    sub = iota((8, nz), 0)
    for x in range(xb):
        for y in range(ny):
            row = x * ny + y
            cols = slice(y * nz, (y + 1) * nz)
            conc = jnp.concatenate(
                [conc32_ref[pl.ds(row + 8 * q * pitch, 8, stride=pitch), :] for q in range(4)], axis=0
            ).astype(BF16)
            x_ref[x, 0:32, cols] = conc
            x_ref[x, 32:64, cols] = conc
            lam = [adj_rows[pl.ds(row + first * pitch, 8, stride=pitch), :] for first in (0, 8, carried - 8)]
            level = jnp.broadcast_to(lev_ref[x, y : y + 1, :], (8, nz))
            marks = jnp.where(level <= sub, 1.0, 0.0)
            x_ref[x, 64:96, cols] = jnp.concatenate(lam + [marks], axis=0).astype(BF16)
    per_tile = TILE // nz
    for x in range(xb):
        for tile in range(ny // per_tile):
            slot = (x * (ny // per_tile) + tile) % act_ref.shape[0]
            data = x_ref[x, :, tile * TILE : (tile + 1) * TILE]
            every = dot(w_ref[...], data)
            for start, size in CHUNKS:
                got = every[3 * start : 3 * (start + size)]
                weight = got[2 * size :]
                act_ref[slot, 0, start : start + size, :] = (jnp.exp2(got[:size]) * weight).astype(BF16)
                act_ref[slot, 1, start : start + size, :] = (jnp.exp2(got[size : 2 * size]) * weight).astype(BF16)
            chem = dot(c_ref[0], act_ref[slot, 0]) + dot(c_ref[1], act_ref[slot, 1])
            for part in range(per_tile):
                row = x * ny + tile * per_tile + part
                for q, first in enumerate((0, 8, carried - 8)):
                    out_rows[pl.ds(row + first * pitch, 8, stride=pitch), :] = chem[
                        8 * q : 8 * q + 8, part * nz : (part + 1) * nz
                    ]


def chemistry(adjoint, log_conc, levels, conduct, orders_fwd, orders_rev, stoich, rate_fwd, rate_rev):
    carried, nx, ny, nz = adjoint.shape
    species, react = log_conc.shape[0], orders_fwd.shape[0]
    whole = lambda a: pl.BlockSpec(a.shape, lambda i: (0,) * len(a.shape))
    small = [orders_fwd.T, orders_rev.T, stoich.T, rate_fwd.reshape(1, react), rate_rev.reshape(1, react)]
    return pl.pallas_call(
        chem_kernel,
        grid=(nx // XB,),
        in_specs=[
            pl.BlockSpec((carried, XB, ny, nz), lambda i: (0, i, 0, 0)),
            pl.BlockSpec((species, XB, ny, nz), lambda i: (0, i, 0, 0)),
            pl.BlockSpec((XB, ny, nz), lambda i: (i, 0, 0)),
            whole(conduct),
        ]
        + [whole(a) for a in small],
        out_specs=[
            pl.BlockSpec((carried, XB, ny, nz), lambda i: (0, i, 0, 0)),
            pl.BlockSpec((3, nx + 1, ny, nz), lambda i: (0, 0, 0, 0)),
            pl.BlockSpec((nx // XB, 3, ny, nz), lambda i: (0, 0, 0, 0)),
        ],
        out_shape=[
            jax.ShapeDtypeStruct(adjoint.shape, F32),
            jax.ShapeDtypeStruct((3, nx + 1, ny, nz), F32),
            jax.ShapeDtypeStruct((nx // XB, 3, ny, nz), F32),
        ],
        scratch_shapes=[
            pltpu.VMEM((K_ROWS, 256), F32),
            pltpu.VMEM((3 * R_PAD, K_ROWS), BF16),
            pltpu.VMEM((2, 32, R_PAD), BF16),
            pltpu.VMEM((species * XB * ny, nz), F32),
            pltpu.VMEM((XB, K_ROWS, ny * nz), BF16),
            pltpu.VMEM((2, 2, R_PAD, TILE), BF16),
            pltpu.VMEM((3, ny, nz), F32),
        ],
        compiler_params=pltpu.CompilerParams(dimension_semantics=("arbitrary",), vmem_limit_bytes=LIMIT),
        cost_estimate=pl.CostEstimate(flops=12 * 10**9, bytes_accessed=4 * 10**6, transcendentals=6_750_000),
        name="chem",
    )(adjoint, log_conc, levels, conduct, *small)


GROUP = 6
GROUPS = 4
ROWS = 16
SB = 2
ANY = pl.BlockSpec(memory_space=pl.ANY)
WHOLE = pl.BlockSpec(memory_space=pltpu.VMEM)
SMALL = pltpu.CompilerParams(vmem_limit_bytes=LIMIT)


def place(s):
    return s // GROUP * ROWS + s % GROUP


def edges_kernel(adj_ref, low_ref, high_ref):
    carried, nx, ny, nz = adj_ref.shape

    @pl.loop(0, carried)
    def _(s):
        for x in range(nx):
            low_ref[s, x] = adj_ref[s, x, ny - 2 : ny, :]
            high_ref[s, x] = adj_ref[s, x, 0:2, :]


def edges(adjoint):
    carried, nx, ny, nz = adjoint.shape
    shape = pltpu.VMEM((carried, nx, 2, nz), F32)
    return pl.pallas_call(
        edges_kernel,
        in_specs=[WHOLE],
        out_specs=[WHOLE, WHOLE],
        out_shape=[shape, shape],
        compiler_params=SMALL,
        cost_estimate=pl.CostEstimate(flops=0, bytes_accessed=2 * 10**6, transcendentals=0),
        name="edges",
    )(adjoint)


def split(value):
    high = value.astype(BF16)
    return high, (value - high.astype(F32)).astype(BF16)


def local_kernel(
    diff_ref, cond_ref, adj_ref, chem_ref, near_ref, low_ref, high_ref, coef_ref, tail_ref,
    part_ref, msg_ref, band_ref, zz_ref,
):
    nx, ny, nz = cond_ref.shape
    carried = adj_ref.shape[0]
    stride = GROUPS * ROWS
    msg_ref[...] = jnp.zeros(msg_ref.shape, F32)
    at = nx // XB - 2
    face = cond_ref[nx - 1] - THIRD
    for group in range(GROUPS):
        for r, value in ((6, tail_ref[at, 0]), (7, tail_ref[at, 1]), (14, face), (15, tail_ref[at, 2])):
            msg_ref[pl.ds(group * ROWS + r, ny, stride=stride), :] = value

    k, z = iota((2 * nz, nz), 0), iota((2 * nz, nz), 1)
    offset = jnp.where(lax.axis_index("gz") == 0, nz, -nz)
    gap = jnp.abs(jnp.where(k < nz, k, k - nz + offset) - z)
    band_ref[...] = jnp.where(
        gap == 0, -60.0, jnp.where(gap == 1, 16.0, jnp.where(gap == 2, -1.0, 0.0))
    ).astype(BF16)
    row = iota((ny, nz), 0)

    @pl.loop(0, carried // SB)
    def _(g):
        for t in range(SB):
            s = g * SB + t
            own_hi, own_lo = split(adj_ref[s].reshape(nx * ny, nz))
            near_hi, near_lo = split(near_ref[s].reshape(nx * ny, nz))
            sides = jnp.concatenate(
                [jnp.concatenate([own_hi, near_hi], axis=1), jnp.concatenate([own_lo, near_lo], axis=1)], axis=0
            )
            spread_z = dot(sides, band_ref[...])
            zz_ref[t] = spread_z[: nx * ny] + spread_z[nx * ny :]
        for t in range(SB):
            s = g * SB + t
            scale = diff_ref[s] * (SECTION * STEP / 12.0)
            b_first, carry = None, None
            for p in range(nx):
                own = adj_ref[s, p]
                low0, low1 = low_ref[s, p, 0:1, :], low_ref[s, p, 1:2, :]
                high0, high1 = high_ref[s, p, 0:1, :], high_ref[s, p, 1:2, :]
                y_up1 = jnp.where(row == ny - 1, high0, pltpu.roll(own, ny - 1, 0))
                y_up2 = jnp.where(row == ny - 1, high1, jnp.where(row == ny - 2, high0, pltpu.roll(own, ny - 2, 0)))
                y_dn1 = jnp.where(row == 0, low1, pltpu.roll(own, 1, 0))
                y_dn2 = jnp.where(row == 0, low0, jnp.where(row == 1, low1, pltpu.roll(own, 2, 0)))
                spread = 16.0 * (y_up1 + y_dn1) - (y_up2 + y_dn2) + zz_ref[t, p * ny : (p + 1) * ny, :]
                b = SECTION * own + (SECTION * STEP) * chem_ref[s, p] + scale * spread
                if p == 0:
                    b_first = b
                elif p < nx - 1:
                    full = b if carry is None else b + carry
                    part_ref[s, p] = full * coef_ref[2, p]
                    b_first = b_first + coef_ref[0, p] * full
                    carry = coef_ref[1, p] * full
                else:
                    b_last = b + carry
            msg_ref[pl.ds(place(s), ny, stride=stride), :] = b_first
            msg_ref[pl.ds(place(s) + 8, ny, stride=stride), :] = b_last


def local_part(diffusivity, adjoint, chem, near, low, high, conduct, coef, ends):
    carried, nx, ny, nz = adjoint.shape
    smem = pl.BlockSpec(memory_space=pltpu.SMEM)
    return pl.pallas_call(
        local_kernel,
        in_specs=[smem] + [WHOLE] * 8,
        out_specs=[WHOLE] * 2,
        out_shape=[
            pltpu.VMEM(adjoint.shape, F32),
            pltpu.VMEM((GROUPS * ny * ROWS, nz), F32),
        ],
        scratch_shapes=[pltpu.VMEM((2 * nz, nz), BF16), pltpu.VMEM((SB, nx * ny, nz), F32)],
        compiler_params=SMALL,
        cost_estimate=pl.CostEstimate(flops=20 * 10**6, bytes_accessed=7 * 10**6, transcendentals=0),
        name="local",
    )(diffusivity, conduct, adjoint, chem, near, low, high, coef, ends)


def chain_kernel(in_ref, out_ref):
    count, _, nz = in_ref.shape
    h, mass, rhs, ends = [], [], [], []
    passed_m = passed_b = None
    for i in range(count):
        low, high = in_ref[i, 0:8, :], in_ref[i, 8:16, :]
        g = jnp.broadcast_to(in_ref[i, 6:7, :], (8, nz))
        m_f = jnp.broadcast_to(in_ref[i, 7:8, :], (8, nz))
        face = jnp.broadcast_to(in_ref[i, 14:15, :], (8, nz))
        m_l = jnp.broadcast_to(in_ref[i, 15:16, :], (8, nz))
        inv = 1.0 / (g + face + m_l)
        a, c = g * inv, face * inv
        m, b = m_f + a * m_l, low + a * high
        if i > 0:
            m, b = m + passed_m, b + passed_b
        passed_m, passed_b = c * m_l, c * high
        h.append(a * face)
        mass.append(m)
        rhs.append(b)
        ends.append((a, c, high * inv))
    half = count // 2
    scale, ratio = [None] * count, [None] * count
    for i in range(half - 1):
        inv = 1.0 / (mass[i] + h[i])
        q = h[i] * inv
        scale[i], ratio[i] = rhs[i] * inv, q
        mass[i + 1] = mass[i + 1] + q * mass[i]
        rhs[i + 1] = rhs[i + 1] + q * rhs[i]
    mass[count - 1] = mass[count - 1] + h[count - 1]
    for i in range(count - 1, half, -1):
        inv = 1.0 / (mass[i] + h[i - 1])
        q = h[i - 1] * inv
        scale[i], ratio[i] = rhs[i] * inv, q
        mass[i - 1] = mass[i - 1] + q * mass[i]
        rhs[i - 1] = rhs[i - 1] + q * rhs[i]
    inv = 1.0 / (mass[half - 1] + h[half - 1])
    q = h[half - 1] * inv
    first = [None] * (count + 1)
    first[half] = (rhs[half] + q * rhs[half - 1]) / (mass[half] + q * mass[half - 1])
    first[half - 1] = rhs[half - 1] * inv + q * first[half]
    for i in range(half - 2, -1, -1):
        first[i] = scale[i] + ratio[i] * first[i + 1]
    for i in range(half + 1, count):
        first[i] = scale[i] + ratio[i] * first[i - 1]
    for i in range(count):
        a, c, part = ends[i]
        last = part + a * first[i]
        if i < count - 1:
            last = last + c * first[i + 1]
        out_ref[i, 0:8, :] = first[i]
        out_ref[i, 8:16, :] = last


def chain(message):
    return pl.pallas_call(
        chain_kernel,
        in_specs=[WHOLE],
        out_specs=WHOLE,
        out_shape=pltpu.VMEM(message.shape, F32),
        compiler_params=SMALL,
        cost_estimate=pl.CostEstimate(flops=10**6, bytes_accessed=10**6, transcendentals=0),
        name="chain",
    )(message)


def back_kernel(coef_ref, ends_ref, part_ref, out_hbm, out_ref, out_sem):
    carried, nx, ny, _ = part_ref.shape
    groups = carried // SB

    def put(g):
        return pltpu.make_async_copy(out_ref.at[pl.ds(g * SB, SB)], out_hbm.at[pl.ds(g * SB, SB)], out_sem.at[g])

    @pl.loop(0, groups)
    def _(g):
        for t in range(SB):
            s = g * SB + t
            first = ends_ref[pl.ds(place(s), ny, stride=GROUPS * ROWS), :]
            value = ends_ref[pl.ds(place(s) + 8, ny, stride=GROUPS * ROWS), :]
            out_ref[s, 0] = first
            out_ref[s, nx - 1] = value
            for p in range(nx - 2, 0, -1):
                value = part_ref[s, p] + coef_ref[0, p] * first + coef_ref[1, p] * value
                out_ref[s, p] = value
        put(g).start()

    @pl.loop(0, groups)
    def _(g):
        put(g).wait()


def back(part, coef, ends):
    groups = part.shape[0] // SB
    return pl.pallas_call(
        back_kernel,
        in_specs=[WHOLE, WHOLE, WHOLE],
        out_specs=ANY,
        out_shape=jax.ShapeDtypeStruct(part.shape, F32),
        scratch_shapes=[pltpu.VMEM(part.shape, F32), pltpu.SemaphoreType.DMA((groups,))],
        compiler_params=SMALL,
        cost_estimate=pl.CostEstimate(flops=2 * 10**6, bytes_accessed=3 * 10**6, transcendentals=0),
        name="back",
    )(coef, ends, part)


def resident(value):
    return pltpu.with_memory_space_constraint(value, pltpu.VMEM)


def shards(
    adjoint, log_conc, levels, conduct, orders_fwd, orders_rev, stoich, rate_fwd, rate_rev, diffusivity
):
    carried, nx, ny, nz = adjoint.shape
    rows_y, blocks = lax.axis_size("gy"), lax.axis_size("gx")
    near = lax.ppermute(adjoint, "gz", [(0, 1), (1, 0)])
    tail, head = edges(adjoint)
    low = lax.ppermute(tail, "gy", [(i, i + 1) for i in range(rows_y - 1)])
    high = lax.ppermute(head, "gy", [(i + 1, i) for i in range(rows_y - 1)])
    chem, coef, ends_m = chemistry(adjoint, log_conc, levels, conduct, orders_fwd, orders_rev, stoich, rate_fwd, rate_rev)
    part, message = local_part(diffusivity, adjoint, chem, near, low, high, conduct, coef, ends_m)
    message = lax.all_to_all(message.reshape(blocks, ROWS, nz), "gx", 0, 0, tiled=True)
    ends = lax.all_to_all(chain(message), "gx", 0, 0, tiled=True)
    return back(part, coef, ends.reshape(blocks * ROWS, nz))


def solution(mesh):
    cells = P(None, "gx", "gy", "gz")
    planes = P("gx", "gy", "gz")
    in_specs = (cells, cells, planes, planes, P(), P(), P(), P(), P(), P())
    return jax.shard_map(shards, mesh=mesh, in_specs=in_specs, out_specs=cells, check_vma=False)
```

```python
import math

import jax
import jax.numpy as jnp
from jax import lax
from jax.experimental import pallas as pl
from jax.experimental.pallas import tpu as pltpu
from jax.sharding import PartitionSpec as P

SECTION = 0.02
STEP = 0.3
MASS = 0.001
THIRD = MASS / 3.0
BODY = MASS + 2.0 * THIRD
LOG2E = math.log2(math.e)
OFF = -1024.0

K_ROWS = 96
R_PAD = 208
STRIP = 16
CHUNKS = tuple((start, STRIP) for start in range(0, R_PAD, STRIP))
TILE = 1024
XB = 4
LIMIT = 24 * 1024 * 1024
F32 = jnp.float32
BF16 = jnp.bfloat16


def iota(shape, dim):
    return lax.broadcasted_iota(jnp.int32, shape, dim)


def dot(a, b):
    return lax.dot_general(a, b, (((1,), (0,)), ((), ())), preferred_element_type=F32)


def dot_nt(a, b):
    return lax.dot_general(a, b, (((1,), (1,)), ((), ())), preferred_element_type=F32)


def one_hot(mask):
    return jnp.where(mask, 1.0, 0.0).astype(BF16)


def build_weights(of_ref, or_ref, st_ref, rf_ref, rr_ref, wide_ref, w_ref, c_ref):
    species, react = of_ref.shape
    carried = st_ref.shape[0]
    eye = one_hot(iota((R_PAD, 256), 0) == iota((R_PAD, 256), 1))
    pick_row, pick_col = iota((32, 32), 0), iota((32, 32), 1)
    pick = one_hot(pick_col == jnp.where(pick_row < 16, pick_row, jnp.where(pick_row < 24, pick_row - 2, -1)))
    sub, tier = iota((8, 256), 0), 4 * iota((8, 256), 1) // react
    full = []
    for index, (orders, rate) in enumerate(((of_ref, rf_ref), (or_ref, rr_ref))):
        wide_ref[...] = jnp.zeros(wide_ref.shape, F32)
        wide_ref[0:species, 0:react] = orders[...].astype(F32)
        plain = wide_ref[0:32, :]
        sign = 1.0 if index == 0 else -1.0
        c_ref[index] = (sign * dot(pick, plain.astype(BF16)))[:, 0:R_PAD].astype(BF16)
        scaled = plain * LOG2E
        hi = scaled.astype(BF16).astype(F32)
        wide_ref[0:32, :] = hi
        wide_ref[32:64, :] = scaled - hi
        wide_ref[88:89, 0:react] = jnp.log(rate[...]) * LOG2E
        r = jnp.broadcast_to(wide_ref[88:89, :], (8, 256))
        r0 = r.astype(BF16).astype(F32)
        r1 = (r - r0).astype(BF16).astype(F32)
        parts = jnp.where(sub == 3, r0, jnp.where(sub == 4, r1, jnp.where(sub == 5, r - r0 - r1, 0.0)))
        wide_ref[88:96, :] = jnp.where(sub < 3, jnp.where(tier > sub, OFF, 0.0), parts)
        full.append(dot_nt(eye, wide_ref[...].astype(BF16)).astype(BF16))
    wide_ref[...] = jnp.zeros(wide_ref.shape, F32)
    wide_ref[64:80, 0:react] = st_ref[0:16, :].astype(F32)
    wide_ref[82 : 66 + carried, 0:react] = st_ref[16:carried, :].astype(F32)
    full.append(dot_nt(eye, wide_ref[...].astype(BF16)).astype(BF16))
    base = 0
    for start, size in CHUNKS:
        for part in full:
            w_ref[base : base + size, :] = part[start : start + size]
            base += size


def chem_kernel(
    adj_ref, conc_ref, lev_ref, cond_ref, of_ref, or_ref, st_ref, rf_ref, rr_ref,
    out_ref, coef_ref, tail_ref,
    wide_ref, w_ref, c_ref, conc32_ref, x_ref, act_ref, run_ref,
):
    step = pl.program_id(0)

    @pl.when(step == 0)
    def _():
        run_ref[0] = cond_ref[0] - THIRD
        run_ref[1] = jnp.where(lax.axis_index("gx") == 0, MASS + THIRD, BODY) * jnp.ones(run_ref.shape[1:], F32)
        run_ref[2] = jnp.full(run_ref.shape[1:], BODY, F32)
        build_weights(of_ref, or_ref, st_ref, rf_ref, rr_ref, wide_ref, w_ref, c_ref)

    gap, mass_first, mass = run_ref[0], run_ref[1], run_ref[2]
    for q in range(1, XB + 1):
        p = step * XB + q
        after = cond_ref[jnp.minimum(p, cond_ref.shape[0] - 1)] - THIRD
        inv = 1.0 / (gap + after + mass)
        alpha, beta = gap * inv, after * inv
        coef_ref[0, p], coef_ref[1, p], coef_ref[2, p] = alpha, beta, inv
        mass_first = mass_first + alpha * mass
        mass = BODY + beta * mass
        gap = alpha * after
        tail_ref[p, 0], tail_ref[p, 1], tail_ref[p, 2] = gap, mass_first, mass
    run_ref[0], run_ref[1], run_ref[2] = gap, mass_first, mass

    carried, xb, ny, nz = adj_ref.shape
    species = conc_ref.shape[0]
    adj_rows = adj_ref.reshape(carried * xb * ny, nz)
    out_rows = out_ref.reshape(carried * xb * ny, nz)
    pitch = xb * ny
    conc32_ref[...] = conc_ref[...].astype(F32).reshape(species * pitch, nz)
    sub = iota((8, nz), 0)
    for x in range(xb):
        for y in range(ny):
            row = x * ny + y
            cols = slice(y * nz, (y + 1) * nz)
            conc = jnp.concatenate(
                [conc32_ref[pl.ds(row + 8 * q * pitch, 8, stride=pitch), :] for q in range(4)], axis=0
            ).astype(BF16)
            x_ref[x, 0:32, cols] = conc
            x_ref[x, 32:64, cols] = conc
            lam = [adj_rows[pl.ds(row + first * pitch, 8, stride=pitch), :] for first in (0, 8, carried - 8)]
            level = jnp.broadcast_to(lev_ref[x, y : y + 1, :], (8, nz))
            marks = jnp.where(level <= sub, 1.0, 0.0)
            x_ref[x, 64:96, cols] = jnp.concatenate(lam + [marks], axis=0).astype(BF16)
    per_tile = TILE // nz
    for x in range(xb):
        for tile in range(ny // per_tile):
            slot = (x * (ny // per_tile) + tile) % act_ref.shape[0]
            data = x_ref[x, :, tile * TILE : (tile + 1) * TILE]
            every = dot(w_ref[...], data)
            for start, size in CHUNKS:
                got = every[3 * start : 3 * (start + size)]
                weight = got[2 * size :]
                act_ref[slot, 0, start : start + size, :] = (jnp.exp2(got[:size]) * weight).astype(BF16)
                act_ref[slot, 1, start : start + size, :] = (jnp.exp2(got[size : 2 * size]) * weight).astype(BF16)
            chem = dot(c_ref[0], act_ref[slot, 0]) + dot(c_ref[1], act_ref[slot, 1])
            for part in range(per_tile):
                row = x * ny + tile * per_tile + part
                for q, first in enumerate((0, 8, carried - 8)):
                    out_rows[pl.ds(row + first * pitch, 8, stride=pitch), :] = chem[
                        8 * q : 8 * q + 8, part * nz : (part + 1) * nz
                    ]


def chemistry(adjoint, log_conc, levels, conduct, orders_fwd, orders_rev, stoich, rate_fwd, rate_rev):
    carried, nx, ny, nz = adjoint.shape
    species, react = log_conc.shape[0], orders_fwd.shape[0]
    whole = lambda a: pl.BlockSpec(a.shape, lambda i: (0,) * len(a.shape))
    small = [orders_fwd.T, orders_rev.T, stoich.T, rate_fwd.reshape(1, react), rate_rev.reshape(1, react)]
    return pl.pallas_call(
        chem_kernel,
        grid=(nx // XB,),
        in_specs=[
            pl.BlockSpec((carried, XB, ny, nz), lambda i: (0, i, 0, 0)),
            pl.BlockSpec((species, XB, ny, nz), lambda i: (0, i, 0, 0)),
            pl.BlockSpec((XB, ny, nz), lambda i: (i, 0, 0)),
            whole(conduct),
        ]
        + [whole(a) for a in small],
        out_specs=[
            pl.BlockSpec((carried, XB, ny, nz), lambda i: (0, i, 0, 0)),
            pl.BlockSpec((3, nx + 1, ny, nz), lambda i: (0, 0, 0, 0)),
            pl.BlockSpec((nx + 1, 3, ny, nz), lambda i: (0, 0, 0, 0)),
        ],
        out_shape=[
            jax.ShapeDtypeStruct(adjoint.shape, F32),
            jax.ShapeDtypeStruct((3, nx + 1, ny, nz), F32),
            jax.ShapeDtypeStruct((nx + 1, 3, ny, nz), F32),
        ],
        scratch_shapes=[
            pltpu.VMEM((K_ROWS, 256), F32),
            pltpu.VMEM((3 * R_PAD, K_ROWS), BF16),
            pltpu.VMEM((2, 32, R_PAD), BF16),
            pltpu.VMEM((species * XB * ny, nz), F32),
            pltpu.VMEM((XB, K_ROWS, ny * nz), BF16),
            pltpu.VMEM((2, 2, R_PAD, TILE), BF16),
            pltpu.VMEM((3, ny, nz), F32),
        ],
        compiler_params=pltpu.CompilerParams(dimension_semantics=("arbitrary",), vmem_limit_bytes=LIMIT),
        cost_estimate=pl.CostEstimate(flops=12 * 10**9, bytes_accessed=4 * 10**6, transcendentals=6_750_000),
        name="chem",
    )(adjoint, log_conc, levels, conduct, *small)


GROUP = 6
GROUPS = 4
ROWS = 16
SB = 2
LB = 11
ANY = pl.BlockSpec(memory_space=pl.ANY)
WHOLE = pl.BlockSpec(memory_space=pltpu.VMEM)
SMALL = pltpu.CompilerParams(vmem_limit_bytes=LIMIT)


def place(s):
    return s // GROUP * ROWS + s % GROUP


def edges_kernel(adj_ref, low_ref, high_ref):
    carried, nx, ny, nz = adj_ref.shape
    mine = lax.axis_index("gy")
    to_high = jnp.where(mine == lax.axis_size("gy") - 1, 0.0, 1.0)
    to_low = jnp.where(mine == 0, 0.0, 1.0)

    @pl.loop(0, carried)
    def _(s):
        for x in range(nx):
            low_ref[s, x] = adj_ref[s, x, ny - 2 : ny, :] * to_high
            high_ref[s, x] = adj_ref[s, x, 0:2, :] * to_low


def edges(adjoint):
    carried, nx, ny, nz = adjoint.shape
    shape = pltpu.VMEM((carried, nx, 2, nz), F32)
    return pl.pallas_call(
        edges_kernel,
        in_specs=[WHOLE],
        out_specs=[WHOLE, WHOLE],
        out_shape=[shape, shape],
        compiler_params=SMALL,
        cost_estimate=pl.CostEstimate(flops=0, bytes_accessed=2 * 10**6, transcendentals=0),
        name="edges",
    )(adjoint)


def split(value):
    high = value.astype(BF16)
    return high, (value - high.astype(F32)).astype(BF16)


def local_kernel(
    diff_ref, cond_ref, adj_ref, chem_ref, near_ref, low_ref, high_ref, coef_ref, tail_ref,
    part_ref, msg_ref, band_ref, zz_ref,
):
    nx, ny, nz = cond_ref.shape
    carried = adj_ref.shape[0]
    stride = GROUPS * ROWS
    msg_ref[...] = jnp.zeros(msg_ref.shape, F32)
    at = nx - 2
    face = cond_ref[nx - 1] - THIRD
    for group in range(GROUPS):
        for r, value in ((6, tail_ref[at, 0]), (7, tail_ref[at, 1]), (14, face), (15, tail_ref[at, 2])):
            msg_ref[pl.ds(group * ROWS + r, ny, stride=stride), :] = value

    k, z = iota((2 * nz, nz), 0), iota((2 * nz, nz), 1)
    offset = jnp.where(lax.axis_index("gz") == 0, nz, -nz)
    gap = jnp.abs(jnp.where(k < nz, k, k - nz + offset) - z)
    band_ref[...] = jnp.where(
        gap == 0, -60.0, jnp.where(gap == 1, 16.0, jnp.where(gap == 2, -1.0, 0.0))
    ).astype(BF16)
    row = iota((ny, nz), 0)

    @pl.loop(0, carried // LB)
    def _(g):
        for t in range(LB):
            s = g * LB + t
            own_hi, own_lo = split(adj_ref[s].reshape(nx * ny, nz))
            near_hi, near_lo = split(near_ref[s].reshape(nx * ny, nz))
            sides = jnp.concatenate(
                [jnp.concatenate([own_hi, near_hi], axis=1), jnp.concatenate([own_lo, near_lo], axis=1)], axis=0
            )
            spread_z = dot(sides, band_ref[...])
            zz_ref[t] = spread_z[: nx * ny] + spread_z[nx * ny :]
        for t in range(LB):
            s = g * LB + t
            scale = diff_ref[s] * (SECTION * STEP / 12.0)
            b_first, carry = None, None
            for p in range(nx):
                own = adj_ref[s, p]
                low0, low1 = low_ref[s, p, 0:1, :], low_ref[s, p, 1:2, :]
                high0, high1 = high_ref[s, p, 0:1, :], high_ref[s, p, 1:2, :]
                y_up1 = jnp.where(row == ny - 1, high0, pltpu.roll(own, ny - 1, 0))
                y_up2 = jnp.where(row == ny - 1, high1, jnp.where(row == ny - 2, high0, pltpu.roll(own, ny - 2, 0)))
                y_dn1 = jnp.where(row == 0, low1, pltpu.roll(own, 1, 0))
                y_dn2 = jnp.where(row == 0, low0, jnp.where(row == 1, low1, pltpu.roll(own, 2, 0)))
                spread = 16.0 * (y_up1 + y_dn1) - (y_up2 + y_dn2) + zz_ref[t, p * ny : (p + 1) * ny, :]
                b = SECTION * own + (SECTION * STEP) * chem_ref[s, p] + scale * spread
                if p == 0:
                    b_first = b
                elif p < nx - 1:
                    full = b if carry is None else b + carry
                    part_ref[s, p] = full * coef_ref[2, p]
                    b_first = b_first + coef_ref[0, p] * full
                    carry = coef_ref[1, p] * full
                else:
                    b_last = b + carry
            msg_ref[pl.ds(place(s), ny, stride=stride), :] = b_first
            msg_ref[pl.ds(place(s) + 8, ny, stride=stride), :] = b_last


def local_part(diffusivity, adjoint, chem, near, low, high, conduct, coef, ends):
    carried, nx, ny, nz = adjoint.shape
    smem = pl.BlockSpec(memory_space=pltpu.SMEM)
    return pl.pallas_call(
        local_kernel,
        in_specs=[smem] + [WHOLE] * 8,
        out_specs=[WHOLE] * 2,
        out_shape=[
            pltpu.VMEM(adjoint.shape, F32),
            pltpu.VMEM((GROUPS * ny * ROWS, nz), F32),
        ],
        scratch_shapes=[pltpu.VMEM((2 * nz, nz), BF16), pltpu.VMEM((LB, nx * ny, nz), F32)],
        compiler_params=SMALL,
        cost_estimate=pl.CostEstimate(flops=20 * 10**6, bytes_accessed=7 * 10**6, transcendentals=0),
        name="local",
    )(diffusivity, conduct, adjoint, chem, near, low, high, coef, ends)


def chain_kernel(in_ref, out_ref):
    count, _, nz = in_ref.shape
    h, mass, rhs, ends = [], [], [], []
    passed_m = passed_b = None
    for i in range(count):
        low, high = in_ref[i, 0:8, :], in_ref[i, 8:16, :]
        g = jnp.broadcast_to(in_ref[i, 6:7, :], (8, nz))
        m_f = jnp.broadcast_to(in_ref[i, 7:8, :], (8, nz))
        face = jnp.broadcast_to(in_ref[i, 14:15, :], (8, nz))
        m_l = jnp.broadcast_to(in_ref[i, 15:16, :], (8, nz))
        inv = 1.0 / (g + face + m_l)
        a, c = g * inv, face * inv
        m, b = m_f + a * m_l, low + a * high
        if i > 0:
            m, b = m + passed_m, b + passed_b
        passed_m, passed_b = c * m_l, c * high
        h.append(a * face)
        mass.append(m)
        rhs.append(b)
        ends.append((a, c, high * inv))
    half = count // 2
    scale, ratio = [None] * count, [None] * count
    for i in range(half - 1):
        inv = 1.0 / (mass[i] + h[i])
        q = h[i] * inv
        scale[i], ratio[i] = rhs[i] * inv, q
        mass[i + 1] = mass[i + 1] + q * mass[i]
        rhs[i + 1] = rhs[i + 1] + q * rhs[i]
    mass[count - 1] = mass[count - 1] + h[count - 1]
    for i in range(count - 1, half, -1):
        inv = 1.0 / (mass[i] + h[i - 1])
        q = h[i - 1] * inv
        scale[i], ratio[i] = rhs[i] * inv, q
        mass[i - 1] = mass[i - 1] + q * mass[i]
        rhs[i - 1] = rhs[i - 1] + q * rhs[i]
    inv = 1.0 / (mass[half - 1] + h[half - 1])
    q = h[half - 1] * inv
    first = [None] * (count + 1)
    first[half] = (rhs[half] + q * rhs[half - 1]) / (mass[half] + q * mass[half - 1])
    first[half - 1] = rhs[half - 1] * inv + q * first[half]
    for i in range(half - 2, -1, -1):
        first[i] = scale[i] + ratio[i] * first[i + 1]
    for i in range(half + 1, count):
        first[i] = scale[i] + ratio[i] * first[i - 1]
    for i in range(count):
        a, c, part = ends[i]
        last = part + a * first[i]
        if i < count - 1:
            last = last + c * first[i + 1]
        out_ref[i, 0:8, :] = first[i]
        out_ref[i, 8:16, :] = last


def chain(message):
    return pl.pallas_call(
        chain_kernel,
        in_specs=[WHOLE],
        out_specs=WHOLE,
        out_shape=pltpu.VMEM(message.shape, F32),
        compiler_params=SMALL,
        cost_estimate=pl.CostEstimate(flops=10**6, bytes_accessed=10**6, transcendentals=0),
        name="chain",
    )(message)


def back_kernel(coef_ref, ends_ref, part_ref, out_hbm, out_ref, out_sem):
    carried, nx, ny, _ = part_ref.shape
    groups = carried // SB

    def put(g):
        return pltpu.make_async_copy(out_ref.at[pl.ds(g * SB, SB)], out_hbm.at[pl.ds(g * SB, SB)], out_sem.at[g])

    @pl.loop(0, groups)
    def _(g):
        for t in range(SB):
            s = g * SB + t
            first = ends_ref[pl.ds(place(s), ny, stride=GROUPS * ROWS), :]
            value = ends_ref[pl.ds(place(s) + 8, ny, stride=GROUPS * ROWS), :]
            out_ref[s, 0] = first
            out_ref[s, nx - 1] = value
            for p in range(nx - 2, 0, -1):
                value = part_ref[s, p] + coef_ref[0, p] * first + coef_ref[1, p] * value
                out_ref[s, p] = value
        put(g).start()

    @pl.loop(0, groups)
    def _(g):
        put(g).wait()


def back(part, coef, ends):
    groups = part.shape[0] // SB
    return pl.pallas_call(
        back_kernel,
        in_specs=[WHOLE, WHOLE, WHOLE],
        out_specs=ANY,
        out_shape=jax.ShapeDtypeStruct(part.shape, F32),
        scratch_shapes=[pltpu.VMEM(part.shape, F32), pltpu.SemaphoreType.DMA((groups,))],
        compiler_params=SMALL,
        cost_estimate=pl.CostEstimate(flops=2 * 10**6, bytes_accessed=3 * 10**6, transcendentals=0),
        name="back",
    )(coef, ends, part)


def resident(value):
    return pltpu.with_memory_space_constraint(value, pltpu.VMEM)


def shards(
    adjoint, log_conc, levels, conduct, orders_fwd, orders_rev, stoich, rate_fwd, rate_rev, diffusivity
):
    carried, nx, ny, nz = adjoint.shape
    rows_y, blocks = lax.axis_size("gy"), lax.axis_size("gx")
    near = lax.ppermute(adjoint, "gz", [(0, 1), (1, 0)])
    tail, head = edges(adjoint)
    low = lax.ppermute(tail, "gy", [(i, (i + 1) % rows_y) for i in range(rows_y)])
    high = lax.ppermute(head, "gy", [((i + 1) % rows_y, i) for i in range(rows_y)])
    chem, coef, ends_m = chemistry(adjoint, log_conc, levels, conduct, orders_fwd, orders_rev, stoich, rate_fwd, rate_rev)
    part, message = local_part(diffusivity, adjoint, chem, near, low, high, conduct, coef, ends_m)
    message = lax.all_to_all(message.reshape(blocks, ROWS, nz), "gx", 0, 0, tiled=True)
    ends = lax.all_to_all(chain(message), "gx", 0, 0, tiled=True)
    return back(part, coef, ends.reshape(blocks * ROWS, nz))


def solution(mesh):
    cells = P(None, "gx", "gy", "gz")
    planes = P("gx", "gy", "gz")
    in_specs = (cells, cells, planes, planes, P(), P(), P(), P(), P(), P())
    return jax.shard_map(shards, mesh=mesh, in_specs=in_specs, out_specs=cells, check_vma=False)
```

```python
import math

import jax
import jax.numpy as jnp
from jax import lax
from jax.experimental import pallas as pl
from jax.experimental.pallas import tpu as pltpu
from jax.sharding import PartitionSpec as P

SECTION = 0.02
STEP = 0.3
MASS = 0.001
THIRD = MASS / 3.0
BODY = MASS + 2.0 * THIRD
LOG2E = math.log2(math.e)
OFF = -1024.0

K_ROWS = 96
R_PAD = 208
STRIP = 16
CHUNKS = tuple((start, STRIP) for start in range(0, R_PAD, STRIP))
TILE = 1024
XB = 4
LIMIT = 24 * 1024 * 1024
F32 = jnp.float32
BF16 = jnp.bfloat16


def iota(shape, dim):
    return lax.broadcasted_iota(jnp.int32, shape, dim)


def dot(a, b):
    return lax.dot_general(a, b, (((1,), (0,)), ((), ())), preferred_element_type=F32)


def dot_nt(a, b):
    return lax.dot_general(a, b, (((1,), (1,)), ((), ())), preferred_element_type=F32)


def one_hot(mask):
    return jnp.where(mask, 1.0, 0.0).astype(BF16)


def build_weights(of_ref, or_ref, st_ref, rf_ref, rr_ref, wide_ref, w_ref, c_ref):
    species, react = of_ref.shape
    carried = st_ref.shape[0]
    eye = one_hot(iota((R_PAD, 256), 0) == iota((R_PAD, 256), 1))
    pick_row, pick_col = iota((32, 32), 0), iota((32, 32), 1)
    pick = one_hot(pick_col == jnp.where(pick_row < 16, pick_row, jnp.where(pick_row < 24, pick_row - 2, -1)))
    sub, tier = iota((8, 256), 0), 4 * iota((8, 256), 1) // react
    full = []
    for index, (orders, rate) in enumerate(((of_ref, rf_ref), (or_ref, rr_ref))):
        wide_ref[...] = jnp.zeros(wide_ref.shape, F32)
        wide_ref[0:species, 0:react] = orders[...].astype(F32)
        plain = wide_ref[0:32, :]
        sign = 1.0 if index == 0 else -1.0
        c_ref[index] = (sign * dot(pick, plain.astype(BF16)))[:, 0:R_PAD].astype(BF16)
        scaled = plain * LOG2E
        hi = scaled.astype(BF16).astype(F32)
        wide_ref[0:32, :] = hi
        wide_ref[32:64, :] = scaled - hi
        wide_ref[88:89, 0:react] = jnp.log(rate[...]) * LOG2E
        r = jnp.broadcast_to(wide_ref[88:89, :], (8, 256))
        r0 = r.astype(BF16).astype(F32)
        r1 = (r - r0).astype(BF16).astype(F32)
        parts = jnp.where(sub == 3, r0, jnp.where(sub == 4, r1, jnp.where(sub == 5, r - r0 - r1, 0.0)))
        wide_ref[88:96, :] = jnp.where(sub < 3, jnp.where(tier > sub, OFF, 0.0), parts)
        full.append(dot_nt(eye, wide_ref[...].astype(BF16)).astype(BF16))
    wide_ref[...] = jnp.zeros(wide_ref.shape, F32)
    wide_ref[64:80, 0:react] = st_ref[0:16, :].astype(F32)
    wide_ref[82 : 66 + carried, 0:react] = st_ref[16:carried, :].astype(F32)
    full.append(dot_nt(eye, wide_ref[...].astype(BF16)).astype(BF16))
    base = 0
    for start, size in CHUNKS:
        for part in full:
            w_ref[base : base + size, :] = part[start : start + size]
            base += size


def chem_kernel(
    adj_ref, conc_ref, lev_ref, cond_ref, of_ref, or_ref, st_ref, rf_ref, rr_ref,
    out_ref, coef_ref, tail_ref,
    wide_ref, w_ref, c_ref, conc32_ref, x_ref, act_ref, run_ref,
):
    step = pl.program_id(0)

    @pl.when(step == 0)
    def _():
        run_ref[0] = cond_ref[0] - THIRD
        run_ref[1] = jnp.where(lax.axis_index("gx") == 0, MASS + THIRD, BODY) * jnp.ones(run_ref.shape[1:], F32)
        run_ref[2] = jnp.full(run_ref.shape[1:], BODY, F32)
        build_weights(of_ref, or_ref, st_ref, rf_ref, rr_ref, wide_ref, w_ref, c_ref)

    gap, mass_first, mass = run_ref[0], run_ref[1], run_ref[2]
    for q in range(1, XB + 1):
        p = step * XB + q
        after = cond_ref[jnp.minimum(p, cond_ref.shape[0] - 1)] - THIRD
        inv = 1.0 / (gap + after + mass)
        alpha, beta = gap * inv, after * inv
        coef_ref[0, p], coef_ref[1, p], coef_ref[2, p] = alpha, beta, inv
        mass_first = mass_first + alpha * mass
        mass = BODY + beta * mass
        gap = alpha * after
        tail_ref[p, 0], tail_ref[p, 1], tail_ref[p, 2] = gap, mass_first, mass
    run_ref[0], run_ref[1], run_ref[2] = gap, mass_first, mass

    carried, xb, ny, nz = adj_ref.shape
    species = conc_ref.shape[0]
    adj_rows = adj_ref.reshape(carried * xb * ny, nz)
    out_rows = out_ref.reshape(carried * xb * ny, nz)
    pitch = xb * ny
    conc32_ref[...] = conc_ref[...].astype(F32).reshape(species * pitch, nz)
    sub = iota((8, nz), 0)
    for x in range(xb):
        for y in range(ny):
            row = x * ny + y
            cols = slice(y * nz, (y + 1) * nz)
            conc = jnp.concatenate(
                [conc32_ref[pl.ds(row + 8 * q * pitch, 8, stride=pitch), :] for q in range(4)], axis=0
            ).astype(BF16)
            x_ref[x, 0:32, cols] = conc
            x_ref[x, 32:64, cols] = conc
            lam = [adj_rows[pl.ds(row + first * pitch, 8, stride=pitch), :] for first in (0, 8, carried - 8)]
            level = jnp.broadcast_to(lev_ref[x, y : y + 1, :], (8, nz))
            marks = jnp.where(level <= sub, 1.0, 0.0)
            x_ref[x, 64:96, cols] = jnp.concatenate(lam + [marks], axis=0).astype(BF16)
    per_tile = TILE // nz
    for x in range(xb):
        for tile in range(ny // per_tile):
            slot = (x * (ny // per_tile) + tile) % act_ref.shape[0]
            data = x_ref[x, :, tile * TILE : (tile + 1) * TILE]
            every = dot(w_ref[...], data)
            for start, size in CHUNKS:
                got = every[3 * start : 3 * (start + size)]
                weight = got[2 * size :]
                act_ref[slot, 0, start : start + size, :] = (jnp.exp2(got[:size]) * weight).astype(BF16)
                act_ref[slot, 1, start : start + size, :] = (jnp.exp2(got[size : 2 * size]) * weight).astype(BF16)
            chem = dot(c_ref[0], act_ref[slot, 0]) + dot(c_ref[1], act_ref[slot, 1])
            for part in range(per_tile):
                row = x * ny + tile * per_tile + part
                for q, first in enumerate((0, 8, carried - 8)):
                    out_rows[pl.ds(row + first * pitch, 8, stride=pitch), :] = chem[
                        8 * q : 8 * q + 8, part * nz : (part + 1) * nz
                    ]


def chemistry(adjoint, log_conc, levels, conduct, orders_fwd, orders_rev, stoich, rate_fwd, rate_rev):
    carried, nx, ny, nz = adjoint.shape
    species, react = log_conc.shape[0], orders_fwd.shape[0]
    whole = lambda a: pl.BlockSpec(a.shape, lambda i: (0,) * len(a.shape))
    small = [orders_fwd.T, orders_rev.T, stoich.T, rate_fwd.reshape(1, react), rate_rev.reshape(1, react)]
    return pl.pallas_call(
        chem_kernel,
        grid=(nx // XB,),
        in_specs=[
            pl.BlockSpec((carried, XB, ny, nz), lambda i: (0, i, 0, 0)),
            pl.BlockSpec((species, XB, ny, nz), lambda i: (0, i, 0, 0)),
            pl.BlockSpec((XB, ny, nz), lambda i: (i, 0, 0)),
            whole(conduct),
        ]
        + [whole(a) for a in small],
        out_specs=[
            pl.BlockSpec((carried, XB, ny, nz), lambda i: (0, i, 0, 0)),
            pl.BlockSpec((3, nx + 1, ny, nz), lambda i: (0, 0, 0, 0)),
            pl.BlockSpec((nx + 1, 3, ny, nz), lambda i: (0, 0, 0, 0)),
        ],
        out_shape=[
            jax.ShapeDtypeStruct(adjoint.shape, F32),
            jax.ShapeDtypeStruct((3, nx + 1, ny, nz), F32),
            jax.ShapeDtypeStruct((nx + 1, 3, ny, nz), F32),
        ],
        scratch_shapes=[
            pltpu.VMEM((K_ROWS, 256), F32),
            pltpu.VMEM((3 * R_PAD, K_ROWS), BF16),
            pltpu.VMEM((2, 32, R_PAD), BF16),
            pltpu.VMEM((species * XB * ny, nz), F32),
            pltpu.VMEM((XB, K_ROWS, ny * nz), BF16),
            pltpu.VMEM((2, 2, R_PAD, TILE), BF16),
            pltpu.VMEM((3, ny, nz), F32),
        ],
        compiler_params=pltpu.CompilerParams(dimension_semantics=("arbitrary",), vmem_limit_bytes=LIMIT),
        cost_estimate=pl.CostEstimate(flops=12 * 10**9, bytes_accessed=4 * 10**6, transcendentals=6_750_000),
        name="chem",
    )(adjoint, log_conc, levels, conduct, *small)


GROUP = 6
GROUPS = 4
ROWS = 16
SB = 2
LB = 11
ANY = pl.BlockSpec(memory_space=pl.ANY)
WHOLE = pl.BlockSpec(memory_space=pltpu.VMEM)
SMALL = pltpu.CompilerParams(vmem_limit_bytes=LIMIT)


def edges_kernel(adj_ref, low_ref, high_ref):
    carried, nx, ny, nz = adj_ref.shape
    mine = lax.axis_index("gy")
    to_high = jnp.where(mine == lax.axis_size("gy") - 1, 0.0, 1.0)
    to_low = jnp.where(mine == 0, 0.0, 1.0)

    @pl.loop(0, carried)
    def _(s):
        for x in range(nx):
            low_ref[s, x] = adj_ref[s, x, ny - 2 : ny, :] * to_high
            high_ref[s, x] = adj_ref[s, x, 0:2, :] * to_low


def edges(adjoint):
    carried, nx, ny, nz = adjoint.shape
    shape = pltpu.VMEM((carried, nx, 2, nz), F32)
    return pl.pallas_call(
        edges_kernel,
        in_specs=[WHOLE],
        out_specs=[WHOLE, WHOLE],
        out_shape=[shape, shape],
        compiler_params=SMALL,
        cost_estimate=pl.CostEstimate(flops=0, bytes_accessed=2 * 10**6, transcendentals=0),
        name="edges",
    )(adjoint)


def split(value):
    high = value.astype(BF16)
    return high, (value - high.astype(F32)).astype(BF16)


def local_kernel(
    diff_ref, cond_ref, adj_ref, chem_ref, near_ref, low_ref, high_ref, coef_ref, tail_ref,
    part_ref, *rest,
):
    send_refs, (msg_ref, band_ref, zz_ref) = rest[:GROUPS], rest[GROUPS:]
    nx, ny, nz = cond_ref.shape
    carried = adj_ref.shape[0]
    at = nx - 2
    face = cond_ref[nx - 1] - THIRD
    for group in range(GROUPS):
        for r, value in ((6, tail_ref[at, 0]), (7, tail_ref[at, 1]), (14, face), (15, tail_ref[at, 2])):
            msg_ref[group, r] = value
    for r in range(carried - GROUP * (GROUPS - 1), GROUP):
        msg_ref[GROUPS - 1, r] = jnp.zeros((ny, nz), F32)
        msg_ref[GROUPS - 1, r + 8] = jnp.zeros((ny, nz), F32)

    k, z = iota((2 * nz, nz), 0), iota((2 * nz, nz), 1)
    offset = jnp.where(lax.axis_index("gz") == 0, nz, -nz)
    gap = jnp.abs(jnp.where(k < nz, k, k - nz + offset) - z)
    band_ref[...] = jnp.where(
        gap == 0, -60.0, jnp.where(gap == 1, 16.0, jnp.where(gap == 2, -1.0, 0.0))
    ).astype(BF16)
    row = iota((ny, nz), 0)

    @pl.loop(0, carried // LB)
    def _(g):
        for t in range(LB):
            s = g * LB + t
            own_hi, own_lo = split(adj_ref[s].reshape(nx * ny, nz))
            near_hi, near_lo = split(near_ref[s].reshape(nx * ny, nz))
            sides = jnp.concatenate(
                [jnp.concatenate([own_hi, near_hi], axis=1), jnp.concatenate([own_lo, near_lo], axis=1)], axis=0
            )
            spread_z = dot(sides, band_ref[...])
            zz_ref[t] = spread_z[: nx * ny] + spread_z[nx * ny :]
        for t in range(LB):
            s = g * LB + t
            scale = diff_ref[s] * (SECTION * STEP / 12.0)
            b_first, carry = None, None
            for p in range(nx):
                own = adj_ref[s, p]
                low0, low1 = low_ref[s, p, 0:1, :], low_ref[s, p, 1:2, :]
                high0, high1 = high_ref[s, p, 0:1, :], high_ref[s, p, 1:2, :]
                y_up1 = jnp.where(row == ny - 1, high0, pltpu.roll(own, ny - 1, 0))
                y_up2 = jnp.where(row == ny - 1, high1, jnp.where(row == ny - 2, high0, pltpu.roll(own, ny - 2, 0)))
                y_dn1 = jnp.where(row == 0, low1, pltpu.roll(own, 1, 0))
                y_dn2 = jnp.where(row == 0, low0, jnp.where(row == 1, low1, pltpu.roll(own, 2, 0)))
                spread = 16.0 * (y_up1 + y_dn1) - (y_up2 + y_dn2) + zz_ref[t, p * ny : (p + 1) * ny, :]
                b = SECTION * own + (SECTION * STEP) * chem_ref[s, p] + scale * spread
                if p == 0:
                    b_first = b
                elif p < nx - 1:
                    full = b if carry is None else b + carry
                    part_ref[s, p] = full * coef_ref[2, p]
                    b_first = b_first + coef_ref[0, p] * full
                    carry = coef_ref[1, p] * full
                else:
                    b_last = b + carry
            msg_ref[s // GROUP, s % GROUP] = b_first
            msg_ref[s // GROUP, s % GROUP + 8] = b_last

    mine = lax.axis_index("gx") % GROUPS
    for turn in range(GROUPS):
        send_refs[turn][...] = msg_ref[(mine + turn) % GROUPS]


def local_part(diffusivity, adjoint, chem, near, low, high, conduct, coef, ends):
    carried, nx, ny, nz = adjoint.shape
    smem = pl.BlockSpec(memory_space=pltpu.SMEM)
    return pl.pallas_call(
        local_kernel,
        in_specs=[smem] + [WHOLE] * 8,
        out_specs=[WHOLE] * (1 + GROUPS),
        out_shape=[pltpu.VMEM(adjoint.shape, F32)] + [pltpu.VMEM((ROWS, ny, nz), F32)] * GROUPS,
        scratch_shapes=[
            pltpu.VMEM((GROUPS, ROWS, ny, nz), F32),
            pltpu.VMEM((2 * nz, nz), BF16),
            pltpu.VMEM((LB, nx * ny, nz), F32),
        ],
        compiler_params=SMALL,
        cost_estimate=pl.CostEstimate(flops=20 * 10**6, bytes_accessed=7 * 10**6, transcendentals=0),
        name="local",
    )(diffusivity, conduct, adjoint, chem, near, low, high, coef, ends)


def reduce_kernel(*refs):
    got_refs, (msg_ref, part_ref, coef_ref, in_ref) = refs[:GROUPS], refs[GROUPS:]
    mine = lax.axis_index("gx") % GROUPS
    for turn in range(GROUPS):
        in_ref[(mine + GROUPS - turn) % GROUPS] = got_refs[turn][...]
    gap, mass_first = in_ref[0, 6], in_ref[0, 7]
    first = [in_ref[0, r] for r in range(GROUP)]
    mass = in_ref[0, 15]
    rhs = [in_ref[0, 8 + r] for r in range(GROUP)]
    for node in range(2 * GROUPS - 2):
        block, end = (node + 1) // 2, node % 2 == 1
        after = in_ref[block, 6] if end else in_ref[block, 14]
        inv = 1.0 / (gap + after + mass)
        alpha, beta = gap * inv, after * inv
        coef_ref[0, node], coef_ref[1, node] = alpha, beta
        base, block = (8, block) if end else (0, block + 1)
        for r in range(GROUP):
            part_ref[node, r] = rhs[r] * inv
            first[r] = first[r] + alpha * rhs[r]
            rhs[r] = in_ref[block, base + r] + beta * rhs[r]
        mass_first = mass_first + alpha * mass
        mass = in_ref[block, base + 7] + beta * mass
        gap = alpha * after
    for r, plane in enumerate(first + [gap, mass_first] + rhs + [in_ref[GROUPS - 1, 14], mass]):
        msg_ref[r] = plane


def reduce_blocks(got):
    plane = got[0].shape[1:]
    return pl.pallas_call(
        reduce_kernel,
        in_specs=[WHOLE] * GROUPS,
        out_specs=[WHOLE] * 3,
        out_shape=[
            pltpu.VMEM((ROWS,) + plane, F32),
            pltpu.VMEM((2 * GROUPS - 2, GROUP) + plane, F32),
            pltpu.VMEM((2, 2 * GROUPS - 2) + plane, F32),
        ],
        scratch_shapes=[pltpu.VMEM((GROUPS, ROWS) + plane, F32)],
        compiler_params=SMALL,
        cost_estimate=pl.CostEstimate(flops=10**6, bytes_accessed=10**6, transcendentals=0),
        name="reduce",
    )(*got)


def chain_kernel(*refs):
    count = len(refs) - GROUPS - 5
    got_refs, (part_ref, coef_ref) = refs[:count], refs[count : count + 2]
    send_refs, (in_ref, ends_ref, out_ref) = refs[count + 2 : count + 2 + GROUPS], refs[count + 2 + GROUPS :]
    device = lax.axis_index("gx")
    mine, home = device % GROUPS, device // GROUPS
    for turn in range(count):
        in_ref[(home + count - turn) % count] = got_refs[turn][...]
    h, mass, rhs, ends = [], [], [], []
    passed_m = passed_b = None
    for i in range(count):
        g, m_f, face, m_l = in_ref[i, 6], in_ref[i, 7], in_ref[i, 14], in_ref[i, 15]
        inv = 1.0 / (g + face + m_l)
        a, c = g * inv, face * inv
        m = m_f + a * m_l
        b = [in_ref[i, r] + a * in_ref[i, 8 + r] for r in range(GROUP)]
        if i > 0:
            m, b = m + passed_m, [p + q for p, q in zip(b, passed_b)]
        passed_m, passed_b = c * m_l, [c * in_ref[i, 8 + r] for r in range(GROUP)]
        h.append(a * face)
        mass.append(m)
        rhs.append(b)
        ends.append((a, c, inv))
    half = count // 2
    scale, ratio = [None] * count, [None] * count

    def pass_on(i, k, link):
        inv = 1.0 / (mass[i] + link)
        q = link * inv
        scale[i], ratio[i] = [v * inv for v in rhs[i]], q
        mass[k] = mass[k] + q * mass[i]
        rhs[k] = [v + q * w for v, w in zip(rhs[k], rhs[i])]

    for i in range(half):
        pass_on(i, i + 1, h[i])
    mass[count - 1] = mass[count - 1] + h[count - 1]
    for i in range(count - 1, half, -1):
        pass_on(i, i - 1, h[i - 1])
    first = [None] * count
    inv = 1.0 / mass[half]
    first[half] = [v * inv for v in rhs[half]]
    for i in list(range(half - 1, -1, -1)) + list(range(half + 1, count)):
        k = i + 1 if i < half else i - 1
        first[i] = [v + ratio[i] * w for v, w in zip(scale[i], first[k])]
    for i in range(count):
        a, c, inv = ends[i]
        for r in range(GROUP):
            last = in_ref[i, 8 + r] * inv + a * first[i][r]
            if i < count - 1:
                last = last + c * first[i + 1][r]
            ends_ref[i, r] = first[i][r]
            ends_ref[i, GROUP + r] = last
    for r in range(GROUP):
        start = ends_ref[home, r]
        value = ends_ref[home, GROUP + r]
        out_ref[0, r] = start
        out_ref[GROUPS - 1, GROUP + r] = value
        for node in range(2 * GROUPS - 3, -1, -1):
            value = part_ref[node, r] + coef_ref[0, node] * start + coef_ref[1, node] * value
            block, end = (node + 1) // 2, node % 2 == 1
            out_ref[block, r if end else GROUP + r] = value
    for turn in range(GROUPS):
        send_refs[turn][...] = out_ref[(mine + turn) % GROUPS]


def chain(got, part, coef):
    plane = part.shape[2:]
    count = len(got)
    return pl.pallas_call(
        chain_kernel,
        in_specs=[WHOLE] * (count + 2),
        out_specs=[WHOLE] * GROUPS,
        out_shape=[pltpu.VMEM((2 * GROUP,) + plane, F32)] * GROUPS,
        scratch_shapes=[
            pltpu.VMEM((count, ROWS) + plane, F32),
            pltpu.VMEM((count, 2 * GROUP) + plane, F32),
            pltpu.VMEM((GROUPS, 2 * GROUP) + plane, F32),
        ],
        compiler_params=SMALL,
        cost_estimate=pl.CostEstimate(flops=10**6, bytes_accessed=10**6, transcendentals=0),
        name="chain",
    )(*got, part, coef)


def back_kernel(coef_ref, part_ref, *refs):
    got_refs, (out_hbm, ends_ref, out_ref, out_sem) = refs[:GROUPS], refs[GROUPS:]
    carried, nx, ny, _ = part_ref.shape
    groups = carried // SB
    mine = lax.axis_index("gx") % GROUPS
    for turn in range(GROUPS):
        ends_ref[(mine + GROUPS - turn) % GROUPS] = got_refs[turn][...]

    def put(g):
        return pltpu.make_async_copy(out_ref.at[pl.ds(g * SB, SB)], out_hbm.at[pl.ds(g * SB, SB)], out_sem.at[g])

    @pl.loop(0, groups)
    def _(g):
        for t in range(SB):
            s = g * SB + t
            first = ends_ref[s // GROUP, s % GROUP]
            value = ends_ref[s // GROUP, s % GROUP + GROUP]
            out_ref[s, 0] = first
            out_ref[s, nx - 1] = value
            for p in range(nx - 2, 0, -1):
                value = part_ref[s, p] + coef_ref[0, p] * first + coef_ref[1, p] * value
                out_ref[s, p] = value
        put(g).start()

    @pl.loop(0, groups)
    def _(g):
        put(g).wait()


def back(part, coef, got):
    groups = part.shape[0] // SB
    return pl.pallas_call(
        back_kernel,
        in_specs=[WHOLE] * (2 + GROUPS),
        out_specs=ANY,
        out_shape=jax.ShapeDtypeStruct(part.shape, F32),
        scratch_shapes=[
            pltpu.VMEM((GROUPS, 2 * GROUP) + part.shape[2:], F32),
            pltpu.VMEM(part.shape, F32),
            pltpu.SemaphoreType.DMA((groups,)),
        ],
        compiler_params=SMALL,
        cost_estimate=pl.CostEstimate(flops=2 * 10**6, bytes_accessed=3 * 10**6, transcendentals=0),
        name="back",
    )(coef, part, *got)


def shards(
    adjoint, log_conc, levels, conduct, orders_fwd, orders_rev, stoich, rate_fwd, rate_rev, diffusivity
):
    rows_y, blocks = lax.axis_size("gy"), lax.axis_size("gx")
    supers = blocks // GROUPS
    near = lax.ppermute(adjoint, "gz", [(0, 1), (1, 0)])
    tail, head = edges(adjoint)
    low = lax.ppermute(tail, "gy", [(i, (i + 1) % rows_y) for i in range(rows_y)])
    high = lax.ppermute(head, "gy", [((i + 1) % rows_y, i) for i in range(rows_y)])
    chem, coef, ends_m = chemistry(
        adjoint, log_conc, levels, conduct, orders_fwd, orders_rev, stoich, rate_fwd, rate_rev
    )
    part, *send = local_part(diffusivity, adjoint, chem, near, low, high, conduct, coef, ends_m)

    def close(value, turn):
        if turn == 0:
            return value
        pairs = [(i, i // GROUPS * GROUPS + (i + turn) % GROUPS) for i in range(blocks)]
        return lax.ppermute(value, "gx", pairs)

    def far(value, turn):
        if turn == 0:
            return value
        return lax.ppermute(value, "gx", [(i, (i + turn * GROUPS) % blocks) for i in range(blocks)])

    message, inner, links = reduce_blocks([close(value, turn) for turn, value in enumerate(send)])
    send = chain([far(message, turn) for turn in range(supers)], inner, links)
    return back(part, coef, [close(value, turn) for turn, value in enumerate(send)])


def solution(mesh):
    cells = P(None, "gx", "gy", "gz")
    planes = P("gx", "gy", "gz")
    in_specs = (cells, cells, planes, planes, P(), P(), P(), P(), P(), P())
    return jax.shard_map(shards, mesh=mesh, in_specs=in_specs, out_specs=cells, check_vma=False)
```

```python
import math

import jax
import jax.numpy as jnp
from jax import lax
from jax.experimental import pallas as pl
from jax.experimental.pallas import tpu as pltpu
from jax.sharding import PartitionSpec as P

SECTION = 0.02
STEP = 0.3
MASS = 0.001
THIRD = MASS / 3.0
BODY = MASS + 2.0 * THIRD
LOG2E = math.log2(math.e)
OFF = -1024.0

K_ROWS = 96
R_PAD = 208
STRIP = 16
CHUNKS = tuple((start, STRIP) for start in range(0, R_PAD, STRIP))
TILE = 1024
XB = 4
LIMIT = 24 * 1024 * 1024
F32 = jnp.float32
BF16 = jnp.bfloat16


def iota(shape, dim):
    return lax.broadcasted_iota(jnp.int32, shape, dim)


def dot(a, b):
    return lax.dot_general(a, b, (((1,), (0,)), ((), ())), preferred_element_type=F32)


def dot_nt(a, b):
    return lax.dot_general(a, b, (((1,), (1,)), ((), ())), preferred_element_type=F32)


def one_hot(mask):
    return jnp.where(mask, 1.0, 0.0).astype(BF16)


def build_weights(of_ref, or_ref, st_ref, rf_ref, rr_ref, wide_ref, w_ref, c_ref):
    species, react = of_ref.shape
    carried = st_ref.shape[0]
    eye = one_hot(iota((R_PAD, 256), 0) == iota((R_PAD, 256), 1))
    pick_row, pick_col = iota((32, 32), 0), iota((32, 32), 1)
    pick = one_hot(pick_col == jnp.where(pick_row < 16, pick_row, jnp.where(pick_row < 24, pick_row - 2, -1)))
    sub, tier = iota((8, 256), 0), 4 * iota((8, 256), 1) // react
    full = []
    for index, (orders, rate) in enumerate(((of_ref, rf_ref), (or_ref, rr_ref))):
        wide_ref[...] = jnp.zeros(wide_ref.shape, F32)
        wide_ref[0:species, 0:react] = orders[...].astype(F32)
        plain = wide_ref[0:32, :]
        sign = 1.0 if index == 0 else -1.0
        c_ref[index] = (sign * dot(pick, plain.astype(BF16)))[:, 0:R_PAD].astype(BF16)
        scaled = plain * LOG2E
        hi = scaled.astype(BF16).astype(F32)
        wide_ref[0:32, :] = hi
        wide_ref[32:64, :] = scaled - hi
        wide_ref[88:89, 0:react] = jnp.log(rate[...]) * LOG2E
        r = jnp.broadcast_to(wide_ref[88:89, :], (8, 256))
        r0 = r.astype(BF16).astype(F32)
        r1 = (r - r0).astype(BF16).astype(F32)
        parts = jnp.where(sub == 3, r0, jnp.where(sub == 4, r1, jnp.where(sub == 5, r - r0 - r1, 0.0)))
        wide_ref[88:96, :] = jnp.where(sub < 3, jnp.where(tier > sub, OFF, 0.0), parts)
        full.append(dot_nt(eye, wide_ref[...].astype(BF16)).astype(BF16))
    wide_ref[...] = jnp.zeros(wide_ref.shape, F32)
    wide_ref[64:80, 0:react] = st_ref[0:16, :].astype(F32)
    wide_ref[82 : 66 + carried, 0:react] = st_ref[16:carried, :].astype(F32)
    full.append(dot_nt(eye, wide_ref[...].astype(BF16)).astype(BF16))
    base = 0
    for start, size in CHUNKS:
        for part in full:
            w_ref[base : base + size, :] = part[start : start + size]
            base += size


def chem_kernel(
    adj_ref, conc_ref, lev_ref, cond_ref, of_ref, or_ref, st_ref, rf_ref, rr_ref,
    out_ref, coef_ref, tail_ref,
    wide_ref, w_ref, c_ref, conc32_ref, x_ref, act_ref, run_ref,
):
    step = pl.program_id(0)

    @pl.when(step == 0)
    def _():
        run_ref[0] = cond_ref[0] - THIRD
        run_ref[1] = jnp.where(lax.axis_index("gx") == 0, MASS + THIRD, BODY) * jnp.ones(run_ref.shape[1:], F32)
        run_ref[2] = jnp.full(run_ref.shape[1:], BODY, F32)
        build_weights(of_ref, or_ref, st_ref, rf_ref, rr_ref, wide_ref, w_ref, c_ref)

    gap, mass_first, mass = run_ref[0], run_ref[1], run_ref[2]
    for q in range(1, XB + 1):
        p = step * XB + q
        after = cond_ref[jnp.minimum(p, cond_ref.shape[0] - 1)] - THIRD
        inv = 1.0 / (gap + after + mass)
        alpha, beta = gap * inv, after * inv
        coef_ref[0, p], coef_ref[1, p], coef_ref[2, p] = alpha, beta, inv
        mass_first = mass_first + alpha * mass
        mass = BODY + beta * mass
        gap = alpha * after
        tail_ref[p, 0], tail_ref[p, 1], tail_ref[p, 2] = gap, mass_first, mass
    run_ref[0], run_ref[1], run_ref[2] = gap, mass_first, mass

    carried, xb, ny, nz = adj_ref.shape
    species = conc_ref.shape[0]
    adj_rows = adj_ref.reshape(carried * xb * ny, nz)
    out_rows = out_ref.reshape(carried * xb * ny, nz)
    pitch = xb * ny
    conc32_ref[...] = conc_ref[...].astype(F32).reshape(species * pitch, nz)
    sub = iota((8, nz), 0)
    for x in range(xb):
        for y in range(ny):
            row = x * ny + y
            cols = slice(y * nz, (y + 1) * nz)
            conc = jnp.concatenate(
                [conc32_ref[pl.ds(row + 8 * q * pitch, 8, stride=pitch), :] for q in range(4)], axis=0
            ).astype(BF16)
            x_ref[x, 0:32, cols] = conc
            x_ref[x, 32:64, cols] = conc
            lam = [adj_rows[pl.ds(row + first * pitch, 8, stride=pitch), :] for first in (0, 8, carried - 8)]
            level = jnp.broadcast_to(lev_ref[x, y : y + 1, :], (8, nz))
            marks = jnp.where(level <= sub, 1.0, 0.0)
            x_ref[x, 64:96, cols] = jnp.concatenate(lam + [marks], axis=0).astype(BF16)
    per_tile = TILE // nz
    for x in range(xb):
        for tile in range(ny // per_tile):
            slot = (x * (ny // per_tile) + tile) % act_ref.shape[0]
            data = x_ref[x, :, tile * TILE : (tile + 1) * TILE]
            every = dot(w_ref[...], data)
            for start, size in CHUNKS:
                got = every[3 * start : 3 * (start + size)]
                weight = got[2 * size :]
                act_ref[slot, 0, start : start + size, :] = (jnp.exp2(got[:size]) * weight).astype(BF16)
                act_ref[slot, 1, start : start + size, :] = (jnp.exp2(got[size : 2 * size]) * weight).astype(BF16)
            chem = dot(c_ref[0], act_ref[slot, 0]) + dot(c_ref[1], act_ref[slot, 1])
            for part in range(per_tile):
                row = x * ny + tile * per_tile + part
                for q, first in enumerate((0, 8, carried - 8)):
                    out_rows[pl.ds(row + first * pitch, 8, stride=pitch), :] = chem[
                        8 * q : 8 * q + 8, part * nz : (part + 1) * nz
                    ]


def chemistry(adjoint, log_conc, levels, conduct, orders_fwd, orders_rev, stoich, rate_fwd, rate_rev):
    carried, nx, ny, nz = adjoint.shape
    species, react = log_conc.shape[0], orders_fwd.shape[0]
    whole = lambda a: pl.BlockSpec(a.shape, lambda i: (0,) * len(a.shape))
    small = [orders_fwd.T, orders_rev.T, stoich.T, rate_fwd.reshape(1, react), rate_rev.reshape(1, react)]
    return pl.pallas_call(
        chem_kernel,
        grid=(nx // XB,),
        in_specs=[
            pl.BlockSpec((carried, XB, ny, nz), lambda i: (0, i, 0, 0)),
            pl.BlockSpec((species, XB, ny, nz), lambda i: (0, i, 0, 0)),
            pl.BlockSpec((XB, ny, nz), lambda i: (i, 0, 0)),
            whole(conduct),
        ]
        + [whole(a) for a in small],
        out_specs=[
            pl.BlockSpec((carried, XB, ny, nz), lambda i: (0, i, 0, 0)),
            pl.BlockSpec((3, nx + 1, ny, nz), lambda i: (0, 0, 0, 0)),
            pl.BlockSpec((nx + 1, 3, ny, nz), lambda i: (0, 0, 0, 0)),
        ],
        out_shape=[
            jax.ShapeDtypeStruct(adjoint.shape, F32),
            jax.ShapeDtypeStruct((3, nx + 1, ny, nz), F32),
            jax.ShapeDtypeStruct((nx + 1, 3, ny, nz), F32),
        ],
        scratch_shapes=[
            pltpu.VMEM((K_ROWS, 256), F32),
            pltpu.VMEM((3 * R_PAD, K_ROWS), BF16),
            pltpu.VMEM((2, 32, R_PAD), BF16),
            pltpu.VMEM((species * XB * ny, nz), F32),
            pltpu.VMEM((XB, K_ROWS, ny * nz), BF16),
            pltpu.VMEM((2, 2, R_PAD, TILE), BF16),
            pltpu.VMEM((3, ny, nz), F32),
        ],
        compiler_params=pltpu.CompilerParams(dimension_semantics=("arbitrary",), vmem_limit_bytes=LIMIT),
        cost_estimate=pl.CostEstimate(flops=12 * 10**9, bytes_accessed=4 * 10**6, transcendentals=6_750_000),
        name="chem",
    )(adjoint, log_conc, levels, conduct, *small)


GROUP = 6
GROUPS = 4
ROWS = 16
PAIR = 2
SB = 2
LB = 11
ANY = pl.BlockSpec(memory_space=pl.ANY)
WHOLE = pl.BlockSpec(memory_space=pltpu.VMEM)
SMALL = pltpu.CompilerParams(vmem_limit_bytes=LIMIT)


def edges_kernel(adj_ref, low_ref, high_ref):
    carried, nx, ny, nz = adj_ref.shape
    mine = lax.axis_index("gy")
    to_high = jnp.where(mine == lax.axis_size("gy") - 1, 0.0, 1.0)
    to_low = jnp.where(mine == 0, 0.0, 1.0)

    @pl.loop(0, carried)
    def _(s):
        for x in range(nx):
            low_ref[s, x] = adj_ref[s, x, ny - 2 : ny, :] * to_high
            high_ref[s, x] = adj_ref[s, x, 0:2, :] * to_low


def edges(adjoint):
    carried, nx, ny, nz = adjoint.shape
    shape = pltpu.VMEM((carried, nx, 2, nz), F32)
    return pl.pallas_call(
        edges_kernel,
        in_specs=[WHOLE],
        out_specs=[WHOLE, WHOLE],
        out_shape=[shape, shape],
        compiler_params=SMALL,
        cost_estimate=pl.CostEstimate(flops=0, bytes_accessed=2 * 10**6, transcendentals=0),
        name="edges",
    )(adjoint)


def split(value):
    high = value.astype(BF16)
    return high, (value - high.astype(F32)).astype(BF16)


def local_kernel(
    diff_ref, cond_ref, adj_ref, chem_ref, near_ref, low_ref, high_ref, coef_ref, tail_ref,
    part_ref, *rest,
):
    send_refs, (msg_ref, band_ref, zz_ref) = rest[:GROUPS], rest[GROUPS:]
    nx, ny, nz = cond_ref.shape
    carried = adj_ref.shape[0]
    at = nx - 2
    face = cond_ref[nx - 1] - THIRD
    for group in range(GROUPS):
        for r, value in ((6, tail_ref[at, 0]), (7, tail_ref[at, 1]), (14, face), (15, tail_ref[at, 2])):
            msg_ref[group, r] = value
    for r in range(carried - GROUP * (GROUPS - 1), GROUP):
        msg_ref[GROUPS - 1, r] = jnp.zeros((ny, nz), F32)
        msg_ref[GROUPS - 1, r + 8] = jnp.zeros((ny, nz), F32)

    k, z = iota((2 * nz, nz), 0), iota((2 * nz, nz), 1)
    offset = jnp.where(lax.axis_index("gz") == 0, nz, -nz)
    gap = jnp.abs(jnp.where(k < nz, k, k - nz + offset) - z)
    band_ref[...] = jnp.where(
        gap == 0, -60.0, jnp.where(gap == 1, 16.0, jnp.where(gap == 2, -1.0, 0.0))
    ).astype(BF16)
    row = iota((ny, nz), 0)

    @pl.loop(0, carried // LB)
    def _(g):
        for t in range(LB):
            s = g * LB + t
            own_hi, own_lo = split(adj_ref[s].reshape(nx * ny, nz))
            near_hi, near_lo = split(near_ref[s].reshape(nx * ny, nz))
            sides = jnp.concatenate(
                [jnp.concatenate([own_hi, near_hi], axis=1), jnp.concatenate([own_lo, near_lo], axis=1)], axis=0
            )
            spread_z = dot(sides, band_ref[...])
            zz_ref[t] = spread_z[: nx * ny] + spread_z[nx * ny :]
        for t in range(LB):
            s = g * LB + t
            scale = diff_ref[s] * (SECTION * STEP / 12.0)
            b_first, carry = None, None
            for p in range(nx):
                own = adj_ref[s, p]
                low0, low1 = low_ref[s, p, 0:1, :], low_ref[s, p, 1:2, :]
                high0, high1 = high_ref[s, p, 0:1, :], high_ref[s, p, 1:2, :]
                y_up1 = jnp.where(row == ny - 1, high0, pltpu.roll(own, ny - 1, 0))
                y_up2 = jnp.where(row == ny - 1, high1, jnp.where(row == ny - 2, high0, pltpu.roll(own, ny - 2, 0)))
                y_dn1 = jnp.where(row == 0, low1, pltpu.roll(own, 1, 0))
                y_dn2 = jnp.where(row == 0, low0, jnp.where(row == 1, low1, pltpu.roll(own, 2, 0)))
                spread = 16.0 * (y_up1 + y_dn1) - (y_up2 + y_dn2) + zz_ref[t, p * ny : (p + 1) * ny, :]
                b = SECTION * own + (SECTION * STEP) * chem_ref[s, p] + scale * spread
                if p == 0:
                    b_first = b
                elif p < nx - 1:
                    full = b if carry is None else b + carry
                    part_ref[s, p] = full * coef_ref[2, p]
                    b_first = b_first + coef_ref[0, p] * full
                    carry = coef_ref[1, p] * full
                else:
                    b_last = b + carry
            msg_ref[s // GROUP, s % GROUP] = b_first
            msg_ref[s // GROUP, s % GROUP + 8] = b_last

    mine = lax.axis_index("gx") % GROUPS
    for turn in range(GROUPS):
        send_refs[turn][...] = msg_ref[(mine + turn) % GROUPS]


def local_part(diffusivity, adjoint, chem, near, low, high, conduct, coef, ends):
    carried, nx, ny, nz = adjoint.shape
    smem = pl.BlockSpec(memory_space=pltpu.SMEM)
    return pl.pallas_call(
        local_kernel,
        in_specs=[smem] + [WHOLE] * 8,
        out_specs=[WHOLE] * (1 + GROUPS),
        out_shape=[pltpu.VMEM(adjoint.shape, F32)] + [pltpu.VMEM((ROWS, ny, nz), F32)] * GROUPS,
        scratch_shapes=[
            pltpu.VMEM((GROUPS, ROWS, ny, nz), F32),
            pltpu.VMEM((2 * nz, nz), BF16),
            pltpu.VMEM((LB, nx * ny, nz), F32),
        ],
        compiler_params=SMALL,
        cost_estimate=pl.CostEstimate(flops=20 * 10**6, bytes_accessed=7 * 10**6, transcendentals=0),
        name="local",
    )(diffusivity, conduct, adjoint, chem, near, low, high, coef, ends)


def reduce_kernel(*refs):
    got_refs, send_refs = refs[:GROUPS], refs[GROUPS : 2 * GROUPS]
    part_ref, coef_ref, in_ref, msg_ref = refs[2 * GROUPS :]
    device = lax.axis_index("gx")
    mine, home = device % GROUPS, device // GROUPS % GROUPS
    ny = in_ref.shape[2]
    for turn in range(GROUPS):
        in_ref[(mine + GROUPS - turn) % GROUPS] = got_refs[turn][...]
    gap, mass_first = in_ref[0, 6], in_ref[0, 7]
    first = [in_ref[0, r] for r in range(GROUP)]
    mass = in_ref[0, 15]
    rhs = [in_ref[0, 8 + r] for r in range(GROUP)]
    for node in range(2 * GROUPS - 2):
        block, end = (node + 1) // 2, node % 2 == 1
        after = in_ref[block, 6] if end else in_ref[block, 14]
        inv = 1.0 / (gap + after + mass)
        alpha, beta = gap * inv, after * inv
        coef_ref[0, node], coef_ref[1, node] = alpha, beta
        base, block = (8, block) if end else (0, block + 1)
        for r in range(GROUP):
            part_ref[node, r] = rhs[r] * inv
            first[r] = first[r] + alpha * rhs[r]
            rhs[r] = in_ref[block, base + r] + beta * rhs[r]
        mass_first = mass_first + alpha * mass
        mass = in_ref[block, base + 7] + beta * mass
        gap = alpha * after
    for r, plane in enumerate(first + [gap, mass_first] + rhs + [in_ref[GROUPS - 1, 14], mass]):
        msg_ref[pl.ds(r, ny, stride=ROWS), :] = plane
    size = PAIR * ROWS
    for turn in range(GROUPS):
        send_refs[turn][...] = msg_ref[pl.ds(pl.multiple_of((home + turn) % GROUPS * size, size), size), :]


def reduce_blocks(got):
    plane = got[0].shape[1:]
    return pl.pallas_call(
        reduce_kernel,
        in_specs=[WHOLE] * GROUPS,
        out_specs=[WHOLE] * (GROUPS + 2),
        out_shape=[pltpu.VMEM((PAIR * ROWS, plane[1]), F32)] * GROUPS
        + [
            pltpu.VMEM((2 * GROUPS - 2, GROUP) + plane, F32),
            pltpu.VMEM((2, 2 * GROUPS - 2) + plane, F32),
        ],
        scratch_shapes=[
            pltpu.VMEM((GROUPS, ROWS) + plane, F32),
            pltpu.VMEM((plane[0] * ROWS, plane[1]), F32),
        ],
        compiler_params=SMALL,
        cost_estimate=pl.CostEstimate(flops=10**6, bytes_accessed=10**6, transcendentals=0),
        name="reduce",
    )(*got)


def merge_kernel(*refs):
    got_refs, (msg_ref, part_ref, coef_ref, in_ref) = refs[:GROUPS], refs[GROUPS:]
    home = lax.axis_index("gx") // GROUPS % GROUPS
    for turn in range(GROUPS):
        in_ref[(home + GROUPS - turn) % GROUPS] = got_refs[turn][...]
    shape = (8, in_ref.shape[2])
    sub = iota(shape, 0)
    for pair in range(PAIR):
        top = pair * ROWS

        def row(block, r):
            return jnp.broadcast_to(in_ref[block, top + r : top + r + 1, :], shape)

        gap, mass = row(0, 6), row(0, 15)
        first = in_ref[0, top : top + 8, :]
        rhs = in_ref[0, top + 8 : top + 16, :]
        for node in range(2 * GROUPS - 2):
            block, end = (node + 1) // 2, node % 2 == 1
            after = row(block, 6 if end else 14)
            inv = 1.0 / (gap + after + mass)
            alpha, beta = gap * inv, after * inv
            coef_ref[0, pair, node], coef_ref[1, pair, node] = alpha, beta
            part_ref[pair, node] = rhs * inv
            base, block = (8, block) if end else (0, block + 1)
            first = first + alpha * rhs
            rhs = in_ref[block, top + base : top + base + 8, :] + beta * rhs
            mass = row(block, base + 7) + beta * mass
            gap = alpha * after
        msg_ref[top : top + 8, :] = jnp.where(sub == 6, gap, first)
        msg_ref[top + 8 : top + 16, :] = jnp.where(sub == 6, row(GROUPS - 1, 14), rhs)


def merge(got):
    nz = got[0].shape[1]
    nodes = 2 * GROUPS - 2
    return pl.pallas_call(
        merge_kernel,
        in_specs=[WHOLE] * GROUPS,
        out_specs=[WHOLE] * 3,
        out_shape=[
            pltpu.VMEM((PAIR * ROWS, nz), F32),
            pltpu.VMEM((PAIR, nodes, 8, nz), F32),
            pltpu.VMEM((2, PAIR, nodes, 8, nz), F32),
        ],
        scratch_shapes=[pltpu.VMEM((GROUPS, PAIR * ROWS, nz), F32)],
        compiler_params=SMALL,
        cost_estimate=pl.CostEstimate(flops=10**6, bytes_accessed=10**6, transcendentals=0),
        name="merge",
    )(*got)


def chain_kernel(own_ref, other_ref, part_ref, coef_ref, *refs):
    send_refs, (in_ref, ends_ref, out_ref) = refs[:GROUPS], refs[GROUPS:]
    device = lax.axis_index("gx")
    home, side = device // GROUPS % GROUPS, device // (GROUPS * GROUPS)
    in_ref[side] = own_ref[...]
    in_ref[1 - side] = other_ref[...]
    shape = (8, in_ref.shape[2])
    for pair in range(PAIR):
        top = pair * ROWS

        def row(block, r):
            return jnp.broadcast_to(in_ref[block, top + r : top + r + 1, :], shape)

        def rows(block, r):
            return in_ref[block, top + r : top + r + 8, :]

        inv0 = 1.0 / (row(0, 6) + row(0, 14) + row(0, 15))
        a0, c0 = row(0, 6) * inv0, row(0, 14) * inv0
        inv1 = 1.0 / (row(1, 6) + row(1, 14) + row(1, 15))
        a1 = row(1, 6) * inv1
        link = a0 * row(0, 14)
        mass0, rhs0 = row(0, 7) + a0 * row(0, 15), rows(0, 0) + a0 * rows(0, 8)
        mass1 = row(1, 7) + a1 * row(1, 15) + c0 * row(0, 15) + a1 * row(1, 14)
        rhs1 = rows(1, 0) + a1 * rows(1, 8) + c0 * rows(0, 8)
        inv = 1.0 / (mass0 + link)
        q = link * inv
        first1 = (rhs1 + q * rhs0) / (mass1 + q * mass0)
        first0 = rhs0 * inv + q * first1
        ends_ref[0, pair, 0], ends_ref[0, pair, 1] = first0, rows(0, 8) * inv0 + a0 * first0 + c0 * first1
        ends_ref[1, pair, 0], ends_ref[1, pair, 1] = first1, rows(1, 8) * inv1 + a1 * first1
        start, value = ends_ref[side, pair, 0], ends_ref[side, pair, 1]
        out_ref[0, top : top + 8, :] = start
        out_ref[GROUPS - 1, top + 8 : top + 16, :] = value
        for node in range(2 * GROUPS - 3, -1, -1):
            value = part_ref[pair, node] + coef_ref[0, pair, node] * start + coef_ref[1, pair, node] * value
            block, end = (node + 1) // 2, node % 2 == 1
            base = top if end else top + 8
            out_ref[block, base : base + 8, :] = value
    for turn in range(GROUPS):
        send_refs[turn][...] = out_ref[(home + turn) % GROUPS]


def chain(own, other, part, coef):
    nz = own.shape[1]
    return pl.pallas_call(
        chain_kernel,
        in_specs=[WHOLE] * 4,
        out_specs=[WHOLE] * GROUPS,
        out_shape=[pltpu.VMEM(own.shape, F32)] * GROUPS,
        scratch_shapes=[
            pltpu.VMEM((2, PAIR * ROWS, nz), F32),
            pltpu.VMEM((2, PAIR, 2, 8, nz), F32),
            pltpu.VMEM((GROUPS, PAIR * ROWS, nz), F32),
        ],
        compiler_params=SMALL,
        cost_estimate=pl.CostEstimate(flops=10**6, bytes_accessed=10**6, transcendentals=0),
        name="chain",
    )(own, other, part, coef)


def expand_kernel(*refs):
    got_refs, (part_ref, coef_ref) = refs[:GROUPS], refs[GROUPS : GROUPS + 2]
    send_refs, (ends_ref, out_ref) = refs[GROUPS + 2 : 2 * GROUPS + 2], refs[2 * GROUPS + 2 :]
    device = lax.axis_index("gx")
    mine, home = device % GROUPS, device // GROUPS % GROUPS
    ny = out_ref.shape[2]
    size = PAIR * ROWS
    for turn in range(GROUPS):
        at = pl.multiple_of((home + GROUPS - turn) % GROUPS * size, size)
        ends_ref[pl.ds(at, size), :] = got_refs[turn][...]
    for r in range(GROUP):
        start = ends_ref[pl.ds(r, ny, stride=ROWS), :]
        value = ends_ref[pl.ds(r + 8, ny, stride=ROWS), :]
        out_ref[0, r] = start
        out_ref[GROUPS - 1, GROUP + r] = value
        for node in range(2 * GROUPS - 3, -1, -1):
            value = part_ref[node, r] + coef_ref[0, node] * start + coef_ref[1, node] * value
            block, end = (node + 1) // 2, node % 2 == 1
            out_ref[block, r if end else GROUP + r] = value
    for turn in range(GROUPS):
        send_refs[turn][...] = out_ref[(mine + turn) % GROUPS]


def expand(got, part, coef):
    plane = part.shape[2:]
    return pl.pallas_call(
        expand_kernel,
        in_specs=[WHOLE] * (GROUPS + 2),
        out_specs=[WHOLE] * GROUPS,
        out_shape=[pltpu.VMEM((2 * GROUP,) + plane, F32)] * GROUPS,
        scratch_shapes=[
            pltpu.VMEM((plane[0] * ROWS, plane[1]), F32),
            pltpu.VMEM((GROUPS, 2 * GROUP) + plane, F32),
        ],
        compiler_params=SMALL,
        cost_estimate=pl.CostEstimate(flops=10**6, bytes_accessed=10**6, transcendentals=0),
        name="expand",
    )(*got, part, coef)


def back_kernel(coef_ref, part_ref, *refs):
    got_refs, (out_hbm, ends_ref, out_ref, out_sem) = refs[:GROUPS], refs[GROUPS:]
    carried, nx, ny, _ = part_ref.shape
    groups = carried // SB
    mine = lax.axis_index("gx") % GROUPS
    for turn in range(GROUPS):
        ends_ref[(mine + GROUPS - turn) % GROUPS] = got_refs[turn][...]

    def put(g):
        return pltpu.make_async_copy(out_ref.at[pl.ds(g * SB, SB)], out_hbm.at[pl.ds(g * SB, SB)], out_sem.at[g])

    @pl.loop(0, groups)
    def _(g):
        for t in range(SB):
            s = g * SB + t
            first = ends_ref[s // GROUP, s % GROUP]
            value = ends_ref[s // GROUP, s % GROUP + GROUP]
            out_ref[s, 0] = first
            out_ref[s, nx - 1] = value
            for p in range(nx - 2, 0, -1):
                value = part_ref[s, p] + coef_ref[0, p] * first + coef_ref[1, p] * value
                out_ref[s, p] = value
        put(g).start()

    @pl.loop(0, groups)
    def _(g):
        put(g).wait()


def back(part, coef, got):
    groups = part.shape[0] // SB
    return pl.pallas_call(
        back_kernel,
        in_specs=[WHOLE] * (2 + GROUPS),
        out_specs=ANY,
        out_shape=jax.ShapeDtypeStruct(part.shape, F32),
        scratch_shapes=[
            pltpu.VMEM((GROUPS, 2 * GROUP) + part.shape[2:], F32),
            pltpu.VMEM(part.shape, F32),
            pltpu.SemaphoreType.DMA((groups,)),
        ],
        compiler_params=SMALL,
        cost_estimate=pl.CostEstimate(flops=2 * 10**6, bytes_accessed=3 * 10**6, transcendentals=0),
        name="back",
    )(coef, part, *got)


def shards(
    adjoint, log_conc, levels, conduct, orders_fwd, orders_rev, stoich, rate_fwd, rate_rev, diffusivity
):
    rows_y, blocks = lax.axis_size("gy"), lax.axis_size("gx")
    near = lax.ppermute(adjoint, "gz", [(0, 1), (1, 0)])
    tail, head = edges(adjoint)
    low = lax.ppermute(tail, "gy", [(i, (i + 1) % rows_y) for i in range(rows_y)])
    high = lax.ppermute(head, "gy", [((i + 1) % rows_y, i) for i in range(rows_y)])
    chem, coef, ends_m = chemistry(
        adjoint, log_conc, levels, conduct, orders_fwd, orders_rev, stoich, rate_fwd, rate_rev
    )
    part, *send = local_part(diffusivity, adjoint, chem, near, low, high, conduct, coef, ends_m)

    def turned(values, inner):
        span = inner * GROUPS

        def shift(i, turn):
            return i // span * span + (i % span + turn * inner) % span

        return [
            value if turn == 0 else lax.ppermute(value, "gx", [(i, shift(i, turn)) for i in range(blocks)])
            for turn, value in enumerate(values)
        ]

    *send, close_part, close_coef = reduce_blocks(turned(send, 1))
    message, far_part, far_coef = merge(turned(send, GROUPS))
    other = lax.ppermute(message, "gx", [(i, (i + blocks // 2) % blocks) for i in range(blocks)])
    send = expand(turned(chain(message, other, far_part, far_coef), GROUPS), close_part, close_coef)
    return back(part, coef, turned(send, 1))


def solution(mesh):
    cells = P(None, "gx", "gy", "gz")
    planes = P("gx", "gy", "gz")
    in_specs = (cells, cells, planes, planes, P(), P(), P(), P(), P(), P())
    return jax.shard_map(shards, mesh=mesh, in_specs=in_specs, out_specs=cells, check_vma=False)
```

```python
import math

import jax
import jax.numpy as jnp
from jax import lax
from jax.experimental import pallas as pl
from jax.experimental.pallas import tpu as pltpu
from jax.sharding import PartitionSpec as P

SECTION = 0.02
STEP = 0.3
MASS = 0.001
THIRD = MASS / 3.0
BODY = MASS + 2.0 * THIRD
LOG2E = math.log2(math.e)
OFF = -1024.0

K_ROWS = 96
R_PAD = 208
STRIP = 16
CHUNKS = tuple((start, STRIP) for start in range(0, R_PAD, STRIP))
TILE = 2048
XB = 4
LIMIT = 24 * 1024 * 1024
F32 = jnp.float32
BF16 = jnp.bfloat16


def iota(shape, dim):
    return lax.broadcasted_iota(jnp.int32, shape, dim)


def dot(a, b):
    return lax.dot_general(a, b, (((1,), (0,)), ((), ())), preferred_element_type=F32)


def dot_nt(a, b):
    return lax.dot_general(a, b, (((1,), (1,)), ((), ())), preferred_element_type=F32)


def one_hot(mask):
    return jnp.where(mask, 1.0, 0.0).astype(BF16)


def build_weights(of_ref, or_ref, st_ref, rf_ref, rr_ref, wide_ref, w_ref, c_ref):
    species, react = of_ref.shape
    carried = st_ref.shape[0]
    eye = one_hot(iota((R_PAD, 256), 0) == iota((R_PAD, 256), 1))
    pick_row, pick_col = iota((32, 32), 0), iota((32, 32), 1)
    pick = one_hot(pick_col == jnp.where(pick_row < 16, pick_row, jnp.where(pick_row < 24, pick_row - 2, -1)))
    sub, tier = iota((8, 256), 0), 4 * iota((8, 256), 1) // react
    full = []
    for index, (orders, rate) in enumerate(((of_ref, rf_ref), (or_ref, rr_ref))):
        wide_ref[...] = jnp.zeros(wide_ref.shape, F32)
        wide_ref[0:species, 0:react] = orders[...].astype(F32)
        plain = wide_ref[0:32, :]
        sign = 1.0 if index == 0 else -1.0
        c_ref[index] = (sign * dot(pick, plain.astype(BF16)))[:, 0:R_PAD].astype(BF16)
        scaled = plain * LOG2E
        hi = scaled.astype(BF16).astype(F32)
        wide_ref[0:32, :] = hi
        wide_ref[32:64, :] = scaled - hi
        wide_ref[88:89, 0:react] = jnp.log(rate[...]) * LOG2E
        r = jnp.broadcast_to(wide_ref[88:89, :], (8, 256))
        r0 = r.astype(BF16).astype(F32)
        r1 = (r - r0).astype(BF16).astype(F32)
        parts = jnp.where(sub == 3, r0, jnp.where(sub == 4, r1, jnp.where(sub == 5, r - r0 - r1, 0.0)))
        wide_ref[88:96, :] = jnp.where(sub < 3, jnp.where(tier > sub, OFF, 0.0), parts)
        full.append(dot_nt(eye, wide_ref[...].astype(BF16)).astype(BF16))
    wide_ref[...] = jnp.zeros(wide_ref.shape, F32)
    wide_ref[64:80, 0:react] = st_ref[0:16, :].astype(F32)
    wide_ref[82 : 66 + carried, 0:react] = st_ref[16:carried, :].astype(F32)
    full.append(dot_nt(eye, wide_ref[...].astype(BF16)).astype(BF16))
    base = 0
    for start, size in CHUNKS:
        for part in full:
            w_ref[base : base + size, :] = part[start : start + size]
            base += size


def chem_kernel(
    adj_ref, conc_ref, lev_ref, cond_ref, of_ref, or_ref, st_ref, rf_ref, rr_ref,
    out_ref, coef_ref, tail_ref,
    wide_ref, w_ref, c_ref, conc32_ref, x_ref, act_ref, run_ref,
):
    step = pl.program_id(0)

    @pl.when(step == 0)
    def _():
        run_ref[0] = cond_ref[0] - THIRD
        run_ref[1] = jnp.where(lax.axis_index("gx") == 0, MASS + THIRD, BODY) * jnp.ones(run_ref.shape[1:], F32)
        run_ref[2] = jnp.full(run_ref.shape[1:], BODY, F32)
        build_weights(of_ref, or_ref, st_ref, rf_ref, rr_ref, wide_ref, w_ref, c_ref)

    gap, mass_first, mass = run_ref[0], run_ref[1], run_ref[2]
    for q in range(1, XB + 1):
        p = step * XB + q
        after = cond_ref[jnp.minimum(p, cond_ref.shape[0] - 1)] - THIRD
        inv = 1.0 / (gap + after + mass)
        alpha, beta = gap * inv, after * inv
        coef_ref[0, p], coef_ref[1, p], coef_ref[2, p] = alpha, beta, inv
        mass_first = mass_first + alpha * mass
        mass = BODY + beta * mass
        gap = alpha * after
        tail_ref[p, 0], tail_ref[p, 1], tail_ref[p, 2] = gap, mass_first, mass
    run_ref[0], run_ref[1], run_ref[2] = gap, mass_first, mass

    carried, xb, ny, nz = adj_ref.shape
    species = conc_ref.shape[0]
    adj_rows = adj_ref.reshape(carried * xb * ny, nz)
    out_rows = out_ref.reshape(carried * xb * ny, nz)
    pitch = xb * ny
    conc32_ref[...] = conc_ref[...].astype(F32).reshape(species * pitch, nz)
    sub = iota((8, nz), 0)
    for x in range(xb):
        for y in range(ny):
            row = x * ny + y
            cols = slice(row * nz, (row + 1) * nz)
            conc = jnp.concatenate(
                [conc32_ref[pl.ds(row + 8 * q * pitch, 8, stride=pitch), :] for q in range(4)], axis=0
            ).astype(BF16)
            x_ref[0:32, cols] = conc
            x_ref[32:64, cols] = conc
            lam = [adj_rows[pl.ds(row + first * pitch, 8, stride=pitch), :] for first in (0, 8, carried - 8)]
            level = jnp.broadcast_to(lev_ref[x, y : y + 1, :], (8, nz))
            marks = jnp.where(level <= sub, 1.0, 0.0)
            x_ref[64:96, cols] = jnp.concatenate(lam + [marks], axis=0).astype(BF16)
    per_tile = TILE // nz
    for tile in range(xb * ny // per_tile):
        slot = tile % act_ref.shape[0]
        every = dot(w_ref[...], x_ref[:, tile * TILE : (tile + 1) * TILE])
        for start, size in CHUNKS:
            got = every[3 * start : 3 * (start + size)]
            weight = got[2 * size :]
            act_ref[slot, 0, start : start + size, :] = (jnp.exp2(got[:size]) * weight).astype(BF16)
            act_ref[slot, 1, start : start + size, :] = (jnp.exp2(got[size : 2 * size]) * weight).astype(BF16)
        chem = dot(c_ref[0], act_ref[slot, 0]) + dot(c_ref[1], act_ref[slot, 1])
        for part in range(per_tile):
            row = tile * per_tile + part
            for q, first in enumerate((0, 8, carried - 8)):
                out_rows[pl.ds(row + first * pitch, 8, stride=pitch), :] = chem[
                    8 * q : 8 * q + 8, part * nz : (part + 1) * nz
                ]


def chemistry(adjoint, log_conc, levels, conduct, orders_fwd, orders_rev, stoich, rate_fwd, rate_rev):
    carried, nx, ny, nz = adjoint.shape
    species, react = log_conc.shape[0], orders_fwd.shape[0]
    whole = lambda a: pl.BlockSpec(a.shape, lambda i: (0,) * len(a.shape))
    small = [orders_fwd.T, orders_rev.T, stoich.T, rate_fwd.reshape(1, react), rate_rev.reshape(1, react)]
    return pl.pallas_call(
        chem_kernel,
        grid=(nx // XB,),
        in_specs=[
            pl.BlockSpec((carried, XB, ny, nz), lambda i: (0, i, 0, 0)),
            pl.BlockSpec((species, XB, ny, nz), lambda i: (0, i, 0, 0)),
            pl.BlockSpec((XB, ny, nz), lambda i: (i, 0, 0)),
            whole(conduct),
        ]
        + [whole(a) for a in small],
        out_specs=[
            pl.BlockSpec((carried, XB, ny, nz), lambda i: (0, i, 0, 0)),
            pl.BlockSpec((3, nx + 1, ny, nz), lambda i: (0, 0, 0, 0)),
            pl.BlockSpec((nx + 1, 3, ny, nz), lambda i: (0, 0, 0, 0)),
        ],
        out_shape=[
            jax.ShapeDtypeStruct(adjoint.shape, F32),
            jax.ShapeDtypeStruct((3, nx + 1, ny, nz), F32),
            jax.ShapeDtypeStruct((nx + 1, 3, ny, nz), F32),
        ],
        scratch_shapes=[
            pltpu.VMEM((K_ROWS, 256), F32),
            pltpu.VMEM((3 * R_PAD, K_ROWS), BF16),
            pltpu.VMEM((2, 32, R_PAD), BF16),
            pltpu.VMEM((species * XB * ny, nz), F32),
            pltpu.VMEM((K_ROWS, XB * ny * nz), BF16),
            pltpu.VMEM((2, 2, R_PAD, TILE), BF16),
            pltpu.VMEM((3, ny, nz), F32),
        ],
        compiler_params=pltpu.CompilerParams(dimension_semantics=("arbitrary",), vmem_limit_bytes=LIMIT),
        cost_estimate=pl.CostEstimate(flops=12 * 10**9, bytes_accessed=4 * 10**6, transcendentals=6_750_000),
        name="chem",
    )(adjoint, log_conc, levels, conduct, *small)


GROUP = 6
GROUPS = 4
ROWS = 16
SB = 2
LB = 11
ANY = pl.BlockSpec(memory_space=pl.ANY)
WHOLE = pl.BlockSpec(memory_space=pltpu.VMEM)
SMALL = pltpu.CompilerParams(vmem_limit_bytes=LIMIT)


def edges_kernel(adj_ref, low_ref, high_ref):
    carried, nx, ny, nz = adj_ref.shape
    mine = lax.axis_index("gy")
    to_high = jnp.where(mine == lax.axis_size("gy") - 1, 0.0, 1.0)
    to_low = jnp.where(mine == 0, 0.0, 1.0)

    @pl.loop(0, carried)
    def _(s):
        for x in range(nx):
            low_ref[s, x] = adj_ref[s, x, ny - 2 : ny, :] * to_high
            high_ref[s, x] = adj_ref[s, x, 0:2, :] * to_low


def edges(adjoint):
    carried, nx, ny, nz = adjoint.shape
    shape = pltpu.VMEM((carried, nx, 2, nz), F32)
    return pl.pallas_call(
        edges_kernel,
        in_specs=[WHOLE],
        out_specs=[WHOLE, WHOLE],
        out_shape=[shape, shape],
        compiler_params=SMALL,
        cost_estimate=pl.CostEstimate(flops=0, bytes_accessed=2 * 10**6, transcendentals=0),
        name="edges",
    )(adjoint)


def split(value):
    high = value.astype(BF16)
    return high, (value - high.astype(F32)).astype(BF16)


def local_kernel(
    diff_ref, cond_ref, adj_ref, chem_ref, near_ref, low_ref, high_ref, coef_ref, tail_ref,
    part_ref, *rest,
):
    send_refs, (msg_ref, band_ref, zz_ref) = rest[:GROUPS], rest[GROUPS:]
    nx, ny, nz = cond_ref.shape
    carried = adj_ref.shape[0]
    at = nx - 2
    face = cond_ref[nx - 1] - THIRD
    for group in range(GROUPS):
        for r, value in ((6, tail_ref[at, 0]), (7, tail_ref[at, 1]), (14, face), (15, tail_ref[at, 2])):
            msg_ref[group, r] = value
    for r in range(carried - GROUP * (GROUPS - 1), GROUP):
        msg_ref[GROUPS - 1, r] = jnp.zeros((ny, nz), F32)
        msg_ref[GROUPS - 1, r + 8] = jnp.zeros((ny, nz), F32)

    k, z = iota((2 * nz, nz), 0), iota((2 * nz, nz), 1)
    offset = jnp.where(lax.axis_index("gz") == 0, nz, -nz)
    gap = jnp.abs(jnp.where(k < nz, k, k - nz + offset) - z)
    band_ref[...] = jnp.where(
        gap == 0, -60.0, jnp.where(gap == 1, 16.0, jnp.where(gap == 2, -1.0, 0.0))
    ).astype(BF16)
    row = iota((ny, nz), 0)

    @pl.loop(0, carried // LB)
    def _(g):
        for t in range(LB):
            s = g * LB + t
            own_hi, own_lo = split(adj_ref[s].reshape(nx * ny, nz))
            near_hi, near_lo = split(near_ref[s].reshape(nx * ny, nz))
            sides = jnp.concatenate(
                [jnp.concatenate([own_hi, near_hi], axis=1), jnp.concatenate([own_lo, near_lo], axis=1)], axis=0
            )
            spread_z = dot(sides, band_ref[...])
            zz_ref[t] = spread_z[: nx * ny] + spread_z[nx * ny :]
        for t in range(LB):
            s = g * LB + t
            scale = diff_ref[s] * (SECTION * STEP / 12.0)
            b_first, carry = None, None
            for p in range(nx):
                own = adj_ref[s, p]
                low0, low1 = low_ref[s, p, 0:1, :], low_ref[s, p, 1:2, :]
                high0, high1 = high_ref[s, p, 0:1, :], high_ref[s, p, 1:2, :]
                y_up1 = jnp.where(row == ny - 1, high0, pltpu.roll(own, ny - 1, 0))
                y_up2 = jnp.where(row == ny - 1, high1, jnp.where(row == ny - 2, high0, pltpu.roll(own, ny - 2, 0)))
                y_dn1 = jnp.where(row == 0, low1, pltpu.roll(own, 1, 0))
                y_dn2 = jnp.where(row == 0, low0, jnp.where(row == 1, low1, pltpu.roll(own, 2, 0)))
                spread = 16.0 * (y_up1 + y_dn1) - (y_up2 + y_dn2) + zz_ref[t, p * ny : (p + 1) * ny, :]
                b = SECTION * own + (SECTION * STEP) * chem_ref[s, p] + scale * spread
                if p == 0:
                    b_first = b
                elif p < nx - 1:
                    full = b if carry is None else b + carry
                    part_ref[s, p] = full * coef_ref[2, p]
                    b_first = b_first + coef_ref[0, p] * full
                    carry = coef_ref[1, p] * full
                else:
                    b_last = b + carry
            msg_ref[s // GROUP, s % GROUP] = b_first
            msg_ref[s // GROUP, s % GROUP + 8] = b_last

    mine = lax.axis_index("gx") % GROUPS
    for turn in range(GROUPS):
        send_refs[turn][...] = msg_ref[(mine + turn) % GROUPS]


def local_part(diffusivity, adjoint, chem, near, low, high, conduct, coef, ends):
    carried, nx, ny, nz = adjoint.shape
    smem = pl.BlockSpec(memory_space=pltpu.SMEM)
    return pl.pallas_call(
        local_kernel,
        in_specs=[smem] + [WHOLE] * 8,
        out_specs=[WHOLE] * (1 + GROUPS),
        out_shape=[pltpu.VMEM(adjoint.shape, F32)] + [pltpu.VMEM((ROWS, ny, nz), F32)] * GROUPS,
        scratch_shapes=[
            pltpu.VMEM((GROUPS, ROWS, ny, nz), F32),
            pltpu.VMEM((2 * nz, nz), BF16),
            pltpu.VMEM((LB, nx * ny, nz), F32),
        ],
        compiler_params=SMALL,
        cost_estimate=pl.CostEstimate(flops=20 * 10**6, bytes_accessed=7 * 10**6, transcendentals=0),
        name="local",
    )(diffusivity, conduct, adjoint, chem, near, low, high, coef, ends)


def reduce_kernel(*refs):
    got_refs, (msg_ref, part_ref, coef_ref, in_ref) = refs[:GROUPS], refs[GROUPS:]
    mine = lax.axis_index("gx") % GROUPS
    for turn in range(GROUPS):
        in_ref[(mine + GROUPS - turn) % GROUPS] = got_refs[turn][...]
    gap, mass_first = in_ref[0, 6], in_ref[0, 7]
    first = [in_ref[0, r] for r in range(GROUP)]
    mass = in_ref[0, 15]
    rhs = [in_ref[0, 8 + r] for r in range(GROUP)]
    for node in range(2 * GROUPS - 2):
        block, end = (node + 1) // 2, node % 2 == 1
        after = in_ref[block, 6] if end else in_ref[block, 14]
        inv = 1.0 / (gap + after + mass)
        alpha, beta = gap * inv, after * inv
        coef_ref[0, node], coef_ref[1, node] = alpha, beta
        base, block = (8, block) if end else (0, block + 1)
        for r in range(GROUP):
            part_ref[node, r] = rhs[r] * inv
            first[r] = first[r] + alpha * rhs[r]
            rhs[r] = in_ref[block, base + r] + beta * rhs[r]
        mass_first = mass_first + alpha * mass
        mass = in_ref[block, base + 7] + beta * mass
        gap = alpha * after
    for r, plane in enumerate(first + [gap, mass_first] + rhs + [in_ref[GROUPS - 1, 14], mass]):
        msg_ref[r] = plane


def reduce_blocks(got):
    plane = got[0].shape[1:]
    return pl.pallas_call(
        reduce_kernel,
        in_specs=[WHOLE] * GROUPS,
        out_specs=[WHOLE] * 3,
        out_shape=[
            pltpu.VMEM((ROWS,) + plane, F32),
            pltpu.VMEM((2 * GROUPS - 2, GROUP) + plane, F32),
            pltpu.VMEM((2, 2 * GROUPS - 2) + plane, F32),
        ],
        scratch_shapes=[pltpu.VMEM((GROUPS, ROWS) + plane, F32)],
        compiler_params=SMALL,
        cost_estimate=pl.CostEstimate(flops=10**6, bytes_accessed=10**6, transcendentals=0),
        name="reduce",
    )(*got)


def chain_kernel(*refs):
    in_ref, part_ref, coef_ref = refs[:3]
    send_refs, (ends_ref, out_ref) = refs[3 : 3 + GROUPS], refs[3 + GROUPS :]
    count = in_ref.shape[0]
    device = lax.axis_index("gx")
    mine, home = device % GROUPS, device // GROUPS
    h, mass, rhs, ends = [], [], [], []
    passed_m = passed_b = None
    for i in range(count):
        g, m_f, face, m_l = in_ref[i, 6], in_ref[i, 7], in_ref[i, 14], in_ref[i, 15]
        inv = 1.0 / (g + face + m_l)
        a, c = g * inv, face * inv
        m = m_f + a * m_l
        b = [in_ref[i, r] + a * in_ref[i, 8 + r] for r in range(GROUP)]
        if i > 0:
            m, b = m + passed_m, [p + q for p, q in zip(b, passed_b)]
        passed_m, passed_b = c * m_l, [c * in_ref[i, 8 + r] for r in range(GROUP)]
        h.append(a * face)
        mass.append(m)
        rhs.append(b)
        ends.append((a, c, inv))
    half = count // 2
    scale, ratio = [None] * count, [None] * count

    def pass_on(i, k, link):
        inv = 1.0 / (mass[i] + link)
        q = link * inv
        scale[i], ratio[i] = [v * inv for v in rhs[i]], q
        mass[k] = mass[k] + q * mass[i]
        rhs[k] = [v + q * w for v, w in zip(rhs[k], rhs[i])]

    for i in range(half):
        pass_on(i, i + 1, h[i])
    mass[count - 1] = mass[count - 1] + h[count - 1]
    for i in range(count - 1, half, -1):
        pass_on(i, i - 1, h[i - 1])
    first = [None] * count
    inv = 1.0 / mass[half]
    first[half] = [v * inv for v in rhs[half]]
    for i in list(range(half - 1, -1, -1)) + list(range(half + 1, count)):
        k = i + 1 if i < half else i - 1
        first[i] = [v + ratio[i] * w for v, w in zip(scale[i], first[k])]
    for i in range(count):
        a, c, inv = ends[i]
        for r in range(GROUP):
            last = in_ref[i, 8 + r] * inv + a * first[i][r]
            if i < count - 1:
                last = last + c * first[i + 1][r]
            ends_ref[i, r] = first[i][r]
            ends_ref[i, GROUP + r] = last
    for r in range(GROUP):
        start = ends_ref[home, r]
        value = ends_ref[home, GROUP + r]
        out_ref[0, r] = start
        out_ref[GROUPS - 1, GROUP + r] = value
        for node in range(2 * GROUPS - 3, -1, -1):
            value = part_ref[node, r] + coef_ref[0, node] * start + coef_ref[1, node] * value
            block, end = (node + 1) // 2, node % 2 == 1
            out_ref[block, r if end else GROUP + r] = value
    for turn in range(GROUPS):
        send_refs[turn][...] = out_ref[(mine + turn) % GROUPS]


def chain(got, part, coef):
    plane = part.shape[2:]
    count = got.shape[0]
    return pl.pallas_call(
        chain_kernel,
        in_specs=[WHOLE] * 3,
        out_specs=[WHOLE] * GROUPS,
        out_shape=[pltpu.VMEM((2 * GROUP,) + plane, F32)] * GROUPS,
        scratch_shapes=[
            pltpu.VMEM((count, 2 * GROUP) + plane, F32),
            pltpu.VMEM((GROUPS, 2 * GROUP) + plane, F32),
        ],
        compiler_params=SMALL,
        cost_estimate=pl.CostEstimate(flops=10**6, bytes_accessed=10**6, transcendentals=0),
        name="chain",
    )(got, part, coef)


def back_kernel(coef_ref, part_ref, *refs):
    got_refs, (out_hbm, ends_ref, out_ref, out_sem) = refs[:GROUPS], refs[GROUPS:]
    carried, nx, ny, _ = part_ref.shape
    groups = carried // SB
    mine = lax.axis_index("gx") % GROUPS
    for turn in range(GROUPS):
        ends_ref[(mine + GROUPS - turn) % GROUPS] = got_refs[turn][...]

    def put(g):
        return pltpu.make_async_copy(out_ref.at[pl.ds(g * SB, SB)], out_hbm.at[pl.ds(g * SB, SB)], out_sem.at[g])

    @pl.loop(0, groups)
    def _(g):
        for t in range(SB):
            s = g * SB + t
            first = ends_ref[s // GROUP, s % GROUP]
            value = ends_ref[s // GROUP, s % GROUP + GROUP]
            out_ref[s, 0] = first
            out_ref[s, nx - 1] = value
            for p in range(nx - 2, 0, -1):
                value = part_ref[s, p] + coef_ref[0, p] * first + coef_ref[1, p] * value
                out_ref[s, p] = value
        put(g).start()

    @pl.loop(0, groups)
    def _(g):
        put(g).wait()


def back(part, coef, got):
    groups = part.shape[0] // SB
    return pl.pallas_call(
        back_kernel,
        in_specs=[WHOLE] * (2 + GROUPS),
        out_specs=ANY,
        out_shape=jax.ShapeDtypeStruct(part.shape, F32),
        scratch_shapes=[
            pltpu.VMEM((GROUPS, 2 * GROUP) + part.shape[2:], F32),
            pltpu.VMEM(part.shape, F32),
            pltpu.SemaphoreType.DMA((groups,)),
        ],
        compiler_params=SMALL,
        cost_estimate=pl.CostEstimate(flops=2 * 10**6, bytes_accessed=3 * 10**6, transcendentals=0),
        name="back",
    )(coef, part, *got)


def shards(
    adjoint, log_conc, levels, conduct, orders_fwd, orders_rev, stoich, rate_fwd, rate_rev, diffusivity
):
    rows_y, blocks = lax.axis_size("gy"), lax.axis_size("gx")
    supers = blocks // GROUPS
    near = lax.ppermute(adjoint, "gz", [(0, 1), (1, 0)])
    tail, head = edges(adjoint)
    low = lax.ppermute(tail, "gy", [(i, (i + 1) % rows_y) for i in range(rows_y)])
    high = lax.ppermute(head, "gy", [((i + 1) % rows_y, i) for i in range(rows_y)])
    chem, coef, ends_m = chemistry(
        adjoint, log_conc, levels, conduct, orders_fwd, orders_rev, stoich, rate_fwd, rate_rev
    )
    part, *send = local_part(diffusivity, adjoint, chem, near, low, high, conduct, coef, ends_m)

    def close(value, turn):
        if turn == 0:
            return value
        pairs = [(i, i // GROUPS * GROUPS + (i + turn) % GROUPS) for i in range(blocks)]
        return lax.ppermute(value, "gx", pairs)

    message, inner, links = reduce_blocks([close(value, turn) for turn, value in enumerate(send)])
    columns = [[GROUPS * z + y for z in range(supers)] for y in range(GROUPS)]
    supers_all = lax.all_gather(message, "gx", axis_index_groups=columns)
    send = chain(supers_all, inner, links)
    return back(part, coef, [close(value, turn) for turn, value in enumerate(send)])


def solution(mesh):
    cells = P(None, "gx", "gy", "gz")
    planes = P("gx", "gy", "gz")
    in_specs = (cells, cells, planes, planes, P(), P(), P(), P(), P(), P())
    return jax.shard_map(shards, mesh=mesh, in_specs=in_specs, out_specs=cells, check_vma=False)
```

```python
import math

import jax
import jax.numpy as jnp
from jax import lax
from jax.experimental import pallas as pl
from jax.experimental.pallas import tpu as pltpu
from jax.sharding import PartitionSpec as P

SECTION = 0.02
STEP = 0.3
MASS = 0.001
THIRD = MASS / 3.0
BODY = MASS + 2.0 * THIRD
LOG2E = math.log2(math.e)
OFF = -1024.0

K_ROWS = 96
R_PAD = 208
STRIP = 16
CHUNKS = tuple((start, STRIP) for start in range(0, R_PAD, STRIP))
TILE = 4096
XB = 4
LIMIT = 24 * 1024 * 1024
F32 = jnp.float32
BF16 = jnp.bfloat16


def iota(shape, dim):
    return lax.broadcasted_iota(jnp.int32, shape, dim)


def dot(a, b):
    return lax.dot_general(a, b, (((1,), (0,)), ((), ())), preferred_element_type=F32)


def dot_nt(a, b):
    return lax.dot_general(a, b, (((1,), (1,)), ((), ())), preferred_element_type=F32)


def one_hot(mask):
    return jnp.where(mask, 1.0, 0.0).astype(BF16)


def build_weights(of_ref, or_ref, st_ref, rf_ref, rr_ref, wide_ref, w_ref, c_ref):
    species, react = of_ref.shape
    carried = st_ref.shape[0]
    eye = one_hot(iota((R_PAD, 256), 0) == iota((R_PAD, 256), 1))
    pick_row, pick_col = iota((32, 32), 0), iota((32, 32), 1)
    pick = one_hot(pick_col == jnp.where(pick_row < 16, pick_row, jnp.where(pick_row < 24, pick_row - 2, -1)))
    sub, tier = iota((8, 256), 0), 4 * iota((8, 256), 1) // react
    full = []
    for index, (orders, rate) in enumerate(((of_ref, rf_ref), (or_ref, rr_ref))):
        wide_ref[...] = jnp.zeros(wide_ref.shape, F32)
        wide_ref[0:species, 0:react] = orders[...].astype(F32)
        plain = wide_ref[0:32, :]
        sign = 1.0 if index == 0 else -1.0
        c_ref[index] = (sign * dot(pick, plain.astype(BF16)))[:, 0:R_PAD].astype(BF16)
        scaled = plain * LOG2E
        hi = scaled.astype(BF16).astype(F32)
        wide_ref[0:32, :] = hi
        wide_ref[32:64, :] = scaled - hi
        wide_ref[88:89, 0:react] = jnp.log(rate[...]) * LOG2E
        r = jnp.broadcast_to(wide_ref[88:89, :], (8, 256))
        r0 = r.astype(BF16).astype(F32)
        r1 = (r - r0).astype(BF16).astype(F32)
        parts = jnp.where(sub == 3, r0, jnp.where(sub == 4, r1, jnp.where(sub == 5, r - r0 - r1, 0.0)))
        wide_ref[88:96, :] = jnp.where(sub < 3, jnp.where(tier > sub, OFF, 0.0), parts)
        full.append(dot_nt(eye, wide_ref[...].astype(BF16)).astype(BF16))
    wide_ref[...] = jnp.zeros(wide_ref.shape, F32)
    wide_ref[64:80, 0:react] = st_ref[0:16, :].astype(F32)
    wide_ref[82 : 66 + carried, 0:react] = st_ref[16:carried, :].astype(F32)
    full.append(dot_nt(eye, wide_ref[...].astype(BF16)).astype(BF16))
    base = 0
    for start, size in CHUNKS:
        for part in full:
            w_ref[base : base + size, :] = part[start : start + size]
            base += size


def chem_kernel(
    adj_ref, conc_ref, lev_ref, cond_ref, of_ref, or_ref, st_ref, rf_ref, rr_ref,
    out_ref, coef_ref, tail_ref,
    wide_ref, w_ref, c_ref, conc32_ref, x_ref, act_ref, run_ref,
):
    step = pl.program_id(0)

    @pl.when(step == 0)
    def _():
        run_ref[0] = cond_ref[0] - THIRD
        run_ref[1] = jnp.where(lax.axis_index("gx") == 0, MASS + THIRD, BODY) * jnp.ones(run_ref.shape[1:], F32)
        run_ref[2] = jnp.full(run_ref.shape[1:], BODY, F32)
        build_weights(of_ref, or_ref, st_ref, rf_ref, rr_ref, wide_ref, w_ref, c_ref)

    gap, mass_first, mass = run_ref[0], run_ref[1], run_ref[2]
    for q in range(1, XB + 1):
        p = step * XB + q
        after = cond_ref[jnp.minimum(p, cond_ref.shape[0] - 1)] - THIRD
        inv = 1.0 / (gap + after + mass)
        alpha, beta = gap * inv, after * inv
        coef_ref[0, p], coef_ref[1, p], coef_ref[2, p] = alpha, beta, inv
        mass_first = mass_first + alpha * mass
        mass = BODY + beta * mass
        gap = alpha * after
        tail_ref[p, 0], tail_ref[p, 1], tail_ref[p, 2] = gap, mass_first, mass
    run_ref[0], run_ref[1], run_ref[2] = gap, mass_first, mass

    carried, xb, ny, nz = adj_ref.shape
    species = conc_ref.shape[0]
    adj_rows = adj_ref.reshape(carried * xb * ny, nz)
    out_rows = out_ref.reshape(carried * xb * ny, nz)
    pitch = xb * ny
    conc32_ref[...] = conc_ref[...].astype(F32).reshape(species * pitch, nz)
    sub = iota((8, nz), 0)
    for x in range(xb):
        for y in range(ny):
            row = x * ny + y
            cols = slice(row * nz, (row + 1) * nz)
            conc = jnp.concatenate(
                [conc32_ref[pl.ds(row + 8 * q * pitch, 8, stride=pitch), :] for q in range(4)], axis=0
            ).astype(BF16)
            x_ref[0:32, cols] = conc
            x_ref[32:64, cols] = conc
            lam = [adj_rows[pl.ds(row + first * pitch, 8, stride=pitch), :] for first in (0, 8, carried - 8)]
            level = jnp.broadcast_to(lev_ref[x, y : y + 1, :], (8, nz))
            marks = jnp.where(level <= sub, 1.0, 0.0)
            x_ref[64:96, cols] = jnp.concatenate(lam + [marks], axis=0).astype(BF16)
    per_tile = TILE // nz
    for tile in range(xb * ny // per_tile):
        slot = tile % act_ref.shape[0]
        every = dot(w_ref[...], x_ref[:, tile * TILE : (tile + 1) * TILE])
        for start, size in CHUNKS:
            got = every[3 * start : 3 * (start + size)]
            weight = got[2 * size :]
            act_ref[slot, 0, start : start + size, :] = (jnp.exp2(got[:size]) * weight).astype(BF16)
            act_ref[slot, 1, start : start + size, :] = (jnp.exp2(got[size : 2 * size]) * weight).astype(BF16)
        chem = dot(c_ref[0], act_ref[slot, 0]) + dot(c_ref[1], act_ref[slot, 1])
        for part in range(per_tile):
            row = tile * per_tile + part
            for q, first in enumerate((0, 8, carried - 8)):
                out_rows[pl.ds(row + first * pitch, 8, stride=pitch), :] = chem[
                    8 * q : 8 * q + 8, part * nz : (part + 1) * nz
                ]


def chemistry(adjoint, log_conc, levels, conduct, orders_fwd, orders_rev, stoich, rate_fwd, rate_rev):
    carried, nx, ny, nz = adjoint.shape
    species, react = log_conc.shape[0], orders_fwd.shape[0]
    whole = lambda a: pl.BlockSpec(a.shape, lambda i: (0,) * len(a.shape))
    small = [orders_fwd.T, orders_rev.T, stoich.T, rate_fwd.reshape(1, react), rate_rev.reshape(1, react)]
    return pl.pallas_call(
        chem_kernel,
        grid=(nx // XB,),
        in_specs=[
            pl.BlockSpec((carried, XB, ny, nz), lambda i: (0, i, 0, 0)),
            pl.BlockSpec((species, XB, ny, nz), lambda i: (0, i, 0, 0)),
            pl.BlockSpec((XB, ny, nz), lambda i: (i, 0, 0)),
            whole(conduct),
        ]
        + [whole(a) for a in small],
        out_specs=[
            pl.BlockSpec((carried, XB, ny, nz), lambda i: (0, i, 0, 0)),
            pl.BlockSpec((3, nx + 1, ny, nz), lambda i: (0, 0, 0, 0)),
            pl.BlockSpec((nx + 1, 3, ny, nz), lambda i: (0, 0, 0, 0)),
        ],
        out_shape=[
            jax.ShapeDtypeStruct(adjoint.shape, F32),
            jax.ShapeDtypeStruct((3, nx + 1, ny, nz), F32),
            jax.ShapeDtypeStruct((nx + 1, 3, ny, nz), F32),
        ],
        scratch_shapes=[
            pltpu.VMEM((K_ROWS, 256), F32),
            pltpu.VMEM((3 * R_PAD, K_ROWS), BF16),
            pltpu.VMEM((2, 32, R_PAD), BF16),
            pltpu.VMEM((species * XB * ny, nz), F32),
            pltpu.VMEM((K_ROWS, XB * ny * nz), BF16),
            pltpu.VMEM((1, 2, R_PAD, TILE), BF16),
            pltpu.VMEM((3, ny, nz), F32),
        ],
        compiler_params=pltpu.CompilerParams(dimension_semantics=("arbitrary",), vmem_limit_bytes=LIMIT),
        cost_estimate=pl.CostEstimate(flops=12 * 10**9, bytes_accessed=4 * 10**6, transcendentals=6_750_000),
        name="chem",
    )(adjoint, log_conc, levels, conduct, *small)


GROUP = 6
GROUPS = 4
ROWS = 16
SB = 2
LB = 11
ANY = pl.BlockSpec(memory_space=pl.ANY)
WHOLE = pl.BlockSpec(memory_space=pltpu.VMEM)
SMALL = pltpu.CompilerParams(vmem_limit_bytes=LIMIT)


def place(s):
    return s // GROUP * ROWS + s % GROUP


def edges_kernel(adj_ref, low_ref, high_ref):
    carried, nx, ny, nz = adj_ref.shape
    mine = lax.axis_index("gy")
    to_high = jnp.where(mine == lax.axis_size("gy") - 1, 0.0, 1.0)
    to_low = jnp.where(mine == 0, 0.0, 1.0)

    @pl.loop(0, carried)
    def _(s):
        for x in range(nx):
            low_ref[s, x] = adj_ref[s, x, ny - 2 : ny, :] * to_high
            high_ref[s, x] = adj_ref[s, x, 0:2, :] * to_low


def edges(adjoint):
    carried, nx, ny, nz = adjoint.shape
    shape = pltpu.VMEM((carried, nx, 2, nz), F32)
    return pl.pallas_call(
        edges_kernel,
        in_specs=[WHOLE],
        out_specs=[WHOLE, WHOLE],
        out_shape=[shape, shape],
        compiler_params=SMALL,
        cost_estimate=pl.CostEstimate(flops=0, bytes_accessed=2 * 10**6, transcendentals=0),
        name="edges",
    )(adjoint)


def split(value):
    high = value.astype(BF16)
    return high, (value - high.astype(F32)).astype(BF16)


def local_kernel(
    diff_ref, cond_ref, adj_ref, chem_ref, near_ref, low_ref, high_ref, coef_ref, tail_ref,
    part_ref, msg_ref, band_ref, parts_ref, zz_ref,
):
    nx, ny, nz = cond_ref.shape
    carried = adj_ref.shape[0]
    stride = GROUPS * ROWS
    msg_ref[...] = jnp.zeros(msg_ref.shape, F32)
    at = nx - 2
    face = cond_ref[nx - 1] - THIRD
    for group in range(GROUPS):
        for r, value in ((6, tail_ref[at, 0]), (7, tail_ref[at, 1]), (14, face), (15, tail_ref[at, 2])):
            msg_ref[pl.ds(group * ROWS + r, ny, stride=stride), :] = value

    k, z = iota((2 * nz, nz), 0), iota((2 * nz, nz), 1)
    gap = jnp.abs(jnp.where(k < nz, k, k - nz) - z)
    band_ref[...] = jnp.where(
        gap == 0, -60.0, jnp.where(gap == 1, 16.0, jnp.where(gap == 2, -1.0, 0.0))
    ).astype(BF16)
    row, lane = iota((ny, nz), 0), iota((ny, nz), 1)
    low_core = lax.axis_index("gz") == 0
    turn1, turn2 = jnp.where(low_core, nz - 1, 1), jnp.where(low_core, nz - 2, 2)
    outer, inner = jnp.where(low_core, nz - 1, 0), jnp.where(low_core, nz - 2, 1)

    @pl.loop(0, carried // LB)
    def _(g):
        for t in range(LB):
            s = g * LB + t
            own_hi, own_lo = split(adj_ref[s].reshape(nx * ny, nz))
            parts_ref[t * nx * ny : (t + 1) * nx * ny, :] = jnp.concatenate([own_hi, own_lo], axis=1)
        zz_ref[...] = dot(parts_ref[...], band_ref[...])
        for t in range(LB):
            s = g * LB + t
            scale = diff_ref[s] * (SECTION * STEP / 12.0)
            b_first, carry = None, None
            for p in range(nx):
                own = adj_ref[s, p]
                low0, low1 = low_ref[s, p, 0:1, :], low_ref[s, p, 1:2, :]
                high0, high1 = high_ref[s, p, 0:1, :], high_ref[s, p, 1:2, :]
                y_up1 = jnp.where(row == ny - 1, high0, pltpu.roll(own, ny - 1, 0))
                y_up2 = jnp.where(row == ny - 1, high1, jnp.where(row == ny - 2, high0, pltpu.roll(own, ny - 2, 0)))
                y_dn1 = jnp.where(row == 0, low1, pltpu.roll(own, 1, 0))
                y_dn2 = jnp.where(row == 0, low0, jnp.where(row == 1, low1, pltpu.roll(own, 2, 0)))
                near = near_ref[s, p]
                near1, near2 = pltpu.roll(near, turn1, 1), pltpu.roll(near, turn2, 1)
                edge = jnp.where(lane == outer, 16.0 * near1 - near2, jnp.where(lane == inner, -near2, 0.0))
                at = (t * nx + p) * ny
                spread = 16.0 * (y_up1 + y_dn1) - (y_up2 + y_dn2) + (zz_ref[at : at + ny, :] + edge)
                b = SECTION * own + (SECTION * STEP) * chem_ref[s, p] + scale * spread
                if p == 0:
                    b_first = b
                elif p < nx - 1:
                    full = b if carry is None else b + carry
                    part_ref[s, p] = full * coef_ref[2, p]
                    b_first = b_first + coef_ref[0, p] * full
                    carry = coef_ref[1, p] * full
                else:
                    b_last = b + carry
            msg_ref[pl.ds(place(s), ny, stride=stride), :] = b_first
            msg_ref[pl.ds(place(s) + 8, ny, stride=stride), :] = b_last


def local_part(diffusivity, adjoint, chem, near, low, high, conduct, coef, ends):
    carried, nx, ny, nz = adjoint.shape
    smem = pl.BlockSpec(memory_space=pltpu.SMEM)
    return pl.pallas_call(
        local_kernel,
        in_specs=[smem] + [WHOLE] * 8,
        out_specs=[WHOLE] * 2,
        out_shape=[
            pltpu.VMEM(adjoint.shape, F32),
            pltpu.VMEM((GROUPS * ny * ROWS, nz), F32),
        ],
        scratch_shapes=[pltpu.VMEM((2 * nz, nz), BF16), pltpu.VMEM((LB * nx * ny, 2 * nz), BF16), pltpu.VMEM((LB * nx * ny, nz), F32)],
        compiler_params=SMALL,
        cost_estimate=pl.CostEstimate(flops=20 * 10**6, bytes_accessed=7 * 10**6, transcendentals=0),
        name="local",
    )(diffusivity, conduct, adjoint, chem, near, low, high, coef, ends)


def chain_kernel(in_ref, out_ref):
    count, _, nz = in_ref.shape
    h, mass, rhs, ends = [], [], [], []
    passed_m = passed_b = None
    for i in range(count):
        low, high = in_ref[i, 0:8, :], in_ref[i, 8:16, :]
        g = jnp.broadcast_to(in_ref[i, 6:7, :], (8, nz))
        m_f = jnp.broadcast_to(in_ref[i, 7:8, :], (8, nz))
        face = jnp.broadcast_to(in_ref[i, 14:15, :], (8, nz))
        m_l = jnp.broadcast_to(in_ref[i, 15:16, :], (8, nz))
        inv = 1.0 / (g + face + m_l)
        a, c = g * inv, face * inv
        m, b = m_f + a * m_l, low + a * high
        if i > 0:
            m, b = m + passed_m, b + passed_b
        passed_m, passed_b = c * m_l, c * high
        h.append(a * face)
        mass.append(m)
        rhs.append(b)
        ends.append((a, c, high * inv))
    half = count // 2
    scale, ratio = [None] * count, [None] * count
    for i in range(half - 1):
        inv = 1.0 / (mass[i] + h[i])
        q = h[i] * inv
        scale[i], ratio[i] = rhs[i] * inv, q
        mass[i + 1] = mass[i + 1] + q * mass[i]
        rhs[i + 1] = rhs[i + 1] + q * rhs[i]
    mass[count - 1] = mass[count - 1] + h[count - 1]
    for i in range(count - 1, half, -1):
        inv = 1.0 / (mass[i] + h[i - 1])
        q = h[i - 1] * inv
        scale[i], ratio[i] = rhs[i] * inv, q
        mass[i - 1] = mass[i - 1] + q * mass[i]
        rhs[i - 1] = rhs[i - 1] + q * rhs[i]
    inv = 1.0 / (mass[half - 1] + h[half - 1])
    q = h[half - 1] * inv
    first = [None] * (count + 1)
    first[half] = (rhs[half] + q * rhs[half - 1]) / (mass[half] + q * mass[half - 1])
    first[half - 1] = rhs[half - 1] * inv + q * first[half]
    for i in range(half - 2, -1, -1):
        first[i] = scale[i] + ratio[i] * first[i + 1]
    for i in range(half + 1, count):
        first[i] = scale[i] + ratio[i] * first[i - 1]
    for i in range(count):
        a, c, part = ends[i]
        last = part + a * first[i]
        if i < count - 1:
            last = last + c * first[i + 1]
        out_ref[i, 0:8, :] = first[i]
        out_ref[i, 8:16, :] = last


def chain(message):
    return pl.pallas_call(
        chain_kernel,
        in_specs=[WHOLE],
        out_specs=WHOLE,
        out_shape=pltpu.VMEM(message.shape, F32),
        compiler_params=SMALL,
        cost_estimate=pl.CostEstimate(flops=10**6, bytes_accessed=10**6, transcendentals=0),
        name="chain",
    )(message)


def back_kernel(coef_ref, ends_ref, part_ref, out_hbm, out_ref, out_sem):
    carried, nx, ny, _ = part_ref.shape
    groups = carried // SB

    def put(g):
        return pltpu.make_async_copy(out_ref.at[pl.ds(g * SB, SB)], out_hbm.at[pl.ds(g * SB, SB)], out_sem.at[g])

    @pl.loop(0, groups)
    def _(g):
        for t in range(SB):
            s = g * SB + t
            first = ends_ref[pl.ds(place(s), ny, stride=GROUPS * ROWS), :]
            value = ends_ref[pl.ds(place(s) + 8, ny, stride=GROUPS * ROWS), :]
            out_ref[s, 0] = first
            out_ref[s, nx - 1] = value
            for p in range(nx - 2, 0, -1):
                value = part_ref[s, p] + coef_ref[0, p] * first + coef_ref[1, p] * value
                out_ref[s, p] = value
        put(g).start()

    @pl.loop(0, groups)
    def _(g):
        put(g).wait()


def back(part, coef, ends):
    groups = part.shape[0] // SB
    return pl.pallas_call(
        back_kernel,
        in_specs=[WHOLE, WHOLE, WHOLE],
        out_specs=ANY,
        out_shape=jax.ShapeDtypeStruct(part.shape, F32),
        scratch_shapes=[pltpu.VMEM(part.shape, F32), pltpu.SemaphoreType.DMA((groups,))],
        compiler_params=SMALL,
        cost_estimate=pl.CostEstimate(flops=2 * 10**6, bytes_accessed=3 * 10**6, transcendentals=0),
        name="back",
    )(coef, ends, part)


def resident(value):
    return pltpu.with_memory_space_constraint(value, pltpu.VMEM)


def shards(
    adjoint, log_conc, levels, conduct, orders_fwd, orders_rev, stoich, rate_fwd, rate_rev, diffusivity
):
    carried, nx, ny, nz = adjoint.shape
    rows_y, blocks = lax.axis_size("gy"), lax.axis_size("gx")
    near = lax.ppermute(adjoint, "gz", [(0, 1), (1, 0)])
    tail, head = edges(adjoint)
    low = lax.ppermute(tail, "gy", [(i, (i + 1) % rows_y) for i in range(rows_y)])
    high = lax.ppermute(head, "gy", [((i + 1) % rows_y, i) for i in range(rows_y)])
    chem, coef, ends_m = chemistry(adjoint, log_conc, levels, conduct, orders_fwd, orders_rev, stoich, rate_fwd, rate_rev)
    part, message = local_part(diffusivity, adjoint, chem, near, low, high, conduct, coef, ends_m)
    message = lax.all_to_all(message.reshape(blocks, ROWS, nz), "gx", 0, 0, tiled=True)
    ends = lax.all_to_all(chain(message), "gx", 0, 0, tiled=True)
    return back(part, coef, ends.reshape(blocks * ROWS, nz))


def solution(mesh):
    cells = P(None, "gx", "gy", "gz")
    planes = P("gx", "gy", "gz")
    in_specs = (cells, cells, planes, planes, P(), P(), P(), P(), P(), P())
    return jax.shard_map(shards, mesh=mesh, in_specs=in_specs, out_specs=cells, check_vma=False)
```

```python
import math

import jax
import jax.numpy as jnp
from jax import lax
from jax.experimental import pallas as pl
from jax.experimental.pallas import tpu as pltpu
from jax.sharding import PartitionSpec as P

SECTION = 0.02
STEP = 0.3
MASS = 0.001
THIRD = MASS / 3.0
BODY = MASS + 2.0 * THIRD
LOG2E = math.log2(math.e)
OFF = -1024.0

K_ROWS = 96
R_PAD = 208
STRIP = 16
CHUNKS = tuple((start, STRIP) for start in range(0, R_PAD, STRIP))
TILE = 4096
XB = 4
LIMIT = 24 * 1024 * 1024
F32 = jnp.float32
BF16 = jnp.bfloat16


def iota(shape, dim):
    return lax.broadcasted_iota(jnp.int32, shape, dim)


def dot(a, b):
    return lax.dot_general(a, b, (((1,), (0,)), ((), ())), preferred_element_type=F32)


def dot_nt(a, b):
    return lax.dot_general(a, b, (((1,), (1,)), ((), ())), preferred_element_type=F32)


def one_hot(mask):
    return jnp.where(mask, 1.0, 0.0).astype(BF16)


def build_weights(of_ref, or_ref, st_ref, rf_ref, rr_ref, wide_ref, w_ref, c_ref):
    species, react = of_ref.shape
    carried = st_ref.shape[0]
    eye = one_hot(iota((R_PAD, 256), 0) == iota((R_PAD, 256), 1))
    pick_row, pick_col = iota((32, 32), 0), iota((32, 32), 1)
    pick = one_hot(pick_col == jnp.where(pick_row < 16, pick_row, jnp.where(pick_row < 24, pick_row - 2, -1)))
    sub, tier = iota((8, 256), 0), 4 * iota((8, 256), 1) // react
    full = []
    for index, (orders, rate) in enumerate(((of_ref, rf_ref), (or_ref, rr_ref))):
        wide_ref[...] = jnp.zeros(wide_ref.shape, F32)
        wide_ref[0:species, 0:react] = orders[...].astype(F32)
        plain = wide_ref[0:32, :]
        sign = 1.0 if index == 0 else -1.0
        c_ref[index] = (sign * dot(pick, plain.astype(BF16)))[:, 0:R_PAD].astype(BF16)
        scaled = plain * LOG2E
        hi = scaled.astype(BF16).astype(F32)
        wide_ref[0:32, :] = hi
        wide_ref[32:64, :] = scaled - hi
        wide_ref[88:89, 0:react] = jnp.log(rate[...]) * LOG2E
        r = jnp.broadcast_to(wide_ref[88:89, :], (8, 256))
        r0 = r.astype(BF16).astype(F32)
        r1 = (r - r0).astype(BF16).astype(F32)
        parts = jnp.where(sub == 3, r0, jnp.where(sub == 4, r1, jnp.where(sub == 5, r - r0 - r1, 0.0)))
        wide_ref[88:96, :] = jnp.where(sub < 3, jnp.where(tier > sub, OFF, 0.0), parts)
        full.append(dot_nt(eye, wide_ref[...].astype(BF16)).astype(BF16))
    wide_ref[...] = jnp.zeros(wide_ref.shape, F32)
    wide_ref[64:80, 0:react] = st_ref[0:16, :].astype(F32)
    wide_ref[82 : 66 + carried, 0:react] = st_ref[16:carried, :].astype(F32)
    full.append(dot_nt(eye, wide_ref[...].astype(BF16)).astype(BF16))
    base = 0
    for start, size in CHUNKS:
        for part in full:
            w_ref[base : base + size, :] = part[start : start + size]
            base += size


def chem_kernel(
    adj_ref, conc_ref, lev_ref, cond_ref, of_ref, or_ref, st_ref, rf_ref, rr_ref,
    out_ref, coef_ref, tail_ref,
    wide_ref, w_ref, c_ref, conc32_ref, x_ref, act_ref, run_ref,
):
    step = pl.program_id(0)

    @pl.when(step == 0)
    def _():
        run_ref[0] = cond_ref[0] - THIRD
        run_ref[1] = jnp.where(lax.axis_index("gx") == 0, MASS + THIRD, BODY) * jnp.ones(run_ref.shape[1:], F32)
        run_ref[2] = jnp.full(run_ref.shape[1:], BODY, F32)
        build_weights(of_ref, or_ref, st_ref, rf_ref, rr_ref, wide_ref, w_ref, c_ref)

    gap, mass_first, mass = run_ref[0], run_ref[1], run_ref[2]
    for q in range(1, XB + 1):
        p = step * XB + q
        after = cond_ref[jnp.minimum(p, cond_ref.shape[0] - 1)] - THIRD
        inv = 1.0 / (gap + after + mass)
        alpha, beta = gap * inv, after * inv
        coef_ref[0, p], coef_ref[1, p], coef_ref[2, p] = alpha, beta, inv
        mass_first = mass_first + alpha * mass
        mass = BODY + beta * mass
        gap = alpha * after
        tail_ref[p, 0], tail_ref[p, 1], tail_ref[p, 2] = gap, mass_first, mass
    run_ref[0], run_ref[1], run_ref[2] = gap, mass_first, mass

    carried, xb, ny, nz = adj_ref.shape
    species = conc_ref.shape[0]
    adj_rows = adj_ref.reshape(carried * xb * ny, nz)
    out_rows = out_ref.reshape(carried * xb * ny, nz)
    pitch = xb * ny
    conc32_ref[...] = conc_ref[...].astype(F32).reshape(species * pitch, nz)
    sub = iota((8, nz), 0)
    for x in range(xb):
        for y in range(ny):
            row = x * ny + y
            cols = slice(row * nz, (row + 1) * nz)
            conc = jnp.concatenate(
                [conc32_ref[pl.ds(row + 8 * q * pitch, 8, stride=pitch), :] for q in range(4)], axis=0
            ).astype(BF16)
            x_ref[0:32, cols] = conc
            x_ref[32:64, cols] = conc
            lam = [adj_rows[pl.ds(row + first * pitch, 8, stride=pitch), :] for first in (0, 8, carried - 8)]
            level = jnp.broadcast_to(lev_ref[x, y : y + 1, :], (8, nz))
            marks = jnp.where(level <= sub, 1.0, 0.0)
            x_ref[64:96, cols] = jnp.concatenate(lam + [marks], axis=0).astype(BF16)
    per_tile = TILE // nz
    for tile in range(xb * ny // per_tile):
        slot = tile % act_ref.shape[0]
        every = dot(w_ref[...], x_ref[:, tile * TILE : (tile + 1) * TILE])
        for start, size in CHUNKS:
            got = every[3 * start : 3 * (start + size)]
            weight = got[2 * size :]
            act_ref[slot, 0, start : start + size, :] = (jnp.exp2(got[:size]) * weight).astype(BF16)
            act_ref[slot, 1, start : start + size, :] = (jnp.exp2(got[size : 2 * size]) * weight).astype(BF16)
        chem = dot(c_ref[0], act_ref[slot, 0]) + dot(c_ref[1], act_ref[slot, 1])
        for part in range(per_tile):
            row = tile * per_tile + part
            for q, first in enumerate((0, 8, carried - 8)):
                out_rows[pl.ds(row + first * pitch, 8, stride=pitch), :] = chem[
                    8 * q : 8 * q + 8, part * nz : (part + 1) * nz
                ]


def chemistry(adjoint, log_conc, levels, conduct, orders_fwd, orders_rev, stoich, rate_fwd, rate_rev):
    carried, nx, ny, nz = adjoint.shape
    species, react = log_conc.shape[0], orders_fwd.shape[0]
    whole = lambda a: pl.BlockSpec(a.shape, lambda i: (0,) * len(a.shape))
    small = [orders_fwd.T, orders_rev.T, stoich.T, rate_fwd.reshape(1, react), rate_rev.reshape(1, react)]
    return pl.pallas_call(
        chem_kernel,
        grid=(nx // XB,),
        in_specs=[
            pl.BlockSpec((carried, XB, ny, nz), lambda i: (0, i, 0, 0)),
            pl.BlockSpec((species, XB, ny, nz), lambda i: (0, i, 0, 0)),
            pl.BlockSpec((XB, ny, nz), lambda i: (i, 0, 0)),
            whole(conduct),
        ]
        + [whole(a) for a in small],
        out_specs=[
            pl.BlockSpec((carried, XB, ny, nz), lambda i: (0, i, 0, 0)),
            pl.BlockSpec((3, nx + 1, ny, nz), lambda i: (0, 0, 0, 0)),
            pl.BlockSpec((nx + 1, 3, ny, nz), lambda i: (0, 0, 0, 0)),
        ],
        out_shape=[
            jax.ShapeDtypeStruct(adjoint.shape, F32),
            jax.ShapeDtypeStruct((3, nx + 1, ny, nz), F32),
            jax.ShapeDtypeStruct((nx + 1, 3, ny, nz), F32),
        ],
        scratch_shapes=[
            pltpu.VMEM((K_ROWS, 256), F32),
            pltpu.VMEM((3 * R_PAD, K_ROWS), BF16),
            pltpu.VMEM((2, 32, R_PAD), BF16),
            pltpu.VMEM((species * XB * ny, nz), F32),
            pltpu.VMEM((K_ROWS, XB * ny * nz), BF16),
            pltpu.VMEM((1, 2, R_PAD, TILE), BF16),
            pltpu.VMEM((3, ny, nz), F32),
        ],
        compiler_params=pltpu.CompilerParams(dimension_semantics=("arbitrary",), vmem_limit_bytes=LIMIT),
        cost_estimate=pl.CostEstimate(flops=12 * 10**9, bytes_accessed=4 * 10**6, transcendentals=6_750_000),
        name="chem",
    )(adjoint, log_conc, levels, conduct, *small)


GROUP = 6
GROUPS = 4
ROWS = 16
SB = 2
LB = 11
ANY = pl.BlockSpec(memory_space=pl.ANY)
WHOLE = pl.BlockSpec(memory_space=pltpu.VMEM)
SMALL = pltpu.CompilerParams(vmem_limit_bytes=LIMIT)


def place(s):
    return s // GROUP * ROWS + s % GROUP


def crossing(adj_ref, s):
    carried, nx, ny, nz = adj_ref.shape
    rows = adj_ref.reshape(carried * nx * ny, nz)
    f0, f1, f6, f7 = [rows[pl.ds(s * nx * ny + r, nx, stride=ny), :] for r in (0, 1, ny - 2, ny - 1)]
    return (16.0 * f7 - f6, -f7), (-f0, 16.0 * f0 - f1)


def edges_kernel(adj_ref, low_ref, high_ref):
    carried, nx, ny, nz = adj_ref.shape
    mine = lax.axis_index("gy")
    to_high = jnp.where(mine == lax.axis_size("gy") - 1, 0.0, 1.0)
    to_low = jnp.where(mine == 0, 0.0, 1.0)

    @pl.loop(0, carried)
    def _(s):
        down, up = crossing(adj_ref, s)
        for k in range(2):
            low_ref[s, k] = down[k] * to_high
            high_ref[s, k] = up[k] * to_low


def edges(adjoint):
    carried, nx, ny, nz = adjoint.shape
    shape = pltpu.VMEM((carried, 2, nx, nz), F32)
    return pl.pallas_call(
        edges_kernel,
        in_specs=[WHOLE],
        out_specs=[WHOLE, WHOLE],
        out_shape=[shape, shape],
        compiler_params=SMALL,
        cost_estimate=pl.CostEstimate(flops=0, bytes_accessed=2 * 10**6, transcendentals=0),
        name="edges",
    )(adjoint)


def split(value):
    high = value.astype(BF16)
    return high, (value - high.astype(F32)).astype(BF16)


def local_kernel(
    diff_ref, cond_ref, adj_ref, chem_ref, near_ref, low_ref, high_ref, coef_ref, tail_ref,
    part_ref, msg_ref, band_ref, parts_ref, zz_ref,
):
    nx, ny, nz = cond_ref.shape
    carried = adj_ref.shape[0]
    stride = GROUPS * ROWS
    msg_ref[...] = jnp.zeros(msg_ref.shape, F32)
    at = nx - 2
    face = cond_ref[nx - 1] - THIRD
    for group in range(GROUPS):
        for r, value in ((6, tail_ref[at, 0]), (7, tail_ref[at, 1]), (14, face), (15, tail_ref[at, 2])):
            msg_ref[pl.ds(group * ROWS + r, ny, stride=stride), :] = value

    k, z = iota((2 * nz, nz), 0), iota((2 * nz, nz), 1)
    gap = jnp.abs(jnp.where(k < nz, k, k - nz) - z)
    band_ref[...] = jnp.where(
        gap == 0, -60.0, jnp.where(gap == 1, 16.0, jnp.where(gap == 2, -1.0, 0.0))
    ).astype(BF16)
    lane = iota((ny, nz), 1)
    low_core = lax.axis_index("gz") == 0
    turn1, turn2 = jnp.where(low_core, nz - 1, 1), jnp.where(low_core, nz - 2, 2)
    outer, inner = jnp.where(low_core, nz - 1, 0), jnp.where(low_core, nz - 2, 1)

    @pl.loop(0, carried // LB)
    def _(g):
        for t in range(LB):
            s = g * LB + t
            own_hi, own_lo = split(adj_ref[s].reshape(nx * ny, nz))
            parts_ref[t * nx * ny : (t + 1) * nx * ny, :] = jnp.concatenate([own_hi, own_lo], axis=1)
        zz_ref[...] = dot(parts_ref[...], band_ref[...])
        for t in range(LB):
            s = g * LB + t
            down, up = crossing(adj_ref, s)
            for r, own_term, got in (
                (0, down[0], low_ref[s, 0]),
                (1, down[1], low_ref[s, 1]),
                (ny - 2, up[0], high_ref[s, 0]),
                (ny - 1, up[1], high_ref[s, 1]),
            ):
                at = pl.ds(t * nx * ny + r, nx, stride=ny)
                zz_ref[at, :] = zz_ref[at, :] + (got - own_term)
        for t in range(LB):
            s = g * LB + t
            scale = diff_ref[s] * (SECTION * STEP / 12.0)
            b_first, carry = None, None
            for p in range(nx):
                own = adj_ref[s, p]
                y_near = pltpu.roll(own, ny - 1, 0) + pltpu.roll(own, 1, 0)
                y_far = pltpu.roll(own, ny - 2, 0) + pltpu.roll(own, 2, 0)
                near = near_ref[s, p]
                near1, near2 = pltpu.roll(near, turn1, 1), pltpu.roll(near, turn2, 1)
                edge = jnp.where(lane == outer, 16.0 * near1 - near2, jnp.where(lane == inner, -near2, 0.0))
                at = (t * nx + p) * ny
                spread = 16.0 * y_near - y_far + (zz_ref[at : at + ny, :] + edge)
                b = SECTION * own + (SECTION * STEP) * chem_ref[s, p] + scale * spread
                if p == 0:
                    b_first = b
                elif p < nx - 1:
                    full = b if carry is None else b + carry
                    part_ref[s, p] = full * coef_ref[2, p]
                    b_first = b_first + coef_ref[0, p] * full
                    carry = coef_ref[1, p] * full
                else:
                    b_last = b + carry
            msg_ref[pl.ds(place(s), ny, stride=stride), :] = b_first
            msg_ref[pl.ds(place(s) + 8, ny, stride=stride), :] = b_last


def local_part(diffusivity, adjoint, chem, near, low, high, conduct, coef, ends):
    carried, nx, ny, nz = adjoint.shape
    smem = pl.BlockSpec(memory_space=pltpu.SMEM)
    return pl.pallas_call(
        local_kernel,
        in_specs=[smem] + [WHOLE] * 8,
        out_specs=[WHOLE] * 2,
        out_shape=[
            pltpu.VMEM(adjoint.shape, F32),
            pltpu.VMEM((GROUPS * ny * ROWS, nz), F32),
        ],
        scratch_shapes=[pltpu.VMEM((2 * nz, nz), BF16), pltpu.VMEM((LB * nx * ny, 2 * nz), BF16), pltpu.VMEM((LB * nx * ny, nz), F32)],
        compiler_params=SMALL,
        cost_estimate=pl.CostEstimate(flops=20 * 10**6, bytes_accessed=7 * 10**6, transcendentals=0),
        name="local",
    )(diffusivity, conduct, adjoint, chem, near, low, high, coef, ends)


def chain_kernel(in_ref, out_ref):
    count, _, nz = in_ref.shape
    h, mass, rhs, ends = [], [], [], []
    passed_m = passed_b = None
    for i in range(count):
        low, high = in_ref[i, 0:8, :], in_ref[i, 8:16, :]
        g = jnp.broadcast_to(in_ref[i, 6:7, :], (8, nz))
        m_f = jnp.broadcast_to(in_ref[i, 7:8, :], (8, nz))
        face = jnp.broadcast_to(in_ref[i, 14:15, :], (8, nz))
        m_l = jnp.broadcast_to(in_ref[i, 15:16, :], (8, nz))
        inv = 1.0 / (g + face + m_l)
        a, c = g * inv, face * inv
        m, b = m_f + a * m_l, low + a * high
        if i > 0:
            m, b = m + passed_m, b + passed_b
        passed_m, passed_b = c * m_l, c * high
        h.append(a * face)
        mass.append(m)
        rhs.append(b)
        ends.append((a, c, high * inv))
    half = count // 2
    scale, ratio = [None] * count, [None] * count
    for i in range(half - 1):
        inv = 1.0 / (mass[i] + h[i])
        q = h[i] * inv
        scale[i], ratio[i] = rhs[i] * inv, q
        mass[i + 1] = mass[i + 1] + q * mass[i]
        rhs[i + 1] = rhs[i + 1] + q * rhs[i]
    mass[count - 1] = mass[count - 1] + h[count - 1]
    for i in range(count - 1, half, -1):
        inv = 1.0 / (mass[i] + h[i - 1])
        q = h[i - 1] * inv
        scale[i], ratio[i] = rhs[i] * inv, q
        mass[i - 1] = mass[i - 1] + q * mass[i]
        rhs[i - 1] = rhs[i - 1] + q * rhs[i]
    inv = 1.0 / (mass[half - 1] + h[half - 1])
    q = h[half - 1] * inv
    first = [None] * (count + 1)
    first[half] = (rhs[half] + q * rhs[half - 1]) / (mass[half] + q * mass[half - 1])
    first[half - 1] = rhs[half - 1] * inv + q * first[half]
    for i in range(half - 2, -1, -1):
        first[i] = scale[i] + ratio[i] * first[i + 1]
    for i in range(half + 1, count):
        first[i] = scale[i] + ratio[i] * first[i - 1]
    for i in range(count):
        a, c, part = ends[i]
        last = part + a * first[i]
        if i < count - 1:
            last = last + c * first[i + 1]
        out_ref[i, 0] = first[i][0:4]
        out_ref[i, 1, 0:2] = first[i][4:6]
        out_ref[i, 1, 2:4] = last[0:2]
        out_ref[i, 2] = last[2:6]


def chain(message):
    return pl.pallas_call(
        chain_kernel,
        in_specs=[WHOLE],
        out_specs=WHOLE,
        out_shape=pltpu.VMEM((message.shape[0], 3, 4, message.shape[2]), F32),
        compiler_params=SMALL,
        cost_estimate=pl.CostEstimate(flops=10**6, bytes_accessed=10**6, transcendentals=0),
        name="chain",
    )(message)


def back_kernel(coef_ref, got_ref, part_ref, out_hbm, ends_ref, out_ref, out_sem):
    carried, nx, ny, _ = part_ref.shape
    groups = carried // SB
    for i in range(got_ref.shape[0]):
        top = i * ROWS
        ends_ref[top : top + 4, :] = got_ref[i, 0]
        ends_ref[top + 4 : top + 6, :] = got_ref[i, 1, 0:2]
        ends_ref[top + 8 : top + 10, :] = got_ref[i, 1, 2:4]
        ends_ref[top + 10 : top + 14, :] = got_ref[i, 2]

    def put(g):
        return pltpu.make_async_copy(out_ref.at[pl.ds(g * SB, SB)], out_hbm.at[pl.ds(g * SB, SB)], out_sem.at[g])

    @pl.loop(0, groups)
    def _(g):
        for t in range(SB):
            s = g * SB + t
            first = ends_ref[pl.ds(place(s), ny, stride=GROUPS * ROWS), :]
            value = ends_ref[pl.ds(place(s) + 8, ny, stride=GROUPS * ROWS), :]
            out_ref[s, 0] = first
            out_ref[s, nx - 1] = value
            for p in range(nx - 2, 0, -1):
                value = part_ref[s, p] + coef_ref[0, p] * first + coef_ref[1, p] * value
                out_ref[s, p] = value
        put(g).start()

    @pl.loop(0, groups)
    def _(g):
        put(g).wait()


def back(part, coef, ends):
    groups = part.shape[0] // SB
    return pl.pallas_call(
        back_kernel,
        in_specs=[WHOLE, WHOLE, WHOLE],
        out_specs=ANY,
        out_shape=jax.ShapeDtypeStruct(part.shape, F32),
        scratch_shapes=[
            pltpu.VMEM((ends.shape[0] * ROWS, part.shape[3]), F32),
            pltpu.VMEM(part.shape, F32),
            pltpu.SemaphoreType.DMA((groups,)),
        ],
        compiler_params=SMALL,
        cost_estimate=pl.CostEstimate(flops=2 * 10**6, bytes_accessed=3 * 10**6, transcendentals=0),
        name="back",
    )(coef, ends, part)


def resident(value):
    return pltpu.with_memory_space_constraint(value, pltpu.VMEM)


def shards(
    adjoint, log_conc, levels, conduct, orders_fwd, orders_rev, stoich, rate_fwd, rate_rev, diffusivity
):
    carried, nx, ny, nz = adjoint.shape
    rows_y, blocks = lax.axis_size("gy"), lax.axis_size("gx")
    near = lax.ppermute(adjoint, "gz", [(0, 1), (1, 0)])
    tail, head = edges(adjoint)
    low = lax.ppermute(tail, "gy", [(i, (i + 1) % rows_y) for i in range(rows_y)])
    high = lax.ppermute(head, "gy", [((i + 1) % rows_y, i) for i in range(rows_y)])
    chem, coef, ends_m = chemistry(adjoint, log_conc, levels, conduct, orders_fwd, orders_rev, stoich, rate_fwd, rate_rev)
    part, message = local_part(diffusivity, adjoint, chem, near, low, high, conduct, coef, ends_m)
    message = lax.all_to_all(message.reshape(blocks, ROWS, nz), "gx", 0, 0, tiled=True)
    ends = lax.all_to_all(chain(message), "gx", 0, 0, tiled=True)
    return back(part, coef, ends)


def solution(mesh):
    cells = P(None, "gx", "gy", "gz")
    planes = P("gx", "gy", "gz")
    in_specs = (cells, cells, planes, planes, P(), P(), P(), P(), P(), P())
    return jax.shard_map(shards, mesh=mesh, in_specs=in_specs, out_specs=cells, check_vma=False)
```

```python
import jax
import jax.numpy as jnp
from jax import lax
from jax.experimental import pallas as pl
from jax.experimental.pallas import tpu as pltpu
from jax.sharding import PartitionSpec as P

SECTION = 0.02
STEP = 0.3
MASS = 0.001
THIRD = MASS / 3.0
BODY = MASS + 2.0 * THIRD
OFF = -1024.0

K_ROWS = 64
R_PAD = 208
STRIP = 16
CHUNKS = tuple((start, STRIP) for start in range(0, R_PAD, STRIP))
TILE = 4096
XB = 4
LIMIT = 24 * 1024 * 1024
F32 = jnp.float32
BF16 = jnp.bfloat16


def iota(shape, dim):
    return lax.broadcasted_iota(jnp.int32, shape, dim)


def dot(a, b):
    return lax.dot_general(a, b, (((1,), (0,)), ((), ())), preferred_element_type=F32)


def dot_nt(a, b):
    return lax.dot_general(a, b, (((1,), (1,)), ((), ())), preferred_element_type=F32)


def one_hot(mask):
    return jnp.where(mask, 1.0, 0.0).astype(BF16)


def build_weights(of_ref, or_ref, st_ref, rf_ref, rr_ref, wide_ref, w_ref, c_ref):
    species, react = of_ref.shape
    carried = st_ref.shape[0]
    eye = one_hot(iota((R_PAD, 256), 0) == iota((R_PAD, 256), 1))
    pick_row, pick_col = iota((32, 32), 0), iota((32, 32), 1)
    pick = one_hot(pick_col == jnp.where(
        pick_row < 16, pick_row, jnp.where((pick_row > 17) & (pick_row < 24), pick_row - 2, -1)
    ))
    sub, tier = iota((8, 256), 0), 4 * iota((8, 256), 1) // react
    full = []
    for index, (orders, rate) in enumerate(((of_ref, rf_ref), (or_ref, rr_ref))):
        wide_ref[...] = jnp.zeros(wide_ref.shape, F32)
        wide_ref[0:species, 0:react] = orders[...].astype(F32)
        plain = wide_ref[0:32, :]
        sign = 1.0 if index == 0 else -1.0
        c_ref[index] = (sign * dot(pick, plain.astype(BF16)))[:, 0:R_PAD].astype(BF16)
        wide_ref[56:57, 0:react] = jnp.log(rate[...])
        r = jnp.broadcast_to(wide_ref[56:57, :], (8, 256))
        r0 = r.astype(BF16).astype(F32)
        r1 = (r - r0).astype(BF16).astype(F32)
        parts = jnp.where(sub == 3, r0, jnp.where(sub == 4, r1, jnp.where(sub == 5, r - r0 - r1, 0.0)))
        wide_ref[56:64, :] = jnp.where(sub < 3, jnp.where(tier > sub, OFF, 0.0), parts)
        full.append(dot_nt(eye, wide_ref[...].astype(BF16)).astype(BF16))
    wide_ref[...] = jnp.zeros(wide_ref.shape, F32)
    wide_ref[32:48, 0:react] = st_ref[0:16, :].astype(F32)
    wide_ref[50 : 34 + carried, 0:react] = st_ref[16:carried, :].astype(F32)
    full.append(dot_nt(eye, wide_ref[...].astype(BF16)).astype(BF16))
    base = 0
    for start, size in CHUNKS:
        for part in full:
            w_ref[base : base + size, :] = part[start : start + size]
            base += size


def chem_kernel(
    adj_ref, conc_ref, lev_ref, cond_ref, of_ref, or_ref, st_ref, rf_ref, rr_ref,
    out_ref, spread_ref, coef_ref, tail_ref,
    wide_ref, w_ref, c_ref, conc32_ref, x_ref, act_ref, run_ref,
):
    step = pl.program_id(0)

    @pl.when(step == 0)
    def _():
        run_ref[0] = cond_ref[0] - THIRD
        run_ref[1] = jnp.where(lax.axis_index("gx") == 0, MASS + THIRD, BODY) * jnp.ones(run_ref.shape[1:], F32)
        run_ref[2] = jnp.full(run_ref.shape[1:], BODY, F32)
        build_weights(of_ref, or_ref, st_ref, rf_ref, rr_ref, wide_ref, w_ref, c_ref)

    gap, mass_first, mass = run_ref[0], run_ref[1], run_ref[2]
    for q in range(1, XB + 1):
        p = step * XB + q
        after = cond_ref[jnp.minimum(p, cond_ref.shape[0] - 1)] - THIRD
        inv = 1.0 / (gap + after + mass)
        alpha, beta = gap * inv, after * inv
        coef_ref[0, p], coef_ref[1, p], coef_ref[2, p] = alpha, beta, inv
        mass_first = mass_first + alpha * mass
        mass = BODY + beta * mass
        gap = alpha * after
        tail_ref[p, 0], tail_ref[p, 1], tail_ref[p, 2] = gap, mass_first, mass
    run_ref[0], run_ref[1], run_ref[2] = gap, mass_first, mass

    carried, xb, ny, nz = adj_ref.shape
    species = conc_ref.shape[0]
    adj_rows = adj_ref.reshape(carried * xb * ny, nz)
    out_rows = out_ref.reshape(carried * xb * ny, nz)
    pitch = xb * ny
    conc32_ref[...] = conc_ref[...].astype(F32).reshape(species * pitch, nz)
    sub = iota((8, nz), 0)
    for x in range(xb):
        for y in range(ny):
            row = x * ny + y
            cols = slice(row * nz, (row + 1) * nz)
            conc = jnp.concatenate(
                [conc32_ref[pl.ds(row + 8 * q * pitch, 8, stride=pitch), :] for q in range(4)], axis=0
            ).astype(BF16)
            x_ref[0:32, cols] = conc
            lam = [adj_rows[pl.ds(row + first * pitch, 8, stride=pitch), :] for first in (0, 8, carried - 8)]
            level = jnp.broadcast_to(lev_ref[x, y : y + 1, :], (8, nz))
            marks = jnp.where(level <= sub, 1.0, 0.0)
            x_ref[32:64, cols] = jnp.concatenate(lam + [marks], axis=0).astype(BF16)
    lane = iota((ny, nz), 1)
    for x in range(xb):
        for k in range(carried):
            own = adj_ref[k, x]
            near = pltpu.roll(own, ny - 1, 0) + pltpu.roll(own, 1, 0)
            near = near + jnp.where(lane == nz - 1, 0.0, pltpu.roll(own, nz - 1, 1))
            near = near + jnp.where(lane == 0, 0.0, pltpu.roll(own, 1, 1))
            far = pltpu.roll(own, ny - 2, 0) + pltpu.roll(own, 2, 0)
            far = far + jnp.where(lane >= nz - 2, 0.0, pltpu.roll(own, nz - 2, 1))
            far = far + jnp.where(lane < 2, 0.0, pltpu.roll(own, 2, 1))
            out_ref[k, x] = SECTION * own
            spread_ref[k, x] = 16.0 * near - far - 60.0 * own
    per_tile = TILE // nz
    for tile in range(xb * ny // per_tile):
        slot = tile % act_ref.shape[0]
        every = dot(w_ref[...], x_ref[:, tile * TILE : (tile + 1) * TILE])
        for start, size in CHUNKS:
            got = every[3 * start : 3 * (start + size)]
            weight = got[2 * size :]
            act_ref[slot, 0, start : start + size, :] = (jnp.exp(got[:size]) * weight).astype(BF16)
            act_ref[slot, 1, start : start + size, :] = (jnp.exp(got[size : 2 * size]) * weight).astype(BF16)
        chem = dot(c_ref[0], act_ref[slot, 0]) + dot(c_ref[1], act_ref[slot, 1])
        for part in range(per_tile):
            row = tile * per_tile + part
            for q, first in enumerate((0, 8, carried - 8)):
                at = pl.ds(row + first * pitch, 8, stride=pitch)
                term = chem[8 * q : 8 * q + 8, part * nz : (part + 1) * nz]
                out_rows[at, :] = out_rows[at, :] + (SECTION * STEP) * term


def chemistry(adjoint, log_conc, levels, conduct, orders_fwd, orders_rev, stoich, rate_fwd, rate_rev):
    carried, nx, ny, nz = adjoint.shape
    species, react = log_conc.shape[0], orders_fwd.shape[0]
    whole = lambda a: pl.BlockSpec(a.shape, lambda i: (0,) * len(a.shape))
    small = [orders_fwd.T, orders_rev.T, stoich.T, rate_fwd.reshape(1, react), rate_rev.reshape(1, react)]
    return pl.pallas_call(
        chem_kernel,
        grid=(nx // XB,),
        in_specs=[
            pl.BlockSpec((carried, XB, ny, nz), lambda i: (0, i, 0, 0)),
            pl.BlockSpec((species, XB, ny, nz), lambda i: (0, i, 0, 0)),
            pl.BlockSpec((XB, ny, nz), lambda i: (i, 0, 0)),
            whole(conduct),
        ]
        + [whole(a) for a in small],
        out_specs=[pl.BlockSpec((carried, XB, ny, nz), lambda i: (0, i, 0, 0))] * 2
        + [
            pl.BlockSpec((3, nx + 1, ny, nz), lambda i: (0, 0, 0, 0)),
            pl.BlockSpec((nx + 1, 3, ny, nz), lambda i: (0, 0, 0, 0)),
        ],
        out_shape=[jax.ShapeDtypeStruct(adjoint.shape, F32)] * 2
        + [
            jax.ShapeDtypeStruct((3, nx + 1, ny, nz), F32),
            jax.ShapeDtypeStruct((nx + 1, 3, ny, nz), F32),
        ],
        scratch_shapes=[
            pltpu.VMEM((K_ROWS, 256), F32),
            pltpu.VMEM((3 * R_PAD, K_ROWS), BF16),
            pltpu.VMEM((2, 32, R_PAD), BF16),
            pltpu.VMEM((species * XB * ny, nz), F32),
            pltpu.VMEM((K_ROWS, XB * ny * nz), BF16),
            pltpu.VMEM((1, 2, R_PAD, TILE), BF16),
            pltpu.VMEM((3, ny, nz), F32),
        ],
        compiler_params=pltpu.CompilerParams(dimension_semantics=("arbitrary",), vmem_limit_bytes=LIMIT),
        cost_estimate=pl.CostEstimate(flops=12 * 10**9, bytes_accessed=4 * 10**6, transcendentals=6_750_000),
        name="chem",
    )(adjoint, log_conc, levels, conduct, *small)


GROUP = 6
GROUPS = 4
ROWS = 16
SB = 2
LB = 11
ANY = pl.BlockSpec(memory_space=pl.ANY)
WHOLE = pl.BlockSpec(memory_space=pltpu.VMEM)
SMALL = pltpu.CompilerParams(vmem_limit_bytes=LIMIT)


def place(s):
    return s // GROUP * ROWS + s % GROUP


def crossing(adj_ref, s):
    carried, nx, ny, nz = adj_ref.shape
    rows = adj_ref.reshape(carried * nx * ny, nz)
    f0, f1, f6, f7 = [rows[pl.ds(s * nx * ny + r, nx, stride=ny), :] for r in (0, 1, ny - 2, ny - 1)]
    return (16.0 * f7 - f6, -f7), (-f0, 16.0 * f0 - f1)


def edges_kernel(adj_ref, low_ref, high_ref):
    carried, nx, ny, nz = adj_ref.shape
    mine = lax.axis_index("gy")
    to_high = jnp.where(mine == lax.axis_size("gy") - 1, 0.0, 1.0)
    to_low = jnp.where(mine == 0, 0.0, 1.0)

    @pl.loop(0, carried)
    def _(s):
        down, up = crossing(adj_ref, s)
        for k in range(2):
            low_ref[s, k] = down[k] * to_high
            high_ref[s, k] = up[k] * to_low


def edges(adjoint):
    carried, nx, ny, nz = adjoint.shape
    shape = pltpu.VMEM((carried, 2, nx, nz), F32)
    return pl.pallas_call(
        edges_kernel,
        in_specs=[WHOLE],
        out_specs=[WHOLE, WHOLE],
        out_shape=[shape, shape],
        compiler_params=SMALL,
        cost_estimate=pl.CostEstimate(flops=0, bytes_accessed=2 * 10**6, transcendentals=0),
        name="edges",
    )(adjoint)


def local_kernel(
    diff_ref, cond_ref, adj_ref, base_ref, spread_ref, near_ref, low_ref, high_ref, coef_ref, tail_ref,
    part_ref, msg_ref, add_ref,
):
    nx, ny, nz = cond_ref.shape
    carried = adj_ref.shape[0]
    stride = GROUPS * ROWS
    msg_ref[...] = jnp.zeros(msg_ref.shape, F32)
    at = nx - 2
    face = cond_ref[nx - 1] - THIRD
    for group in range(GROUPS):
        for r, value in ((6, tail_ref[at, 0]), (7, tail_ref[at, 1]), (14, face), (15, tail_ref[at, 2])):
            msg_ref[pl.ds(group * ROWS + r, ny, stride=stride), :] = value

    add_ref[...] = jnp.zeros(add_ref.shape, F32)
    lane = iota((ny, nz), 1)
    low_core = lax.axis_index("gz") == 0
    turn1, turn2 = jnp.where(low_core, nz - 1, 1), jnp.where(low_core, nz - 2, 2)
    outer, inner = jnp.where(low_core, nz - 1, 0), jnp.where(low_core, nz - 2, 1)

    @pl.loop(0, carried // LB)
    def _(g):
        for t in range(LB):
            s = g * LB + t
            down, up = crossing(adj_ref, s)
            for r, own_term, got in (
                (0, down[0], low_ref[s, 0]),
                (1, down[1], low_ref[s, 1]),
                (ny - 2, up[0], high_ref[s, 0]),
                (ny - 1, up[1], high_ref[s, 1]),
            ):
                add_ref[pl.ds(t * nx * ny + r, nx, stride=ny), :] = got - own_term
        for t in range(LB):
            s = g * LB + t
            scale = diff_ref[s] * (SECTION * STEP / 12.0)
            b_first, carry = None, None
            for p in range(nx):
                near = near_ref[s, p]
                near1, near2 = pltpu.roll(near, turn1, 1), pltpu.roll(near, turn2, 1)
                edge = jnp.where(lane == outer, 16.0 * near1 - near2, jnp.where(lane == inner, -near2, 0.0))
                at = (t * nx + p) * ny
                b = base_ref[s, p] + scale * (spread_ref[s, p] + add_ref[at : at + ny, :] + edge)
                if p == 0:
                    b_first = b
                elif p < nx - 1:
                    full = b if carry is None else b + carry
                    part_ref[s, p] = full * coef_ref[2, p]
                    b_first = b_first + coef_ref[0, p] * full
                    carry = coef_ref[1, p] * full
                else:
                    b_last = b + carry
            msg_ref[pl.ds(place(s), ny, stride=stride), :] = b_first
            msg_ref[pl.ds(place(s) + 8, ny, stride=stride), :] = b_last


def local_part(diffusivity, adjoint, chem, spread, near, low, high, conduct, coef, ends):
    carried, nx, ny, nz = adjoint.shape
    smem = pl.BlockSpec(memory_space=pltpu.SMEM)
    return pl.pallas_call(
        local_kernel,
        in_specs=[smem] + [WHOLE] * 9,
        out_specs=[WHOLE] * 2,
        out_shape=[
            pltpu.VMEM(adjoint.shape, F32),
            pltpu.VMEM((GROUPS * ny * ROWS, nz), F32),
        ],
        scratch_shapes=[pltpu.VMEM((LB * nx * ny, nz), F32)],
        compiler_params=SMALL,
        cost_estimate=pl.CostEstimate(flops=20 * 10**6, bytes_accessed=7 * 10**6, transcendentals=0),
        name="local",
    )(diffusivity, conduct, adjoint, chem, spread, near, low, high, coef, ends)


def chain_kernel(in_ref, out_ref):
    count, _, nz = in_ref.shape
    h, mass, rhs, ends = [], [], [], []
    passed_m = passed_b = None
    for i in range(count):
        low, high = in_ref[i, 0:8, :], in_ref[i, 8:16, :]
        g = jnp.broadcast_to(in_ref[i, 6:7, :], (8, nz))
        m_f = jnp.broadcast_to(in_ref[i, 7:8, :], (8, nz))
        face = jnp.broadcast_to(in_ref[i, 14:15, :], (8, nz))
        m_l = jnp.broadcast_to(in_ref[i, 15:16, :], (8, nz))
        inv = 1.0 / (g + face + m_l)
        a, c = g * inv, face * inv
        m, b = m_f + a * m_l, low + a * high
        if i > 0:
            m, b = m + passed_m, b + passed_b
        passed_m, passed_b = c * m_l, c * high
        h.append(a * face)
        mass.append(m)
        rhs.append(b)
        ends.append((a, c, high * inv))
    half = count // 2
    scale, ratio = [None] * count, [None] * count
    for i in range(half - 1):
        inv = 1.0 / (mass[i] + h[i])
        q = h[i] * inv
        scale[i], ratio[i] = rhs[i] * inv, q
        mass[i + 1] = mass[i + 1] + q * mass[i]
        rhs[i + 1] = rhs[i + 1] + q * rhs[i]
    mass[count - 1] = mass[count - 1] + h[count - 1]
    for i in range(count - 1, half, -1):
        inv = 1.0 / (mass[i] + h[i - 1])
        q = h[i - 1] * inv
        scale[i], ratio[i] = rhs[i] * inv, q
        mass[i - 1] = mass[i - 1] + q * mass[i]
        rhs[i - 1] = rhs[i - 1] + q * rhs[i]
    inv = 1.0 / (mass[half - 1] + h[half - 1])
    q = h[half - 1] * inv
    first = [None] * (count + 1)
    first[half] = (rhs[half] + q * rhs[half - 1]) / (mass[half] + q * mass[half - 1])
    first[half - 1] = rhs[half - 1] * inv + q * first[half]
    for i in range(half - 2, -1, -1):
        first[i] = scale[i] + ratio[i] * first[i + 1]
    for i in range(half + 1, count):
        first[i] = scale[i] + ratio[i] * first[i - 1]
    for i in range(count):
        a, c, part = ends[i]
        last = part + a * first[i]
        if i < count - 1:
            last = last + c * first[i + 1]
        out_ref[i, 0] = first[i][0:4]
        out_ref[i, 1, 0:2] = first[i][4:6]
        out_ref[i, 1, 2:4] = last[0:2]
        out_ref[i, 2] = last[2:6]


def chain(message):
    return pl.pallas_call(
        chain_kernel,
        in_specs=[WHOLE],
        out_specs=WHOLE,
        out_shape=pltpu.VMEM((message.shape[0], 3, 4, message.shape[2]), F32),
        compiler_params=SMALL,
        cost_estimate=pl.CostEstimate(flops=10**6, bytes_accessed=10**6, transcendentals=0),
        name="chain",
    )(message)


def back_kernel(coef_ref, got_ref, part_ref, out_hbm, ends_ref, out_ref, out_sem):
    carried, nx, ny, _ = part_ref.shape
    groups = carried // SB
    for i in range(got_ref.shape[0]):
        top = i * ROWS
        ends_ref[top : top + 4, :] = got_ref[i, 0]
        ends_ref[top + 4 : top + 6, :] = got_ref[i, 1, 0:2]
        ends_ref[top + 8 : top + 10, :] = got_ref[i, 1, 2:4]
        ends_ref[top + 10 : top + 14, :] = got_ref[i, 2]

    def put(g):
        return pltpu.make_async_copy(out_ref.at[pl.ds(g * SB, SB)], out_hbm.at[pl.ds(g * SB, SB)], out_sem.at[g])

    @pl.loop(0, groups)
    def _(g):
        for t in range(SB):
            s = g * SB + t
            first = ends_ref[pl.ds(place(s), ny, stride=GROUPS * ROWS), :]
            value = ends_ref[pl.ds(place(s) + 8, ny, stride=GROUPS * ROWS), :]
            out_ref[s, 0] = first
            out_ref[s, nx - 1] = value
            for p in range(nx - 2, 0, -1):
                value = part_ref[s, p] + coef_ref[0, p] * first + coef_ref[1, p] * value
                out_ref[s, p] = value
        put(g).start()

    @pl.loop(0, groups)
    def _(g):
        put(g).wait()


def back(part, coef, ends):
    groups = part.shape[0] // SB
    return pl.pallas_call(
        back_kernel,
        in_specs=[WHOLE, WHOLE, WHOLE],
        out_specs=ANY,
        out_shape=jax.ShapeDtypeStruct(part.shape, F32),
        scratch_shapes=[
            pltpu.VMEM((ends.shape[0] * ROWS, part.shape[3]), F32),
            pltpu.VMEM(part.shape, F32),
            pltpu.SemaphoreType.DMA((groups,)),
        ],
        compiler_params=SMALL,
        cost_estimate=pl.CostEstimate(flops=2 * 10**6, bytes_accessed=3 * 10**6, transcendentals=0),
        name="back",
    )(coef, ends, part)


def shards(
    adjoint, log_conc, levels, conduct, orders_fwd, orders_rev, stoich, rate_fwd, rate_rev, diffusivity
):
    carried, nx, ny, nz = adjoint.shape
    rows_y, blocks = lax.axis_size("gy"), lax.axis_size("gx")
    near = lax.ppermute(adjoint, "gz", [(0, 1), (1, 0)])
    tail, head = edges(adjoint)
    low = lax.ppermute(tail, "gy", [(i, (i + 1) % rows_y) for i in range(rows_y)])
    high = lax.ppermute(head, "gy", [((i + 1) % rows_y, i) for i in range(rows_y)])
    chem, spread, coef, ends_m = chemistry(
        adjoint, log_conc, levels, conduct, orders_fwd, orders_rev, stoich, rate_fwd, rate_rev
    )
    part, message = local_part(diffusivity, adjoint, chem, spread, near, low, high, conduct, coef, ends_m)
    message = lax.all_to_all(message.reshape(blocks, ROWS, nz), "gx", 0, 0, tiled=True)
    ends = lax.all_to_all(chain(message), "gx", 0, 0, tiled=True)
    return back(part, coef, ends)


def solution(mesh):
    cells = P(None, "gx", "gy", "gz")
    planes = P("gx", "gy", "gz")
    in_specs = (cells, cells, planes, planes, P(), P(), P(), P(), P(), P())
    return jax.shard_map(shards, mesh=mesh, in_specs=in_specs, out_specs=cells, check_vma=False)
```

```python
import jax
import jax.numpy as jnp
from jax import lax
from jax.experimental import pallas as pl
from jax.experimental.pallas import tpu as pltpu
from jax.sharding import PartitionSpec as P

SECTION = 0.02
STEP = 0.3
MASS = 0.001
THIRD = MASS / 3.0
BODY = MASS + 2.0 * THIRD
OFF = -1024.0

K_ROWS = 64
R_PAD = 208
STRIP = 16
CHUNKS = tuple((start, STRIP) for start in range(0, R_PAD, STRIP))
TILE = 4096
XB = 4
LIMIT = 24 * 1024 * 1024
F32 = jnp.float32
BF16 = jnp.bfloat16


def iota(shape, dim):
    return lax.broadcasted_iota(jnp.int32, shape, dim)


def dot(a, b):
    return lax.dot_general(a, b, (((1,), (0,)), ((), ())), preferred_element_type=F32)


def dot_nt(a, b):
    return lax.dot_general(a, b, (((1,), (1,)), ((), ())), preferred_element_type=F32)


def one_hot(mask):
    return jnp.where(mask, 1.0, 0.0).astype(BF16)


def build_weights(of_ref, or_ref, st_ref, rf_ref, rr_ref, wide_ref, w_ref, c_ref):
    species, react = of_ref.shape
    carried = st_ref.shape[0]
    eye = one_hot(iota((R_PAD, 256), 0) == iota((R_PAD, 256), 1))
    pick_row, pick_col = iota((32, 32), 0), iota((32, 32), 1)
    pick = one_hot(pick_col == jnp.where(
        pick_row < 16, pick_row, jnp.where(pick_row < 24, pick_row - 2, -1)
    ))
    sub, tier = iota((8, 256), 0), 4 * iota((8, 256), 1) // react
    full = []
    for index, (orders, rate) in enumerate(((of_ref, rf_ref), (or_ref, rr_ref))):
        wide_ref[...] = jnp.zeros(wide_ref.shape, F32)
        wide_ref[0:species, 0:react] = orders[...].astype(F32)
        plain = wide_ref[0:32, :]
        sign = 1.0 if index == 0 else -1.0
        c_ref[index] = (sign * dot(pick, plain.astype(BF16)))[:, 0:R_PAD].astype(BF16)
        wide_ref[56:57, 0:react] = jnp.log(rate[...])
        r = jnp.broadcast_to(wide_ref[56:57, :], (8, 256))
        r0 = r.astype(BF16).astype(F32)
        r1 = (r - r0).astype(BF16).astype(F32)
        parts = jnp.where(sub == 3, r0, jnp.where(sub == 4, r1, jnp.where(sub == 5, r - r0 - r1, 0.0)))
        wide_ref[56:64, :] = jnp.where(sub < 3, jnp.where(tier > sub, OFF, 0.0), parts)
        full.append(dot_nt(eye, wide_ref[...].astype(BF16)).astype(BF16))
    wide_ref[...] = jnp.zeros(wide_ref.shape, F32)
    wide_ref[32:48, 0:react] = st_ref[0:16, :].astype(F32)
    wide_ref[50 : 34 + carried, 0:react] = st_ref[16:carried, :].astype(F32)
    full.append(dot_nt(eye, wide_ref[...].astype(BF16)).astype(BF16))
    base = 0
    for start, size in CHUNKS:
        for part in full:
            w_ref[base : base + size, :] = part[start : start + size]
            base += size


def chem_kernel(
    adj_ref, conc_ref, lev_ref, cond_ref, of_ref, or_ref, st_ref, rf_ref, rr_ref,
    out_ref, coef_ref, tail_ref,
    wide_ref, w_ref, c_ref, conc32_ref, x_ref, act_ref, run_ref,
):
    step = pl.program_id(0)

    @pl.when(step == 0)
    def _():
        run_ref[0] = cond_ref[0] - THIRD
        run_ref[1] = jnp.where(lax.axis_index("gx") == 0, MASS + THIRD, BODY) * jnp.ones(run_ref.shape[1:], F32)
        run_ref[2] = jnp.full(run_ref.shape[1:], BODY, F32)
        build_weights(of_ref, or_ref, st_ref, rf_ref, rr_ref, wide_ref, w_ref, c_ref)

    gap, mass_first, mass = run_ref[0], run_ref[1], run_ref[2]
    for q in range(1, XB + 1):
        p = step * XB + q
        after = cond_ref[jnp.minimum(p, cond_ref.shape[0] - 1)] - THIRD
        inv = 1.0 / (gap + after + mass)
        alpha, beta = gap * inv, after * inv
        coef_ref[0, p], coef_ref[1, p], coef_ref[2, p] = alpha, beta, inv
        mass_first = mass_first + alpha * mass
        mass = BODY + beta * mass
        gap = alpha * after
        tail_ref[p, 0], tail_ref[p, 1], tail_ref[p, 2] = gap, mass_first, mass
    run_ref[0], run_ref[1], run_ref[2] = gap, mass_first, mass

    carried, xb, ny, nz = adj_ref.shape
    species = conc_ref.shape[0]
    adj_rows = adj_ref.reshape(carried * xb * ny, nz)
    out_rows = out_ref.reshape(carried * xb * ny, nz)
    pitch = xb * ny
    conc32_ref[...] = conc_ref[...].astype(F32).reshape(species * pitch, nz)
    sub = iota((8, nz), 0)
    for x in range(xb):
        for y in range(ny):
            row = x * ny + y
            cols = slice(row * nz, (row + 1) * nz)
            conc = jnp.concatenate(
                [conc32_ref[pl.ds(row + 8 * q * pitch, 8, stride=pitch), :] for q in range(4)], axis=0
            ).astype(BF16)
            x_ref[0:32, cols] = conc
            lam = [adj_rows[pl.ds(row + first * pitch, 8, stride=pitch), :] for first in (0, 8, carried - 8)]
            level = jnp.broadcast_to(lev_ref[x, y : y + 1, :], (8, nz))
            marks = jnp.where(level <= sub, 1.0, 0.0)
            x_ref[32:64, cols] = jnp.concatenate(lam + [marks], axis=0).astype(BF16)
    per_tile = TILE // nz
    for tile in range(xb * ny // per_tile):
        slot = tile % act_ref.shape[0]
        every = dot(w_ref[...], x_ref[:, tile * TILE : (tile + 1) * TILE])
        for start, size in CHUNKS:
            got = every[3 * start : 3 * (start + size)]
            weight = got[2 * size :]
            act_ref[slot, 0, start : start + size, :] = (jnp.exp(got[:size]) * weight).astype(BF16)
            act_ref[slot, 1, start : start + size, :] = (jnp.exp(got[size : 2 * size]) * weight).astype(BF16)
        chem = dot(c_ref[0], act_ref[slot, 0]) + dot(c_ref[1], act_ref[slot, 1])
        for part in range(per_tile):
            row = tile * per_tile + part
            for q, first in enumerate((0, 8, carried - 8)):
                out_rows[pl.ds(row + first * pitch, 8, stride=pitch), :] = chem[
                    8 * q : 8 * q + 8, part * nz : (part + 1) * nz
                ]


def chemistry(adjoint, log_conc, levels, conduct, orders_fwd, orders_rev, stoich, rate_fwd, rate_rev):
    carried, nx, ny, nz = adjoint.shape
    species, react = log_conc.shape[0], orders_fwd.shape[0]
    whole = lambda a: pl.BlockSpec(a.shape, lambda i: (0,) * len(a.shape))
    small = [orders_fwd.T, orders_rev.T, stoich.T, rate_fwd.reshape(1, react), rate_rev.reshape(1, react)]
    return pl.pallas_call(
        chem_kernel,
        grid=(nx // XB,),
        in_specs=[
            pl.BlockSpec((carried, XB, ny, nz), lambda i: (0, i, 0, 0)),
            pl.BlockSpec((species, XB, ny, nz), lambda i: (0, i, 0, 0)),
            pl.BlockSpec((XB, ny, nz), lambda i: (i, 0, 0)),
            whole(conduct),
        ]
        + [whole(a) for a in small],
        out_specs=[
            pl.BlockSpec((carried, XB, ny, nz), lambda i: (0, i, 0, 0)),
            pl.BlockSpec((3, nx + 1, ny, nz), lambda i: (0, 0, 0, 0)),
            pl.BlockSpec((nx + 1, 3, ny, nz), lambda i: (0, 0, 0, 0)),
        ],
        out_shape=[
            jax.ShapeDtypeStruct(adjoint.shape, F32),
            jax.ShapeDtypeStruct((3, nx + 1, ny, nz), F32),
            jax.ShapeDtypeStruct((nx + 1, 3, ny, nz), F32),
        ],
        scratch_shapes=[
            pltpu.VMEM((K_ROWS, 256), F32),
            pltpu.VMEM((3 * R_PAD, K_ROWS), BF16),
            pltpu.VMEM((2, 32, R_PAD), BF16),
            pltpu.VMEM((species * XB * ny, nz), F32),
            pltpu.VMEM((K_ROWS, XB * ny * nz), BF16),
            pltpu.VMEM((1, 2, R_PAD, TILE), BF16),
            pltpu.VMEM((3, ny, nz), F32),
        ],
        compiler_params=pltpu.CompilerParams(dimension_semantics=("arbitrary",), vmem_limit_bytes=LIMIT),
        cost_estimate=pl.CostEstimate(flops=12 * 10**9, bytes_accessed=4 * 10**6, transcendentals=6_750_000),
        name="chem",
    )(adjoint, log_conc, levels, conduct, *small)


GROUP = 6
GROUPS = 4
ROWS = 16
SB = 2
LB = 11
ANY = pl.BlockSpec(memory_space=pl.ANY)
WHOLE = pl.BlockSpec(memory_space=pltpu.VMEM)
SMALL = pltpu.CompilerParams(vmem_limit_bytes=LIMIT)


def place(s):
    return s // GROUP * ROWS + s % GROUP


def crossing(adj_ref, s):
    carried, nx, ny, nz = adj_ref.shape
    rows = adj_ref.reshape(carried * nx * ny, nz)
    f0, f1, f6, f7 = [rows[pl.ds(s * nx * ny + r, nx, stride=ny), :] for r in (0, 1, ny - 2, ny - 1)]
    return (16.0 * f7 - f6, -f7), (-f0, 16.0 * f0 - f1)


def edges_kernel(adj_ref, low_ref, high_ref):
    carried, nx, ny, nz = adj_ref.shape
    mine = lax.axis_index("gy")
    to_high = jnp.where(mine == lax.axis_size("gy") - 1, 0.0, 1.0)
    to_low = jnp.where(mine == 0, 0.0, 1.0)

    @pl.loop(0, carried)
    def _(s):
        down, up = crossing(adj_ref, s)
        for k in range(2):
            low_ref[s, k] = down[k] * to_high
            high_ref[s, k] = up[k] * to_low


def edges(adjoint):
    carried, nx, ny, nz = adjoint.shape
    shape = pltpu.VMEM((carried, 2, nx, nz), F32)
    return pl.pallas_call(
        edges_kernel,
        in_specs=[WHOLE],
        out_specs=[WHOLE, WHOLE],
        out_shape=[shape, shape],
        compiler_params=SMALL,
        cost_estimate=pl.CostEstimate(flops=0, bytes_accessed=2 * 10**6, transcendentals=0),
        name="edges",
    )(adjoint)


def local_kernel(
    diff_ref, cond_ref, adj_ref, chem_ref, near_ref, low_ref, high_ref, coef_ref, tail_ref,
    part_ref, msg_ref, add_ref,
):
    nx, ny, nz = cond_ref.shape
    carried = adj_ref.shape[0]
    stride = GROUPS * ROWS
    msg_ref[...] = jnp.zeros(msg_ref.shape, F32)
    at = nx - 2
    face = cond_ref[nx - 1] - THIRD
    for group in range(GROUPS):
        for r, value in ((6, tail_ref[at, 0]), (7, tail_ref[at, 1]), (14, face), (15, tail_ref[at, 2])):
            msg_ref[pl.ds(group * ROWS + r, ny, stride=stride), :] = value

    add_ref[...] = jnp.zeros(add_ref.shape, F32)
    lane = iota((ny, nz), 1)
    keep_low = jnp.where(lax.axis_index("gz") == 0, 1.0, 0.0)
    keep_high = 1.0 - keep_low

    @pl.loop(0, carried // LB)
    def _(g):
        for t in range(LB):
            s = g * LB + t
            down, up = crossing(adj_ref, s)
            for r, own_term, got in (
                (0, down[0], low_ref[s, 0]),
                (1, down[1], low_ref[s, 1]),
                (ny - 2, up[0], high_ref[s, 0]),
                (ny - 1, up[1], high_ref[s, 1]),
            ):
                add_ref[pl.ds(t * nx * ny + r, nx, stride=ny), :] = got - own_term
        for t in range(LB):
            s = g * LB + t
            scale = diff_ref[s] * (SECTION * STEP / 12.0)
            b_first, carry = None, None
            for p in range(nx):
                own, near = adj_ref[s, p], near_ref[s, p]
                above, below = near * keep_low, near * keep_high
                close = pltpu.roll(own, ny - 1, 0) + pltpu.roll(own, 1, 0)
                close = close + pltpu.roll(jnp.where(lane < 1, above, own), nz - 1, 1)
                close = close + pltpu.roll(jnp.where(lane >= nz - 1, below, own), 1, 1)
                far = pltpu.roll(own, ny - 2, 0) + pltpu.roll(own, 2, 0)
                far = far + pltpu.roll(jnp.where(lane < 2, above, own), nz - 2, 1)
                far = far + pltpu.roll(jnp.where(lane >= nz - 2, below, own), 2, 1)
                at = (t * nx + p) * ny
                spread = 16.0 * close - far - 60.0 * own + add_ref[at : at + ny, :]
                b = SECTION * own + (SECTION * STEP) * chem_ref[s, p] + scale * spread
                if p == 0:
                    b_first = b
                elif p < nx - 1:
                    full = b if carry is None else b + carry
                    part_ref[s, p] = full * coef_ref[2, p]
                    b_first = b_first + coef_ref[0, p] * full
                    carry = coef_ref[1, p] * full
                else:
                    b_last = b + carry
            msg_ref[pl.ds(place(s), ny, stride=stride), :] = b_first
            msg_ref[pl.ds(place(s) + 8, ny, stride=stride), :] = b_last


def local_part(diffusivity, adjoint, chem, near, low, high, conduct, coef, ends):
    carried, nx, ny, nz = adjoint.shape
    smem = pl.BlockSpec(memory_space=pltpu.SMEM)
    return pl.pallas_call(
        local_kernel,
        in_specs=[smem] + [WHOLE] * 8,
        out_specs=[WHOLE] * 2,
        out_shape=[
            pltpu.VMEM(adjoint.shape, F32),
            pltpu.VMEM((GROUPS * ny * ROWS, nz), F32),
        ],
        scratch_shapes=[pltpu.VMEM((LB * nx * ny, nz), F32)],
        compiler_params=SMALL,
        cost_estimate=pl.CostEstimate(flops=20 * 10**6, bytes_accessed=7 * 10**6, transcendentals=0),
        name="local",
    )(diffusivity, conduct, adjoint, chem, near, low, high, coef, ends)


def chain_kernel(in_ref, out_ref):
    count, _, nz = in_ref.shape
    h, mass, rhs, ends = [], [], [], []
    passed_m = passed_b = None
    for i in range(count):
        low, high = in_ref[i, 0:8, :], in_ref[i, 8:16, :]
        g = jnp.broadcast_to(in_ref[i, 6:7, :], (8, nz))
        m_f = jnp.broadcast_to(in_ref[i, 7:8, :], (8, nz))
        face = jnp.broadcast_to(in_ref[i, 14:15, :], (8, nz))
        m_l = jnp.broadcast_to(in_ref[i, 15:16, :], (8, nz))
        inv = 1.0 / (g + face + m_l)
        a, c = g * inv, face * inv
        m, b = m_f + a * m_l, low + a * high
        if i > 0:
            m, b = m + passed_m, b + passed_b
        passed_m, passed_b = c * m_l, c * high
        h.append(a * face)
        mass.append(m)
        rhs.append(b)
        ends.append((a, c, high * inv))
    half = count // 2
    scale, ratio = [None] * count, [None] * count
    for i in range(half - 1):
        inv = 1.0 / (mass[i] + h[i])
        q = h[i] * inv
        scale[i], ratio[i] = rhs[i] * inv, q
        mass[i + 1] = mass[i + 1] + q * mass[i]
        rhs[i + 1] = rhs[i + 1] + q * rhs[i]
    mass[count - 1] = mass[count - 1] + h[count - 1]
    for i in range(count - 1, half, -1):
        inv = 1.0 / (mass[i] + h[i - 1])
        q = h[i - 1] * inv
        scale[i], ratio[i] = rhs[i] * inv, q
        mass[i - 1] = mass[i - 1] + q * mass[i]
        rhs[i - 1] = rhs[i - 1] + q * rhs[i]
    inv = 1.0 / (mass[half - 1] + h[half - 1])
    q = h[half - 1] * inv
    first = [None] * (count + 1)
    first[half] = (rhs[half] + q * rhs[half - 1]) / (mass[half] + q * mass[half - 1])
    first[half - 1] = rhs[half - 1] * inv + q * first[half]
    for i in range(half - 2, -1, -1):
        first[i] = scale[i] + ratio[i] * first[i + 1]
    for i in range(half + 1, count):
        first[i] = scale[i] + ratio[i] * first[i - 1]
    for i in range(count):
        a, c, part = ends[i]
        last = part + a * first[i]
        if i < count - 1:
            last = last + c * first[i + 1]
        out_ref[i, 0] = first[i][0:4]
        out_ref[i, 1, 0:2] = first[i][4:6]
        out_ref[i, 1, 2:4] = last[0:2]
        out_ref[i, 2] = last[2:6]


def chain(message):
    return pl.pallas_call(
        chain_kernel,
        in_specs=[WHOLE],
        out_specs=WHOLE,
        out_shape=pltpu.VMEM((message.shape[0], 3, 4, message.shape[2]), F32),
        compiler_params=SMALL,
        cost_estimate=pl.CostEstimate(flops=10**6, bytes_accessed=10**6, transcendentals=0),
        name="chain",
    )(message)


def back_kernel(coef_ref, got_ref, part_ref, out_hbm, ends_ref, out_ref, out_sem):
    carried, nx, ny, _ = part_ref.shape
    groups = carried // SB
    for i in range(got_ref.shape[0]):
        top = i * ROWS
        ends_ref[top : top + 4, :] = got_ref[i, 0]
        ends_ref[top + 4 : top + 6, :] = got_ref[i, 1, 0:2]
        ends_ref[top + 8 : top + 10, :] = got_ref[i, 1, 2:4]
        ends_ref[top + 10 : top + 14, :] = got_ref[i, 2]

    def put(g):
        return pltpu.make_async_copy(out_ref.at[pl.ds(g * SB, SB)], out_hbm.at[pl.ds(g * SB, SB)], out_sem.at[g])

    @pl.loop(0, groups)
    def _(g):
        for t in range(SB):
            s = g * SB + t
            first = ends_ref[pl.ds(place(s), ny, stride=GROUPS * ROWS), :]
            value = ends_ref[pl.ds(place(s) + 8, ny, stride=GROUPS * ROWS), :]
            out_ref[s, 0] = first
            out_ref[s, nx - 1] = value
            for p in range(nx - 2, 0, -1):
                value = part_ref[s, p] + coef_ref[0, p] * first + coef_ref[1, p] * value
                out_ref[s, p] = value
        put(g).start()

    @pl.loop(0, groups)
    def _(g):
        put(g).wait()


def back(part, coef, ends):
    groups = part.shape[0] // SB
    return pl.pallas_call(
        back_kernel,
        in_specs=[WHOLE, WHOLE, WHOLE],
        out_specs=ANY,
        out_shape=jax.ShapeDtypeStruct(part.shape, F32),
        scratch_shapes=[
            pltpu.VMEM((ends.shape[0] * ROWS, part.shape[3]), F32),
            pltpu.VMEM(part.shape, F32),
            pltpu.SemaphoreType.DMA((groups,)),
        ],
        compiler_params=SMALL,
        cost_estimate=pl.CostEstimate(flops=2 * 10**6, bytes_accessed=3 * 10**6, transcendentals=0),
        name="back",
    )(coef, ends, part)


def shards(
    adjoint, log_conc, levels, conduct, orders_fwd, orders_rev, stoich, rate_fwd, rate_rev, diffusivity
):
    carried, nx, ny, nz = adjoint.shape
    rows_y, blocks = lax.axis_size("gy"), lax.axis_size("gx")
    near = lax.ppermute(adjoint, "gz", [(0, 1), (1, 0)])
    tail, head = edges(adjoint)
    low = lax.ppermute(tail, "gy", [(i, (i + 1) % rows_y) for i in range(rows_y)])
    high = lax.ppermute(head, "gy", [((i + 1) % rows_y, i) for i in range(rows_y)])
    chem, coef, ends_m = chemistry(
        adjoint, log_conc, levels, conduct, orders_fwd, orders_rev, stoich, rate_fwd, rate_rev
    )
    part, message = local_part(diffusivity, adjoint, chem, near, low, high, conduct, coef, ends_m)
    message = lax.all_to_all(message.reshape(blocks, ROWS, nz), "gx", 0, 0, tiled=True)
    ends = lax.all_to_all(chain(message), "gx", 0, 0, tiled=True)
    return back(part, coef, ends)


def solution(mesh):
    cells = P(None, "gx", "gy", "gz")
    planes = P("gx", "gy", "gz")
    in_specs = (cells, cells, planes, planes, P(), P(), P(), P(), P(), P())
    return jax.shard_map(shards, mesh=mesh, in_specs=in_specs, out_specs=cells, check_vma=False)
```

```python
import math

import jax
import jax.numpy as jnp
from jax import lax
from jax.experimental import pallas as pl
from jax.experimental.pallas import tpu as pltpu
from jax.sharding import PartitionSpec as P

SECTION = 0.02
STEP = 0.3
MASS = 0.001
THIRD = MASS / 3.0
BODY = MASS + 2.0 * THIRD
LOG2E = math.log2(math.e)
OFF = -1024.0

K_ROWS = 96
R_PAD = 208
STRIP = 16
CHUNKS = tuple((start, STRIP) for start in range(0, R_PAD, STRIP))
XB = 4
LIMIT = 24 * 1024 * 1024
F32 = jnp.float32
BF16 = jnp.bfloat16


ANY = pl.BlockSpec(memory_space=pl.ANY)
WHOLE = pl.BlockSpec(memory_space=pltpu.VMEM)
SMALL = pltpu.CompilerParams(vmem_limit_bytes=LIMIT)


def iota(shape, dim):
    return lax.broadcasted_iota(jnp.int32, shape, dim)


def dot(a, b):
    return lax.dot_general(a, b, (((1,), (0,)), ((), ())), preferred_element_type=F32)


def dot_nt(a, b):
    return lax.dot_general(a, b, (((1,), (1,)), ((), ())), preferred_element_type=F32)


def one_hot(mask):
    return jnp.where(mask, 1.0, 0.0).astype(BF16)


def build_weights(of_ref, or_ref, st_ref, rf_ref, rr_ref, wide_ref, w_ref, c_ref):
    species, react = of_ref.shape
    carried = st_ref.shape[0]
    eye = one_hot(iota((R_PAD, 256), 0) == iota((R_PAD, 256), 1))
    pick_row, pick_col = iota((32, 32), 0), iota((32, 32), 1)
    pick = one_hot(pick_col == jnp.where(pick_row < 16, pick_row, jnp.where(pick_row < 24, pick_row - 2, -1)))
    sub, tier = iota((8, 256), 0), 4 * iota((8, 256), 1) // react
    full = []
    for index, (orders, rate) in enumerate(((of_ref, rf_ref), (or_ref, rr_ref))):
        wide_ref[...] = jnp.zeros(wide_ref.shape, F32)
        wide_ref[0:species, 0:react] = orders[...].astype(F32)
        plain = wide_ref[0:32, :]
        sign = 1.0 if index == 0 else -1.0
        c_ref[index] = (sign * dot(pick, plain.astype(BF16)))[:, 0:R_PAD].astype(BF16)
        scaled = plain * LOG2E
        hi = scaled.astype(BF16).astype(F32)
        wide_ref[0:32, :] = hi
        wide_ref[32:64, :] = scaled - hi
        wide_ref[88:89, 0:react] = jnp.log(rate[...]) * LOG2E
        r = jnp.broadcast_to(wide_ref[88:89, :], (8, 256))
        r0 = r.astype(BF16).astype(F32)
        r1 = (r - r0).astype(BF16).astype(F32)
        parts = jnp.where(sub == 3, r0, jnp.where(sub == 4, r1, jnp.where(sub == 5, r - r0 - r1, 0.0)))
        wide_ref[88:96, :] = jnp.where(sub < 3, jnp.where(tier > sub, OFF, 0.0), parts)
        full.append(dot_nt(eye, wide_ref[...].astype(BF16)).astype(BF16))
    wide_ref[...] = jnp.zeros(wide_ref.shape, F32)
    wide_ref[64:80, 0:react] = st_ref[0:16, :].astype(F32)
    wide_ref[82 : 66 + carried, 0:react] = st_ref[16:carried, :].astype(F32)
    full.append(dot_nt(eye, wide_ref[...].astype(BF16)).astype(BF16))
    base = 0
    for start, size in CHUNKS:
        for part in full:
            w_ref[base : base + size, :] = part[start : start + size]
            base += size


def chem_kernel(
    adj_ref, conc_ref, lev_ref, cond_ref, of_ref, or_ref, st_ref, rf_ref, rr_ref,
    out_ref, coef_ref, tail_ref,
    wide_ref, w_ref, c_ref, conc32_ref, x_ref, act_ref, run_ref,
):
    run_ref[0] = cond_ref[0] - THIRD
    run_ref[1] = jnp.where(lax.axis_index("gx") == 0, MASS + THIRD, BODY) * jnp.ones(run_ref.shape[1:], F32)
    run_ref[2] = jnp.full(run_ref.shape[1:], BODY, F32)
    build_weights(of_ref, or_ref, st_ref, rf_ref, rr_ref, wide_ref, w_ref, c_ref)

    carried, nx, ny, nz = adj_ref.shape
    species = conc_ref.shape[0]
    pitch = nx * ny
    adj_rows = adj_ref.reshape(carried * pitch, nz)
    out_rows = out_ref.reshape(carried * pitch, nz)
    sub = iota((8, nz), 0)

    @pl.loop(0, nx // XB)
    def _(step):
        gap, mass_first, mass = run_ref[0], run_ref[1], run_ref[2]
        for q in range(1, XB + 1):
            p = step * XB + q
            after = cond_ref[jnp.minimum(p, nx - 1)] - THIRD
            inv = 1.0 / (gap + after + mass)
            alpha, beta = gap * inv, after * inv
            coef_ref[0, p], coef_ref[1, p], coef_ref[2, p] = alpha, beta, inv
            mass_first = mass_first + alpha * mass
            mass = BODY + beta * mass
            gap = alpha * after
            tail_ref[p, 0], tail_ref[p, 1], tail_ref[p, 2] = gap, mass_first, mass
        run_ref[0], run_ref[1], run_ref[2] = gap, mass_first, mass

        conc32_ref[...] = conc_ref[:, pl.ds(step * XB, XB)].astype(F32).reshape(species * XB * ny, nz)
        base = step * XB * ny
        for x in range(XB):
            for y in range(ny):
                row = x * ny + y
                cols = slice(row * nz, (row + 1) * nz)
                conc = jnp.concatenate(
                    [conc32_ref[pl.ds(row + 8 * q * XB * ny, 8, stride=XB * ny), :] for q in range(4)], axis=0
                ).astype(BF16)
                x_ref[0:32, cols] = conc
                x_ref[32:64, cols] = conc
                lam = [
                    adj_rows[pl.ds(base + row + first * pitch, 8, stride=pitch), :] for first in (0, 8, carried - 8)
                ]
                level = jnp.broadcast_to(lev_ref[step * XB + x, y : y + 1, :], (8, nz))
                marks = jnp.where(level <= sub, 1.0, 0.0)
                x_ref[64:96, cols] = jnp.concatenate(lam + [marks], axis=0).astype(BF16)
        every = dot(w_ref[...], x_ref[...])
        for start, size in CHUNKS:
            got = every[3 * start : 3 * (start + size)]
            weight = got[2 * size :]
            act_ref[0, start : start + size, :] = (jnp.exp2(got[:size]) * weight).astype(BF16)
            act_ref[1, start : start + size, :] = (jnp.exp2(got[size : 2 * size]) * weight).astype(BF16)
        chem = dot(c_ref[0], act_ref[0]) + dot(c_ref[1], act_ref[1])
        for row in range(XB * ny):
            for q, first in enumerate((0, 8, carried - 8)):
                out_rows[pl.ds(base + row + first * pitch, 8, stride=pitch), :] = chem[
                    8 * q : 8 * q + 8, row * nz : (row + 1) * nz
                ]


def chemistry(adjoint, log_conc, levels, conduct, orders_fwd, orders_rev, stoich, rate_fwd, rate_rev):
    carried, nx, ny, nz = adjoint.shape
    species, react = log_conc.shape[0], orders_fwd.shape[0]
    small = [orders_fwd.T, orders_rev.T, stoich.T, rate_fwd.reshape(1, react), rate_rev.reshape(1, react)]
    return pl.pallas_call(
        chem_kernel,
        in_specs=[WHOLE] * 9,
        out_specs=[WHOLE] * 3,
        out_shape=[
            pltpu.VMEM(adjoint.shape, F32),
            pltpu.VMEM((3, nx + 1, ny, nz), F32),
            pltpu.VMEM((nx + 1, 3, ny, nz), F32),
        ],
        scratch_shapes=[
            pltpu.VMEM((K_ROWS, 256), F32),
            pltpu.VMEM((3 * R_PAD, K_ROWS), BF16),
            pltpu.VMEM((2, 32, R_PAD), BF16),
            pltpu.VMEM((species * XB * ny, nz), F32),
            pltpu.VMEM((K_ROWS, XB * ny * nz), BF16),
            pltpu.VMEM((2, R_PAD, XB * ny * nz), BF16),
            pltpu.VMEM((3, ny, nz), F32),
        ],
        compiler_params=SMALL,
        cost_estimate=pl.CostEstimate(flops=12 * 10**9, bytes_accessed=4 * 10**6, transcendentals=6_750_000),
        name="chem",
    )(adjoint, log_conc, levels, conduct, *small)


GROUP = 6
GROUPS = 4
ROWS = 16
SB = 2
LB = 11
def place(s):
    return s // GROUP * ROWS + s % GROUP


def crossing(adj_ref, s):
    carried, nx, ny, nz = adj_ref.shape
    rows = adj_ref.reshape(carried * nx * ny, nz)
    f0, f1, f6, f7 = [rows[pl.ds(s * nx * ny + r, nx, stride=ny), :] for r in (0, 1, ny - 2, ny - 1)]
    return (16.0 * f7 - f6, -f7), (-f0, 16.0 * f0 - f1)


def edges_kernel(adj_ref, low_ref, high_ref):
    carried, nx, ny, nz = adj_ref.shape
    mine = lax.axis_index("gy")
    to_high = jnp.where(mine == lax.axis_size("gy") - 1, 0.0, 1.0)
    to_low = jnp.where(mine == 0, 0.0, 1.0)

    @pl.loop(0, carried)
    def _(s):
        down, up = crossing(adj_ref, s)
        for k in range(2):
            low_ref[s, k] = down[k] * to_high
            high_ref[s, k] = up[k] * to_low


def edges(adjoint):
    carried, nx, ny, nz = adjoint.shape
    shape = pltpu.VMEM((carried, 2, nx, nz), F32)
    return pl.pallas_call(
        edges_kernel,
        in_specs=[WHOLE],
        out_specs=[WHOLE, WHOLE],
        out_shape=[shape, shape],
        compiler_params=SMALL,
        cost_estimate=pl.CostEstimate(flops=0, bytes_accessed=2 * 10**6, transcendentals=0),
        name="edges",
    )(adjoint)


def local_kernel(
    diff_ref, cond_ref, adj_ref, chem_ref, near_ref, low_ref, high_ref, coef_ref, tail_ref,
    part_ref, msg_ref, add_ref,
):
    nx, ny, nz = cond_ref.shape
    carried = adj_ref.shape[0]
    stride = GROUPS * ROWS
    msg_ref[...] = jnp.zeros(msg_ref.shape, F32)
    at = nx - 2
    face = cond_ref[nx - 1] - THIRD
    for group in range(GROUPS):
        for r, value in ((6, tail_ref[at, 0]), (7, tail_ref[at, 1]), (14, face), (15, tail_ref[at, 2])):
            msg_ref[pl.ds(group * ROWS + r, ny, stride=stride), :] = value

    add_ref[...] = jnp.zeros(add_ref.shape, F32)
    lane = iota((ny, nz), 1)
    keep_low = jnp.where(lax.axis_index("gz") == 0, 1.0, 0.0)
    keep_high = 1.0 - keep_low

    @pl.loop(0, carried // LB)
    def _(g):
        for t in range(LB):
            s = g * LB + t
            down, up = crossing(adj_ref, s)
            for r, own_term, got in (
                (0, down[0], low_ref[s, 0]),
                (1, down[1], low_ref[s, 1]),
                (ny - 2, up[0], high_ref[s, 0]),
                (ny - 1, up[1], high_ref[s, 1]),
            ):
                add_ref[pl.ds(t * nx * ny + r, nx, stride=ny), :] = got - own_term
        for t in range(LB):
            s = g * LB + t
            scale = diff_ref[s] * (SECTION * STEP / 12.0)
            b_first, carry = None, None
            for p in range(nx):
                own, near = adj_ref[s, p], near_ref[s, p]
                above, below = near * keep_low, near * keep_high
                close = pltpu.roll(own, ny - 1, 0) + pltpu.roll(own, 1, 0)
                close = close + pltpu.roll(jnp.where(lane < 1, above, own), nz - 1, 1)
                close = close + pltpu.roll(jnp.where(lane >= nz - 1, below, own), 1, 1)
                far = pltpu.roll(own, ny - 2, 0) + pltpu.roll(own, 2, 0)
                far = far + pltpu.roll(jnp.where(lane < 2, above, own), nz - 2, 1)
                far = far + pltpu.roll(jnp.where(lane >= nz - 2, below, own), 2, 1)
                at = (t * nx + p) * ny
                spread = 16.0 * close - far - 60.0 * own + add_ref[at : at + ny, :]
                b = SECTION * own + (SECTION * STEP) * chem_ref[s, p] + scale * spread
                if p == 0:
                    b_first = b
                elif p < nx - 1:
                    full = b if carry is None else b + carry
                    part_ref[s, p] = full * coef_ref[2, p]
                    b_first = b_first + coef_ref[0, p] * full
                    carry = coef_ref[1, p] * full
                else:
                    b_last = b + carry
            msg_ref[pl.ds(place(s), ny, stride=stride), :] = b_first
            msg_ref[pl.ds(place(s) + 8, ny, stride=stride), :] = b_last


def local_part(diffusivity, adjoint, chem, near, low, high, conduct, coef, ends):
    carried, nx, ny, nz = adjoint.shape
    smem = pl.BlockSpec(memory_space=pltpu.SMEM)
    return pl.pallas_call(
        local_kernel,
        in_specs=[smem] + [WHOLE] * 8,
        out_specs=[WHOLE] * 2,
        out_shape=[
            pltpu.VMEM(adjoint.shape, F32),
            pltpu.VMEM((GROUPS * ny * ROWS, nz), F32),
        ],
        scratch_shapes=[pltpu.VMEM((LB * nx * ny, nz), F32)],
        compiler_params=SMALL,
        cost_estimate=pl.CostEstimate(flops=20 * 10**6, bytes_accessed=7 * 10**6, transcendentals=0),
        name="local",
    )(diffusivity, conduct, adjoint, chem, near, low, high, coef, ends)


def chain_kernel(in_ref, out_ref):
    count, _, nz = in_ref.shape
    h, mass, rhs, ends = [], [], [], []
    passed_m = passed_b = None
    for i in range(count):
        low, high = in_ref[i, 0:8, :], in_ref[i, 8:16, :]
        g = jnp.broadcast_to(in_ref[i, 6:7, :], (8, nz))
        m_f = jnp.broadcast_to(in_ref[i, 7:8, :], (8, nz))
        face = jnp.broadcast_to(in_ref[i, 14:15, :], (8, nz))
        m_l = jnp.broadcast_to(in_ref[i, 15:16, :], (8, nz))
        inv = 1.0 / (g + face + m_l)
        a, c = g * inv, face * inv
        m, b = m_f + a * m_l, low + a * high
        if i > 0:
            m, b = m + passed_m, b + passed_b
        passed_m, passed_b = c * m_l, c * high
        h.append(a * face)
        mass.append(m)
        rhs.append(b)
        ends.append((a, c, high * inv))
    half = count // 2
    scale, ratio = [None] * count, [None] * count
    for i in range(half - 1):
        inv = 1.0 / (mass[i] + h[i])
        q = h[i] * inv
        scale[i], ratio[i] = rhs[i] * inv, q
        mass[i + 1] = mass[i + 1] + q * mass[i]
        rhs[i + 1] = rhs[i + 1] + q * rhs[i]
    mass[count - 1] = mass[count - 1] + h[count - 1]
    for i in range(count - 1, half, -1):
        inv = 1.0 / (mass[i] + h[i - 1])
        q = h[i - 1] * inv
        scale[i], ratio[i] = rhs[i] * inv, q
        mass[i - 1] = mass[i - 1] + q * mass[i]
        rhs[i - 1] = rhs[i - 1] + q * rhs[i]
    inv = 1.0 / (mass[half - 1] + h[half - 1])
    q = h[half - 1] * inv
    first = [None] * (count + 1)
    first[half] = (rhs[half] + q * rhs[half - 1]) / (mass[half] + q * mass[half - 1])
    first[half - 1] = rhs[half - 1] * inv + q * first[half]
    for i in range(half - 2, -1, -1):
        first[i] = scale[i] + ratio[i] * first[i + 1]
    for i in range(half + 1, count):
        first[i] = scale[i] + ratio[i] * first[i - 1]
    for i in range(count):
        a, c, part = ends[i]
        last = part + a * first[i]
        if i < count - 1:
            last = last + c * first[i + 1]
        out_ref[i, 0] = first[i][0:4]
        out_ref[i, 1, 0:2] = first[i][4:6]
        out_ref[i, 1, 2:4] = last[0:2]
        out_ref[i, 2] = last[2:6]


def chain(message):
    return pl.pallas_call(
        chain_kernel,
        in_specs=[WHOLE],
        out_specs=WHOLE,
        out_shape=pltpu.VMEM((message.shape[0], 3, 4, message.shape[2]), F32),
        compiler_params=SMALL,
        cost_estimate=pl.CostEstimate(flops=10**6, bytes_accessed=10**6, transcendentals=0),
        name="chain",
    )(message)


def back_kernel(coef_ref, got_ref, part_ref, out_hbm, ends_ref, out_ref, out_sem):
    carried, nx, ny, _ = part_ref.shape
    groups = carried // SB
    for i in range(got_ref.shape[0]):
        top = i * ROWS
        ends_ref[top : top + 4, :] = got_ref[i, 0]
        ends_ref[top + 4 : top + 6, :] = got_ref[i, 1, 0:2]
        ends_ref[top + 8 : top + 10, :] = got_ref[i, 1, 2:4]
        ends_ref[top + 10 : top + 14, :] = got_ref[i, 2]

    def put(g):
        return pltpu.make_async_copy(out_ref.at[pl.ds(g * SB, SB)], out_hbm.at[pl.ds(g * SB, SB)], out_sem.at[g])

    @pl.loop(0, groups)
    def _(g):
        for t in range(SB):
            s = g * SB + t
            first = ends_ref[pl.ds(place(s), ny, stride=GROUPS * ROWS), :]
            value = ends_ref[pl.ds(place(s) + 8, ny, stride=GROUPS * ROWS), :]
            out_ref[s, 0] = first
            out_ref[s, nx - 1] = value
            for p in range(nx - 2, 0, -1):
                value = part_ref[s, p] + coef_ref[0, p] * first + coef_ref[1, p] * value
                out_ref[s, p] = value
        @pl.when(g % 2 == 0)
        def _():
            put(g).start(priority=0)

        @pl.when(g % 2 == 1)
        def _():
            put(g).start(priority=1)

    @pl.loop(0, groups)
    def _(g):
        put(g).wait()


def back(part, coef, ends):
    groups = part.shape[0] // SB
    return pl.pallas_call(
        back_kernel,
        in_specs=[WHOLE, WHOLE, WHOLE],
        out_specs=ANY,
        out_shape=jax.ShapeDtypeStruct(part.shape, F32),
        scratch_shapes=[
            pltpu.VMEM((ends.shape[0] * ROWS, part.shape[3]), F32),
            pltpu.VMEM(part.shape, F32),
            pltpu.SemaphoreType.DMA((groups,)),
        ],
        compiler_params=SMALL,
        cost_estimate=pl.CostEstimate(flops=2 * 10**6, bytes_accessed=3 * 10**6, transcendentals=0),
        name="back",
    )(coef, ends, part)


def resident(value):
    return pltpu.with_memory_space_constraint(value, pltpu.VMEM)


def shards(
    adjoint, log_conc, levels, conduct, orders_fwd, orders_rev, stoich, rate_fwd, rate_rev, diffusivity
):
    carried, nx, ny, nz = adjoint.shape
    rows_y, blocks = lax.axis_size("gy"), lax.axis_size("gx")
    near = lax.ppermute(adjoint, "gz", [(0, 1), (1, 0)])
    tail, head = edges(adjoint)
    low = lax.ppermute(tail, "gy", [(i, (i + 1) % rows_y) for i in range(rows_y)])
    high = lax.ppermute(head, "gy", [((i + 1) % rows_y, i) for i in range(rows_y)])
    chem, coef, ends_m = chemistry(adjoint, log_conc, levels, conduct, orders_fwd, orders_rev, stoich, rate_fwd, rate_rev)
    part, message = local_part(diffusivity, adjoint, chem, near, low, high, conduct, coef, ends_m)
    message = lax.all_to_all(message.reshape(blocks, ROWS, nz), "gx", 0, 0, tiled=True)
    ends = lax.all_to_all(chain(message), "gx", 0, 0, tiled=True)
    return back(part, coef, ends)


def solution(mesh):
    cells = P(None, "gx", "gy", "gz")
    planes = P("gx", "gy", "gz")
    in_specs = (cells, cells, planes, planes, P(), P(), P(), P(), P(), P())
    return jax.shard_map(shards, mesh=mesh, in_specs=in_specs, out_specs=cells, check_vma=False)
```

```python
import math

import jax
import jax.numpy as jnp
from jax import lax
from jax.experimental import pallas as pl
from jax.experimental.pallas import tpu as pltpu
from jax.sharding import PartitionSpec as P

SECTION = 0.02
STEP = 0.3
MASS = 0.001
THIRD = MASS / 3.0
BODY = MASS + 2.0 * THIRD
LOG2E = math.log2(math.e)
OFF = -1024.0

K_ROWS = 96
R_PAD = 208
STRIP = 16
CHUNKS = tuple((start, STRIP) for start in range(0, R_PAD, STRIP))
XB = 4
LIMIT = 24 * 1024 * 1024
F32 = jnp.float32
BF16 = jnp.bfloat16


ANY = pl.BlockSpec(memory_space=pl.ANY)
WHOLE = pl.BlockSpec(memory_space=pltpu.VMEM)
SMALL = pltpu.CompilerParams(vmem_limit_bytes=LIMIT)


def iota(shape, dim):
    return lax.broadcasted_iota(jnp.int32, shape, dim)


def dot(a, b):
    return lax.dot_general(a, b, (((1,), (0,)), ((), ())), preferred_element_type=F32)


def dot_nt(a, b):
    return lax.dot_general(a, b, (((1,), (1,)), ((), ())), preferred_element_type=F32)


def one_hot(mask):
    return jnp.where(mask, 1.0, 0.0).astype(BF16)


def build_weights(of_ref, or_ref, st_ref, rf_ref, rr_ref, wide_ref, w_ref, c_ref):
    species, react = of_ref.shape
    carried = st_ref.shape[0]
    eye = one_hot(iota((R_PAD, 256), 0) == iota((R_PAD, 256), 1))
    pick_row, pick_col = iota((32, 32), 0), iota((32, 32), 1)
    pick = one_hot(pick_col == jnp.where(pick_row < 16, pick_row, jnp.where(pick_row < 24, pick_row - 2, -1)))
    sub, tier = iota((8, 256), 0), 4 * iota((8, 256), 1) // react
    full = []
    for index, (orders, rate) in enumerate(((of_ref, rf_ref), (or_ref, rr_ref))):
        wide_ref[...] = jnp.zeros(wide_ref.shape, F32)
        wide_ref[0:species, 0:react] = orders[...].astype(F32)
        plain = wide_ref[0:32, :]
        sign = 1.0 if index == 0 else -1.0
        c_ref[index] = (sign * dot(pick, plain.astype(BF16)))[:, 0:R_PAD].astype(BF16)
        scaled = plain * LOG2E
        hi = scaled.astype(BF16).astype(F32)
        wide_ref[0:32, :] = hi
        wide_ref[32:64, :] = scaled - hi
        wide_ref[88:89, 0:react] = jnp.log(rate[...]) * LOG2E
        r = jnp.broadcast_to(wide_ref[88:89, :], (8, 256))
        r0 = r.astype(BF16).astype(F32)
        r1 = (r - r0).astype(BF16).astype(F32)
        parts = jnp.where(sub == 3, r0, jnp.where(sub == 4, r1, jnp.where(sub == 5, r - r0 - r1, 0.0)))
        wide_ref[88:96, :] = jnp.where(sub < 3, jnp.where(tier > sub, OFF, 0.0), parts)
        full.append(dot_nt(eye, wide_ref[...].astype(BF16)).astype(BF16))
    wide_ref[...] = jnp.zeros(wide_ref.shape, F32)
    wide_ref[64:80, 0:react] = st_ref[0:16, :].astype(F32)
    wide_ref[82 : 66 + carried, 0:react] = st_ref[16:carried, :].astype(F32)
    full.append(dot_nt(eye, wide_ref[...].astype(BF16)).astype(BF16))
    base = 0
    for start, size in CHUNKS:
        for part in full:
            w_ref[base : base + size, :] = part[start : start + size]
            base += size


def chem_kernel(
    adj_ref, conc_ref, lev_ref, cond_ref, of_ref, or_ref, st_ref, rf_ref, rr_ref,
    out_ref, coef_ref, tail_ref,
    wide_ref, w_ref, c_ref, conc32_ref, x_ref, act_ref, run_ref,
):
    run_ref[0] = cond_ref[0] - THIRD
    run_ref[1] = jnp.where(lax.axis_index("gx") == 0, MASS + THIRD, BODY) * jnp.ones(run_ref.shape[1:], F32)
    run_ref[2] = jnp.full(run_ref.shape[1:], BODY, F32)
    build_weights(of_ref, or_ref, st_ref, rf_ref, rr_ref, wide_ref, w_ref, c_ref)

    carried, nx, ny, nz = adj_ref.shape
    species = conc_ref.shape[0]
    pitch = nx * ny
    adj_rows = adj_ref.reshape(carried * pitch, nz)
    out_rows = out_ref.reshape(carried * pitch, nz)
    sub = iota((8, nz), 0)

    @pl.loop(0, nx // XB)
    def _(step):
        gap, mass_first, mass = run_ref[0], run_ref[1], run_ref[2]
        for q in range(1, XB + 1):
            p = step * XB + q
            after = cond_ref[jnp.minimum(p, nx - 1)] - THIRD
            inv = 1.0 / (gap + after + mass)
            alpha, beta = gap * inv, after * inv
            coef_ref[0, p], coef_ref[1, p], coef_ref[2, p] = alpha, beta, inv
            mass_first = mass_first + alpha * mass
            mass = BODY + beta * mass
            gap = alpha * after
            tail_ref[p, 0], tail_ref[p, 1], tail_ref[p, 2] = gap, mass_first, mass
        run_ref[0], run_ref[1], run_ref[2] = gap, mass_first, mass

        conc32_ref[...] = conc_ref[:, pl.ds(step * XB, XB)].astype(F32).reshape(species * XB * ny, nz)
        base = step * XB * ny
        for x in range(XB):
            for y in range(ny):
                row = x * ny + y
                cols = slice(row * nz, (row + 1) * nz)
                conc = jnp.concatenate(
                    [conc32_ref[pl.ds(row + 8 * q * XB * ny, 8, stride=XB * ny), :] for q in range(4)], axis=0
                ).astype(BF16)
                x_ref[0:32, cols] = conc
                x_ref[32:64, cols] = conc
                lam = [
                    adj_rows[pl.ds(base + row + first * pitch, 8, stride=pitch), :] for first in (0, 8, carried - 8)
                ]
                level = jnp.broadcast_to(lev_ref[step * XB + x, y : y + 1, :], (8, nz))
                marks = jnp.where(level <= sub, 1.0, 0.0)
                x_ref[64:96, cols] = jnp.concatenate(lam + [marks], axis=0).astype(BF16)
        every = dot(w_ref[...], x_ref[...])
        for start, size in CHUNKS:
            got = every[3 * start : 3 * (start + size)]
            weight = got[2 * size :]
            act_ref[0, start : start + size, :] = (jnp.exp2(got[:size]) * weight).astype(BF16)
            act_ref[1, start : start + size, :] = (jnp.exp2(got[size : 2 * size]) * weight).astype(BF16)
        chem = dot(c_ref[0], act_ref[0]) + dot(c_ref[1], act_ref[1])
        for row in range(XB * ny):
            for q, first in enumerate((0, 8, carried - 8)):
                out_rows[pl.ds(base + row + first * pitch, 8, stride=pitch), :] = chem[
                    8 * q : 8 * q + 8, row * nz : (row + 1) * nz
                ]


def chemistry(adjoint, log_conc, levels, conduct, orders_fwd, orders_rev, stoich, rate_fwd, rate_rev):
    carried, nx, ny, nz = adjoint.shape
    species, react = log_conc.shape[0], orders_fwd.shape[0]
    small = [orders_fwd.T, orders_rev.T, stoich.T, rate_fwd.reshape(1, react), rate_rev.reshape(1, react)]
    return pl.pallas_call(
        chem_kernel,
        in_specs=[WHOLE] * 9,
        out_specs=[WHOLE] * 3,
        out_shape=[
            pltpu.VMEM(adjoint.shape, F32),
            pltpu.VMEM((3, nx + 1, ny, nz), F32),
            pltpu.VMEM((nx + 1, 3, ny, nz), F32),
        ],
        scratch_shapes=[
            pltpu.VMEM((K_ROWS, 256), F32),
            pltpu.VMEM((3 * R_PAD, K_ROWS), BF16),
            pltpu.VMEM((2, 32, R_PAD), BF16),
            pltpu.VMEM((species * XB * ny, nz), F32),
            pltpu.VMEM((K_ROWS, XB * ny * nz), BF16),
            pltpu.VMEM((2, R_PAD, XB * ny * nz), BF16),
            pltpu.VMEM((3, ny, nz), F32),
        ],
        compiler_params=SMALL,
        cost_estimate=pl.CostEstimate(flops=12 * 10**9, bytes_accessed=4 * 10**6, transcendentals=6_750_000),
        name="chem",
    )(adjoint, log_conc, levels, conduct, *small)


GROUP = 6
GROUPS = 4
ROWS = 16
SB = 2
LB = 11
def place(s):
    return s // GROUP * ROWS + s % GROUP


def crossing(adj_ref, s, shifted=False):
    carried, nx, ny, nz = adj_ref.shape
    rows = adj_ref.reshape(carried * nx * ny, nz)
    f0, f1, f6, f7 = [rows[pl.ds(s * nx * ny + r, nx, stride=ny), :] for r in (0, 1, ny - 2, ny - 1)]
    if shifted:
        x = iota((nx, nz), 0)
        ends = (x == 0) | (x == nx - 1)
        f0, f1 = [jnp.where(ends, f, pltpu.roll(f, nx - 1, 0)) for f in (f0, f1)]
        f6, f7 = [jnp.where(ends, f, pltpu.roll(f, 1, 0)) for f in (f6, f7)]
    return (16.0 * f7 - f6, -f7), (-f0, 16.0 * f0 - f1)


def edges_kernel(adj_ref, low_ref, high_ref):
    carried, nx, ny, nz = adj_ref.shape
    mine = lax.axis_index("gy")
    to_high = jnp.where(mine == lax.axis_size("gy") - 1, 0.0, 1.0)
    to_low = jnp.where(mine == 0, 0.0, 1.0)

    @pl.loop(0, carried)
    def _(s):
        down, up = crossing(adj_ref, s)
        for k in range(2):
            low_ref[s, k] = down[k] * to_high
            high_ref[s, k] = up[k] * to_low


def edges(adjoint):
    carried, nx, ny, nz = adjoint.shape
    shape = pltpu.VMEM((carried, 2, nx, nz), F32)
    return pl.pallas_call(
        edges_kernel,
        in_specs=[WHOLE],
        out_specs=[WHOLE, WHOLE],
        out_shape=[shape, shape],
        compiler_params=SMALL,
        cost_estimate=pl.CostEstimate(flops=0, bytes_accessed=2 * 10**6, transcendentals=0),
        name="edges",
    )(adjoint)


def local_kernel(
    diff_ref, cond_ref, adj_ref, chem_ref, near_ref, low_ref, high_ref, coef_ref, tail_ref,
    part_ref, msg_ref, add_ref,
):
    nx, ny, nz = cond_ref.shape
    carried = adj_ref.shape[0]
    stride = GROUPS * ROWS
    msg_ref[...] = jnp.zeros(msg_ref.shape, F32)
    at = nx - 2
    face = cond_ref[nx - 1] - THIRD
    for group in range(GROUPS):
        for r, value in ((6, tail_ref[at, 0]), (7, tail_ref[at, 1]), (14, face), (15, tail_ref[at, 2])):
            msg_ref[pl.ds(group * ROWS + r, ny, stride=stride), :] = value

    add_ref[...] = jnp.zeros(add_ref.shape, F32)
    lane = iota((ny, nz), 1)
    adj_rows = adj_ref.reshape(carried * nx * ny, nz)
    keep_low = jnp.where(lax.axis_index("gz") == 0, 1.0, 0.0)
    keep_high = 1.0 - keep_low

    @pl.loop(0, carried // LB)
    def _(g):
        for t in range(LB):
            s = g * LB + t
            down, up = crossing(adj_ref, s, shifted=True)
            for r, own_term, got in (
                (0, down[0], low_ref[s, 0]),
                (1, down[1], low_ref[s, 1]),
                (ny - 2, up[0], high_ref[s, 0]),
                (ny - 1, up[1], high_ref[s, 1]),
            ):
                add_ref[pl.ds(t * nx * ny + r, nx, stride=ny), :] = got - own_term
        for t in range(LB):
            s = g * LB + t
            scale = diff_ref[s] * (SECTION * STEP / 12.0)
            b_first, carry = None, None
            for p in range(nx):
                own, near = adj_ref[s, p], near_ref[s, p]
                above, below = near * keep_low, near * keep_high
                if 0 < p < nx - 1:
                    row = (s * nx + p) * ny
                    up1, down1, up2, down2 = [adj_rows[pl.ds(row + k, ny), :] for k in (1, -1, 2, -2)]
                else:
                    up1, down1, up2, down2 = [pltpu.roll(own, k % ny, 0) for k in (-1, 1, -2, 2)]
                close = up1 + down1
                close = close + pltpu.roll(jnp.where(lane < 1, above, own), nz - 1, 1)
                close = close + pltpu.roll(jnp.where(lane >= nz - 1, below, own), 1, 1)
                far = up2 + down2
                far = far + pltpu.roll(jnp.where(lane < 2, above, own), nz - 2, 1)
                far = far + pltpu.roll(jnp.where(lane >= nz - 2, below, own), 2, 1)
                at = (t * nx + p) * ny
                spread = 16.0 * close - far - 60.0 * own + add_ref[at : at + ny, :]
                b = SECTION * own + (SECTION * STEP) * chem_ref[s, p] + scale * spread
                if p == 0:
                    b_first = b
                elif p < nx - 1:
                    full = b if carry is None else b + carry
                    part_ref[s, p] = full * coef_ref[2, p]
                    b_first = b_first + coef_ref[0, p] * full
                    carry = coef_ref[1, p] * full
                else:
                    b_last = b + carry
            msg_ref[pl.ds(place(s), ny, stride=stride), :] = b_first
            msg_ref[pl.ds(place(s) + 8, ny, stride=stride), :] = b_last


def local_part(diffusivity, adjoint, chem, near, low, high, conduct, coef, ends):
    carried, nx, ny, nz = adjoint.shape
    smem = pl.BlockSpec(memory_space=pltpu.SMEM)
    return pl.pallas_call(
        local_kernel,
        in_specs=[smem] + [WHOLE] * 8,
        out_specs=[WHOLE] * 2,
        out_shape=[
            pltpu.VMEM(adjoint.shape, F32),
            pltpu.VMEM((GROUPS * ny * ROWS, nz), F32),
        ],
        scratch_shapes=[pltpu.VMEM((LB * nx * ny, nz), F32)],
        compiler_params=SMALL,
        cost_estimate=pl.CostEstimate(flops=20 * 10**6, bytes_accessed=7 * 10**6, transcendentals=0),
        name="local",
    )(diffusivity, conduct, adjoint, chem, near, low, high, coef, ends)


def chain_kernel(in_ref, out_ref):
    count, _, nz = in_ref.shape
    h, mass, rhs, ends = [], [], [], []
    passed_m = passed_b = None
    for i in range(count):
        low, high = in_ref[i, 0:8, :], in_ref[i, 8:16, :]
        g = jnp.broadcast_to(in_ref[i, 6:7, :], (8, nz))
        m_f = jnp.broadcast_to(in_ref[i, 7:8, :], (8, nz))
        face = jnp.broadcast_to(in_ref[i, 14:15, :], (8, nz))
        m_l = jnp.broadcast_to(in_ref[i, 15:16, :], (8, nz))
        inv = 1.0 / (g + face + m_l)
        a, c = g * inv, face * inv
        m, b = m_f + a * m_l, low + a * high
        if i > 0:
            m, b = m + passed_m, b + passed_b
        passed_m, passed_b = c * m_l, c * high
        h.append(a * face)
        mass.append(m)
        rhs.append(b)
        ends.append((a, c, high * inv))
    half = count // 2
    scale, ratio = [None] * count, [None] * count
    for i in range(half - 1):
        inv = 1.0 / (mass[i] + h[i])
        q = h[i] * inv
        scale[i], ratio[i] = rhs[i] * inv, q
        mass[i + 1] = mass[i + 1] + q * mass[i]
        rhs[i + 1] = rhs[i + 1] + q * rhs[i]
    mass[count - 1] = mass[count - 1] + h[count - 1]
    for i in range(count - 1, half, -1):
        inv = 1.0 / (mass[i] + h[i - 1])
        q = h[i - 1] * inv
        scale[i], ratio[i] = rhs[i] * inv, q
        mass[i - 1] = mass[i - 1] + q * mass[i]
        rhs[i - 1] = rhs[i - 1] + q * rhs[i]
    inv = 1.0 / (mass[half - 1] + h[half - 1])
    q = h[half - 1] * inv
    first = [None] * (count + 1)
    first[half] = (rhs[half] + q * rhs[half - 1]) / (mass[half] + q * mass[half - 1])
    first[half - 1] = rhs[half - 1] * inv + q * first[half]
    for i in range(half - 2, -1, -1):
        first[i] = scale[i] + ratio[i] * first[i + 1]
    for i in range(half + 1, count):
        first[i] = scale[i] + ratio[i] * first[i - 1]
    for i in range(count):
        a, c, part = ends[i]
        last = part + a * first[i]
        if i < count - 1:
            last = last + c * first[i + 1]
        out_ref[i, 0] = first[i][0:4]
        out_ref[i, 1, 0:2] = first[i][4:6]
        out_ref[i, 1, 2:4] = last[0:2]
        out_ref[i, 2] = last[2:6]


def chain(message):
    return pl.pallas_call(
        chain_kernel,
        in_specs=[WHOLE],
        out_specs=WHOLE,
        out_shape=pltpu.VMEM((message.shape[0], 3, 4, message.shape[2]), F32),
        compiler_params=SMALL,
        cost_estimate=pl.CostEstimate(flops=10**6, bytes_accessed=10**6, transcendentals=0),
        name="chain",
    )(message)


def back_kernel(coef_ref, got_ref, part_ref, out_hbm, ends_ref, out_ref, out_sem):
    carried, nx, ny, _ = part_ref.shape
    groups = carried // SB
    for i in range(got_ref.shape[0]):
        top = i * ROWS
        ends_ref[top : top + 4, :] = got_ref[i, 0]
        ends_ref[top + 4 : top + 6, :] = got_ref[i, 1, 0:2]
        ends_ref[top + 8 : top + 10, :] = got_ref[i, 1, 2:4]
        ends_ref[top + 10 : top + 14, :] = got_ref[i, 2]

    def put(g):
        return pltpu.make_async_copy(out_ref.at[pl.ds(g * SB, SB)], out_hbm.at[pl.ds(g * SB, SB)], out_sem.at[g])

    @pl.loop(0, groups)
    def _(g):
        for t in range(SB):
            s = g * SB + t
            first = ends_ref[pl.ds(place(s), ny, stride=GROUPS * ROWS), :]
            value = ends_ref[pl.ds(place(s) + 8, ny, stride=GROUPS * ROWS), :]
            out_ref[s, 0] = first
            out_ref[s, nx - 1] = value
            for p in range(nx - 2, 0, -1):
                value = part_ref[s, p] + coef_ref[0, p] * first + coef_ref[1, p] * value
                out_ref[s, p] = value
        @pl.when(g % 2 == 0)
        def _():
            put(g).start(priority=0)

        @pl.when(g % 2 == 1)
        def _():
            put(g).start(priority=1)

    @pl.loop(0, groups)
    def _(g):
        put(g).wait()


def back(part, coef, ends):
    groups = part.shape[0] // SB
    return pl.pallas_call(
        back_kernel,
        in_specs=[WHOLE, WHOLE, WHOLE],
        out_specs=ANY,
        out_shape=jax.ShapeDtypeStruct(part.shape, F32),
        scratch_shapes=[
            pltpu.VMEM((ends.shape[0] * ROWS, part.shape[3]), F32),
            pltpu.VMEM(part.shape, F32),
            pltpu.SemaphoreType.DMA((groups,)),
        ],
        compiler_params=SMALL,
        cost_estimate=pl.CostEstimate(flops=2 * 10**6, bytes_accessed=3 * 10**6, transcendentals=0),
        name="back",
    )(coef, ends, part)


def resident(value):
    return pltpu.with_memory_space_constraint(value, pltpu.VMEM)


def shards(
    adjoint, log_conc, levels, conduct, orders_fwd, orders_rev, stoich, rate_fwd, rate_rev, diffusivity
):
    carried, nx, ny, nz = adjoint.shape
    rows_y, blocks = lax.axis_size("gy"), lax.axis_size("gx")
    near = lax.ppermute(adjoint, "gz", [(0, 1), (1, 0)])
    tail, head = edges(adjoint)
    low = lax.ppermute(tail, "gy", [(i, (i + 1) % rows_y) for i in range(rows_y)])
    high = lax.ppermute(head, "gy", [((i + 1) % rows_y, i) for i in range(rows_y)])
    chem, coef, ends_m = chemistry(adjoint, log_conc, levels, conduct, orders_fwd, orders_rev, stoich, rate_fwd, rate_rev)
    part, message = local_part(diffusivity, adjoint, chem, near, low, high, conduct, coef, ends_m)
    message = lax.all_to_all(message.reshape(blocks, ROWS, nz), "gx", 0, 0, tiled=True)
    ends = lax.all_to_all(chain(message), "gx", 0, 0, tiled=True)
    return back(part, coef, ends)


def solution(mesh):
    cells = P(None, "gx", "gy", "gz")
    planes = P("gx", "gy", "gz")
    in_specs = (cells, cells, planes, planes, P(), P(), P(), P(), P(), P())
    return jax.shard_map(shards, mesh=mesh, in_specs=in_specs, out_specs=cells, check_vma=False)
```

```python
import math

import jax
import jax.numpy as jnp
from jax import lax
from jax.experimental import pallas as pl
from jax.experimental.pallas import tpu as pltpu
from jax.sharding import PartitionSpec as P

SECTION = 0.02
STEP = 0.3
MASS = 0.001
THIRD = MASS / 3.0
BODY = MASS + 2.0 * THIRD
LOG2E = math.log2(math.e)
OFF = -1024.0

K_ROWS = 96
R_PAD = 208
STRIP = 16
CHUNKS = tuple((start, STRIP) for start in range(0, R_PAD, STRIP))
XB = 4
LIMIT = 24 * 1024 * 1024
F32 = jnp.float32
BF16 = jnp.bfloat16


ANY = pl.BlockSpec(memory_space=pl.ANY)
WHOLE = pl.BlockSpec(memory_space=pltpu.VMEM)
SMALL = pltpu.CompilerParams(vmem_limit_bytes=LIMIT)


def iota(shape, dim):
    return lax.broadcasted_iota(jnp.int32, shape, dim)


def dot(a, b):
    return lax.dot_general(a, b, (((1,), (0,)), ((), ())), preferred_element_type=F32)


def dot_nt(a, b):
    return lax.dot_general(a, b, (((1,), (1,)), ((), ())), preferred_element_type=F32)


def one_hot(mask):
    return jnp.where(mask, 1.0, 0.0).astype(BF16)


def build_weights(of_ref, or_ref, st_ref, rf_ref, rr_ref, wide_ref, w_ref, c_ref):
    species, react = of_ref.shape
    carried = st_ref.shape[0]
    eye = one_hot(iota((R_PAD, 256), 0) == iota((R_PAD, 256), 1))
    pick_row, pick_col = iota((32, 32), 0), iota((32, 32), 1)
    pick = one_hot(pick_col == jnp.where(pick_row < 16, pick_row, jnp.where(pick_row < 24, pick_row - 2, -1)))
    sub, tier = iota((8, 256), 0), 4 * iota((8, 256), 1) // react
    full = []
    for index, (orders, rate) in enumerate(((of_ref, rf_ref), (or_ref, rr_ref))):
        wide_ref[...] = jnp.zeros(wide_ref.shape, F32)
        wide_ref[0:species, 0:react] = orders[...].astype(F32)
        plain = wide_ref[0:32, :]
        sign = 1.0 if index == 0 else -1.0
        c_ref[index] = (sign * dot(pick, plain.astype(BF16)))[:, 0:R_PAD].astype(BF16)
        scaled = plain * LOG2E
        hi = scaled.astype(BF16).astype(F32)
        wide_ref[0:32, :] = hi
        wide_ref[32:64, :] = scaled - hi
        wide_ref[88:89, 0:react] = jnp.log(rate[...]) * LOG2E
        r = jnp.broadcast_to(wide_ref[88:89, :], (8, 256))
        r0 = r.astype(BF16).astype(F32)
        r1 = (r - r0).astype(BF16).astype(F32)
        parts = jnp.where(sub == 3, r0, jnp.where(sub == 4, r1, jnp.where(sub == 5, r - r0 - r1, 0.0)))
        wide_ref[88:96, :] = jnp.where(sub < 3, jnp.where(tier > sub, OFF, 0.0), parts)
        full.append(dot_nt(eye, wide_ref[...].astype(BF16)).astype(BF16))
    wide_ref[...] = jnp.zeros(wide_ref.shape, F32)
    wide_ref[64:80, 0:react] = st_ref[0:16, :].astype(F32)
    wide_ref[82 : 66 + carried, 0:react] = st_ref[16:carried, :].astype(F32)
    full.append(dot_nt(eye, wide_ref[...].astype(BF16)).astype(BF16))
    base = 0
    for start, size in CHUNKS:
        for part in full:
            w_ref[base : base + size, :] = part[start : start + size]
            base += size


def chem_kernel(
    adj_ref, conc_ref, lev_ref, cond_ref, of_ref, or_ref, st_ref, rf_ref, rr_ref,
    out_ref, coef_ref, tail_ref,
    wide_ref, w_ref, c_ref, conc32_ref, x_ref, act_ref, run_ref,
):
    run_ref[0] = cond_ref[0] - THIRD
    run_ref[1] = jnp.where(lax.axis_index("gx") == 0, MASS + THIRD, BODY) * jnp.ones(run_ref.shape[1:], F32)
    run_ref[2] = jnp.full(run_ref.shape[1:], BODY, F32)
    build_weights(of_ref, or_ref, st_ref, rf_ref, rr_ref, wide_ref, w_ref, c_ref)

    carried, nx, ny, nz = adj_ref.shape
    species = conc_ref.shape[0]
    pitch = nx * ny
    adj_rows = adj_ref.reshape(carried * pitch, nz)
    out_rows = out_ref.reshape(carried * pitch, nz)
    sub = iota((8, nz), 0)

    @pl.loop(0, nx // XB)
    def _(step):
        gap, mass_first, mass = run_ref[0], run_ref[1], run_ref[2]
        for q in range(1, XB + 1):
            p = step * XB + q
            after = cond_ref[jnp.minimum(p, nx - 1)] - THIRD
            inv = 1.0 / (gap + after + mass)
            alpha, beta = gap * inv, after * inv
            coef_ref[0, p], coef_ref[1, p], coef_ref[2, p] = alpha, beta, inv
            mass_first = mass_first + alpha * mass
            mass = BODY + beta * mass
            gap = alpha * after
            tail_ref[p, 0], tail_ref[p, 1], tail_ref[p, 2] = gap, mass_first, mass
        run_ref[0], run_ref[1], run_ref[2] = gap, mass_first, mass

        conc32_ref[...] = conc_ref[:, pl.ds(step * XB, XB)].astype(F32).reshape(species * XB * ny, nz)
        base = step * XB * ny
        for x in range(XB):
            for y in range(ny):
                row = x * ny + y
                cols = slice(row * nz, (row + 1) * nz)
                conc = jnp.concatenate(
                    [conc32_ref[pl.ds(row + 8 * q * XB * ny, 8, stride=XB * ny), :] for q in range(4)], axis=0
                ).astype(BF16)
                x_ref[0:32, cols] = conc
                x_ref[32:64, cols] = conc
                lam = [
                    adj_rows[pl.ds(base + row + first * pitch, 8, stride=pitch), :] for first in (0, 8, carried - 8)
                ]
                level = jnp.broadcast_to(lev_ref[step * XB + x, y : y + 1, :], (8, nz))
                marks = jnp.where(level <= sub, 1.0, 0.0)
                x_ref[64:96, cols] = jnp.concatenate(lam + [marks], axis=0).astype(BF16)
        every = dot(w_ref[...], x_ref[...])
        for start, size in CHUNKS:
            got = every[3 * start : 3 * (start + size)]
            weight = got[2 * size :]
            act_ref[0, start : start + size, :] = (jnp.exp2(got[:size]) * weight).astype(BF16)
            act_ref[1, start : start + size, :] = (jnp.exp2(got[size : 2 * size]) * weight).astype(BF16)
        chem = dot(c_ref[0], act_ref[0]) + dot(c_ref[1], act_ref[1])
        for row in range(XB * ny):
            for q, first in enumerate((0, 8, carried - 8)):
                out_rows[pl.ds(base + row + first * pitch, 8, stride=pitch), :] = chem[
                    8 * q : 8 * q + 8, row * nz : (row + 1) * nz
                ]


def chemistry(adjoint, log_conc, levels, conduct, orders_fwd, orders_rev, stoich, rate_fwd, rate_rev):
    carried, nx, ny, nz = adjoint.shape
    species, react = log_conc.shape[0], orders_fwd.shape[0]
    small = [orders_fwd.T, orders_rev.T, stoich.T, rate_fwd.reshape(1, react), rate_rev.reshape(1, react)]
    return pl.pallas_call(
        chem_kernel,
        in_specs=[WHOLE] * 9,
        out_specs=[WHOLE] * 3,
        out_shape=[
            pltpu.VMEM(adjoint.shape, F32),
            pltpu.VMEM((3, nx + 1, ny, nz), F32),
            pltpu.VMEM((nx + 1, 3, ny, nz), F32),
        ],
        scratch_shapes=[
            pltpu.VMEM((K_ROWS, 256), F32),
            pltpu.VMEM((3 * R_PAD, K_ROWS), BF16),
            pltpu.VMEM((2, 32, R_PAD), BF16),
            pltpu.VMEM((species * XB * ny, nz), F32),
            pltpu.VMEM((K_ROWS, XB * ny * nz), BF16),
            pltpu.VMEM((2, R_PAD, XB * ny * nz), BF16),
            pltpu.VMEM((3, ny, nz), F32),
        ],
        compiler_params=SMALL,
        cost_estimate=pl.CostEstimate(flops=12 * 10**9, bytes_accessed=4 * 10**6, transcendentals=6_750_000),
        name="chem",
    )(adjoint, log_conc, levels, conduct, *small)


GROUP = 6
GROUPS = 4
ROWS = 16
SB = 2
LB = 11
def place(s):
    return s // GROUP * ROWS + s % GROUP


def crossing(adj_ref, s):
    carried, nx, ny, nz = adj_ref.shape
    rows = adj_ref.reshape(carried * nx * ny, nz)
    f0, f1, f6, f7 = [rows[pl.ds(s * nx * ny + r, nx, stride=ny), :] for r in (0, 1, ny - 2, ny - 1)]
    return (16.0 * f7 - f6, -f7), (-f0, 16.0 * f0 - f1)


def edges_kernel(adj_ref, low_ref, high_ref):
    carried, nx, ny, nz = adj_ref.shape
    mine = lax.axis_index("gy")
    to_high = jnp.where(mine == lax.axis_size("gy") - 1, 0.0, 1.0)
    to_low = jnp.where(mine == 0, 0.0, 1.0)

    @pl.loop(0, carried)
    def _(s):
        down, up = crossing(adj_ref, s)
        for k in range(2):
            low_ref[s, k] = down[k] * to_high
            high_ref[s, k] = up[k] * to_low


def edges(adjoint):
    carried, nx, ny, nz = adjoint.shape
    shape = pltpu.VMEM((carried, 2, nx, nz), F32)
    return pl.pallas_call(
        edges_kernel,
        in_specs=[WHOLE],
        out_specs=[WHOLE, WHOLE],
        out_shape=[shape, shape],
        compiler_params=SMALL,
        cost_estimate=pl.CostEstimate(flops=0, bytes_accessed=2 * 10**6, transcendentals=0),
        name="edges",
    )(adjoint)


def local_kernel(
    diff_ref, cond_ref, adj_ref, chem_ref, near_ref, low_ref, high_ref, coef_ref, tail_ref,
    part_ref, msg_ref, add_ref,
):
    nx, ny, nz = cond_ref.shape
    carried = adj_ref.shape[0]
    stride = GROUPS * ROWS
    msg_ref[...] = jnp.zeros(msg_ref.shape, F32)
    at = nx - 2
    face = cond_ref[nx - 1] - THIRD
    for group in range(GROUPS):
        for r, value in ((6, tail_ref[at, 0]), (7, tail_ref[at, 1]), (14, face), (15, tail_ref[at, 2])):
            msg_ref[pl.ds(group * ROWS + r, ny, stride=stride), :] = value

    add_ref[...] = jnp.zeros(add_ref.shape, F32)
    lane = iota((ny, nz), 1)
    keep_low = jnp.where(lax.axis_index("gz") == 0, 1.0, 0.0)
    keep_high = 1.0 - keep_low

    @pl.loop(0, carried // LB)
    def _(g):
        for t in range(LB):
            s = g * LB + t
            down, up = crossing(adj_ref, s)
            for r, own_term, got in (
                (0, down[0], low_ref[s, 0]),
                (1, down[1], low_ref[s, 1]),
                (ny - 2, up[0], high_ref[s, 0]),
                (ny - 1, up[1], high_ref[s, 1]),
            ):
                add_ref[pl.ds(t * nx * ny + r, nx, stride=ny), :] = got - own_term
        species = [g * LB + t for t in range(LB)]
        scales = [diff_ref[s] * (SECTION * STEP / 12.0) for s in species]
        first, carry = [None] * LB, [None] * LB
        for p in range(nx):
            for t, s in enumerate(species):
                own, near = adj_ref[s, p], near_ref[s, p]
                above, below = near * keep_low, near * keep_high
                close = pltpu.roll(own, ny - 1, 0) + pltpu.roll(own, 1, 0)
                close = close + pltpu.roll(jnp.where(lane < 1, above, own), nz - 1, 1)
                close = close + pltpu.roll(jnp.where(lane >= nz - 1, below, own), 1, 1)
                far = pltpu.roll(own, ny - 2, 0) + pltpu.roll(own, 2, 0)
                far = far + pltpu.roll(jnp.where(lane < 2, above, own), nz - 2, 1)
                far = far + pltpu.roll(jnp.where(lane >= nz - 2, below, own), 2, 1)
                at = (t * nx + p) * ny
                spread = 16.0 * close - far - 60.0 * own + add_ref[at : at + ny, :]
                b = SECTION * own + (SECTION * STEP) * chem_ref[s, p] + scales[t] * spread
                if p == 0:
                    first[t] = b
                elif p < nx - 1:
                    full = b if carry[t] is None else b + carry[t]
                    part_ref[s, p] = full * coef_ref[2, p]
                    first[t] = first[t] + coef_ref[0, p] * full
                    carry[t] = coef_ref[1, p] * full
                else:
                    msg_ref[pl.ds(place(s) + 8, ny, stride=stride), :] = b + carry[t]
        for t, s in enumerate(species):
            msg_ref[pl.ds(place(s), ny, stride=stride), :] = first[t]


def local_part(diffusivity, adjoint, chem, near, low, high, conduct, coef, ends):
    carried, nx, ny, nz = adjoint.shape
    smem = pl.BlockSpec(memory_space=pltpu.SMEM)
    return pl.pallas_call(
        local_kernel,
        in_specs=[smem] + [WHOLE] * 8,
        out_specs=[WHOLE] * 2,
        out_shape=[
            pltpu.VMEM(adjoint.shape, F32),
            pltpu.VMEM((GROUPS * ny * ROWS, nz), F32),
        ],
        scratch_shapes=[pltpu.VMEM((LB * nx * ny, nz), F32)],
        compiler_params=SMALL,
        cost_estimate=pl.CostEstimate(flops=20 * 10**6, bytes_accessed=7 * 10**6, transcendentals=0),
        name="local",
    )(diffusivity, conduct, adjoint, chem, near, low, high, coef, ends)


def chain_kernel(in_ref, out_ref):
    count, _, nz = in_ref.shape
    h, mass, rhs, ends = [], [], [], []
    passed_m = passed_b = None
    for i in range(count):
        low, high = in_ref[i, 0:8, :], in_ref[i, 8:16, :]
        g = jnp.broadcast_to(in_ref[i, 6:7, :], (8, nz))
        m_f = jnp.broadcast_to(in_ref[i, 7:8, :], (8, nz))
        face = jnp.broadcast_to(in_ref[i, 14:15, :], (8, nz))
        m_l = jnp.broadcast_to(in_ref[i, 15:16, :], (8, nz))
        inv = 1.0 / (g + face + m_l)
        a, c = g * inv, face * inv
        m, b = m_f + a * m_l, low + a * high
        if i > 0:
            m, b = m + passed_m, b + passed_b
        passed_m, passed_b = c * m_l, c * high
        h.append(a * face)
        mass.append(m)
        rhs.append(b)
        ends.append((a, c, high * inv))
    half = count // 2
    scale, ratio = [None] * count, [None] * count
    for i in range(half - 1):
        inv = 1.0 / (mass[i] + h[i])
        q = h[i] * inv
        scale[i], ratio[i] = rhs[i] * inv, q
        mass[i + 1] = mass[i + 1] + q * mass[i]
        rhs[i + 1] = rhs[i + 1] + q * rhs[i]
    mass[count - 1] = mass[count - 1] + h[count - 1]
    for i in range(count - 1, half, -1):
        inv = 1.0 / (mass[i] + h[i - 1])
        q = h[i - 1] * inv
        scale[i], ratio[i] = rhs[i] * inv, q
        mass[i - 1] = mass[i - 1] + q * mass[i]
        rhs[i - 1] = rhs[i - 1] + q * rhs[i]
    inv = 1.0 / (mass[half - 1] + h[half - 1])
    q = h[half - 1] * inv
    first = [None] * (count + 1)
    first[half] = (rhs[half] + q * rhs[half - 1]) / (mass[half] + q * mass[half - 1])
    first[half - 1] = rhs[half - 1] * inv + q * first[half]
    for i in range(half - 2, -1, -1):
        first[i] = scale[i] + ratio[i] * first[i + 1]
    for i in range(half + 1, count):
        first[i] = scale[i] + ratio[i] * first[i - 1]
    for i in range(count):
        a, c, part = ends[i]
        last = part + a * first[i]
        if i < count - 1:
            last = last + c * first[i + 1]
        out_ref[i, 0] = first[i][0:4]
        out_ref[i, 1, 0:2] = first[i][4:6]
        out_ref[i, 1, 2:4] = last[0:2]
        out_ref[i, 2] = last[2:6]


def chain(message):
    return pl.pallas_call(
        chain_kernel,
        in_specs=[WHOLE],
        out_specs=WHOLE,
        out_shape=pltpu.VMEM((message.shape[0], 3, 4, message.shape[2]), F32),
        compiler_params=SMALL,
        cost_estimate=pl.CostEstimate(flops=10**6, bytes_accessed=10**6, transcendentals=0),
        name="chain",
    )(message)


def back_kernel(coef_ref, got_ref, part_ref, out_hbm, ends_ref, out_ref, out_sem):
    carried, nx, ny, _ = part_ref.shape
    groups = carried // SB
    for i in range(got_ref.shape[0]):
        top = i * ROWS
        ends_ref[top : top + 4, :] = got_ref[i, 0]
        ends_ref[top + 4 : top + 6, :] = got_ref[i, 1, 0:2]
        ends_ref[top + 8 : top + 10, :] = got_ref[i, 1, 2:4]
        ends_ref[top + 10 : top + 14, :] = got_ref[i, 2]

    def put(g):
        return pltpu.make_async_copy(out_ref.at[pl.ds(g * SB, SB)], out_hbm.at[pl.ds(g * SB, SB)], out_sem.at[g])

    @pl.loop(0, groups)
    def _(g):
        for t in range(SB):
            s = g * SB + t
            first = ends_ref[pl.ds(place(s), ny, stride=GROUPS * ROWS), :]
            value = ends_ref[pl.ds(place(s) + 8, ny, stride=GROUPS * ROWS), :]
            out_ref[s, 0] = first
            out_ref[s, nx - 1] = value
            for p in range(nx - 2, 0, -1):
                value = part_ref[s, p] + coef_ref[0, p] * first + coef_ref[1, p] * value
                out_ref[s, p] = value
        @pl.when(g % 2 == 0)
        def _():
            put(g).start(priority=0)

        @pl.when(g % 2 == 1)
        def _():
            put(g).start(priority=1)

    @pl.loop(0, groups)
    def _(g):
        put(g).wait()


def back(part, coef, ends):
    groups = part.shape[0] // SB
    return pl.pallas_call(
        back_kernel,
        in_specs=[WHOLE, WHOLE, WHOLE],
        out_specs=ANY,
        out_shape=jax.ShapeDtypeStruct(part.shape, F32),
        scratch_shapes=[
            pltpu.VMEM((ends.shape[0] * ROWS, part.shape[3]), F32),
            pltpu.VMEM(part.shape, F32),
            pltpu.SemaphoreType.DMA((groups,)),
        ],
        compiler_params=SMALL,
        cost_estimate=pl.CostEstimate(flops=2 * 10**6, bytes_accessed=3 * 10**6, transcendentals=0),
        name="back",
    )(coef, ends, part)


def resident(value):
    return pltpu.with_memory_space_constraint(value, pltpu.VMEM)


def shards(
    adjoint, log_conc, levels, conduct, orders_fwd, orders_rev, stoich, rate_fwd, rate_rev, diffusivity
):
    carried, nx, ny, nz = adjoint.shape
    rows_y, blocks = lax.axis_size("gy"), lax.axis_size("gx")
    near = lax.ppermute(adjoint, "gz", [(0, 1), (1, 0)])
    tail, head = edges(adjoint)
    low = lax.ppermute(tail, "gy", [(i, (i + 1) % rows_y) for i in range(rows_y)])
    high = lax.ppermute(head, "gy", [((i + 1) % rows_y, i) for i in range(rows_y)])
    chem, coef, ends_m = chemistry(adjoint, log_conc, levels, conduct, orders_fwd, orders_rev, stoich, rate_fwd, rate_rev)
    part, message = local_part(diffusivity, adjoint, chem, near, low, high, conduct, coef, ends_m)
    message = lax.all_to_all(message.reshape(blocks, ROWS, nz), "gx", 0, 0, tiled=True)
    ends = lax.all_to_all(chain(message), "gx", 0, 0, tiled=True)
    return back(part, coef, ends)


def solution(mesh):
    cells = P(None, "gx", "gy", "gz")
    planes = P("gx", "gy", "gz")
    in_specs = (cells, cells, planes, planes, P(), P(), P(), P(), P(), P())
    return jax.shard_map(shards, mesh=mesh, in_specs=in_specs, out_specs=cells, check_vma=False)
```

```python
import math

import jax
import jax.numpy as jnp
from jax import lax
from jax.experimental import pallas as pl
from jax.experimental.pallas import tpu as pltpu
from jax.sharding import PartitionSpec as P

SECTION = 0.02
STEP = 0.3
MASS = 0.001
THIRD = MASS / 3.0
BODY = MASS + 2.0 * THIRD
LOG2E = math.log2(math.e)
OFF = -1024.0

K_ROWS = 96
R_PAD = 208
STRIP = 16
CHUNKS = tuple((start, STRIP) for start in range(0, R_PAD, STRIP))
XB = 4
LIMIT = 24 * 1024 * 1024
F32 = jnp.float32
BF16 = jnp.bfloat16


ANY = pl.BlockSpec(memory_space=pl.ANY)
WHOLE = pl.BlockSpec(memory_space=pltpu.VMEM)
SMALL = pltpu.CompilerParams(vmem_limit_bytes=LIMIT)


def iota(shape, dim):
    return lax.broadcasted_iota(jnp.int32, shape, dim)


def dot(a, b):
    return lax.dot_general(a, b, (((1,), (0,)), ((), ())), preferred_element_type=F32)


def dot_nt(a, b):
    return lax.dot_general(a, b, (((1,), (1,)), ((), ())), preferred_element_type=F32)


def one_hot(mask):
    return jnp.where(mask, 1.0, 0.0).astype(BF16)


def build_weights(of_ref, or_ref, st_ref, rf_ref, rr_ref, wide_ref, w_ref, c_ref):
    species, react = of_ref.shape
    carried = st_ref.shape[0]
    eye = one_hot(iota((R_PAD, 256), 0) == iota((R_PAD, 256), 1))
    pick_row, pick_col = iota((32, 32), 0), iota((32, 32), 1)
    pick = one_hot(pick_col == jnp.where(pick_row < 16, pick_row, jnp.where(pick_row < 24, pick_row - 2, -1)))
    sub, tier = iota((8, 256), 0), 4 * iota((8, 256), 1) // react
    full = []
    for index, (orders, rate) in enumerate(((of_ref, rf_ref), (or_ref, rr_ref))):
        wide_ref[...] = jnp.zeros(wide_ref.shape, F32)
        wide_ref[0:species, 0:react] = orders[...].astype(F32)
        plain = wide_ref[0:32, :]
        sign = 1.0 if index == 0 else -1.0
        c_ref[index] = (sign * dot(pick, plain.astype(BF16)))[:, 0:R_PAD].astype(BF16)
        scaled = plain * LOG2E
        hi = scaled.astype(BF16).astype(F32)
        wide_ref[0:32, :] = hi
        wide_ref[32:64, :] = scaled - hi
        wide_ref[88:89, 0:react] = jnp.log(rate[...]) * LOG2E
        r = jnp.broadcast_to(wide_ref[88:89, :], (8, 256))
        r0 = r.astype(BF16).astype(F32)
        r1 = (r - r0).astype(BF16).astype(F32)
        parts = jnp.where(sub == 3, r0, jnp.where(sub == 4, r1, jnp.where(sub == 5, r - r0 - r1, 0.0)))
        wide_ref[88:96, :] = jnp.where(sub < 3, jnp.where(tier > sub, OFF, 0.0), parts)
        full.append(dot_nt(eye, wide_ref[...].astype(BF16)).astype(BF16))
    wide_ref[...] = jnp.zeros(wide_ref.shape, F32)
    wide_ref[64:80, 0:react] = st_ref[0:16, :].astype(F32)
    wide_ref[82 : 66 + carried, 0:react] = st_ref[16:carried, :].astype(F32)
    full.append(dot_nt(eye, wide_ref[...].astype(BF16)).astype(BF16))
    base = 0
    for start, size in CHUNKS:
        for part in full:
            w_ref[base : base + size, :] = part[start : start + size]
            base += size


def chem_kernel(
    adj_ref, conc_ref, lev_ref, cond_ref, of_ref, or_ref, st_ref, rf_ref, rr_ref,
    out_ref, coef_ref, tail_ref,
    wide_ref, w_ref, c_ref, conc32_ref, x_ref, act_ref, run_ref,
):
    run_ref[0] = cond_ref[0] - THIRD
    run_ref[1] = jnp.where(lax.axis_index("gx") == 0, MASS + THIRD, BODY) * jnp.ones(run_ref.shape[1:], F32)
    run_ref[2] = jnp.full(run_ref.shape[1:], BODY, F32)
    build_weights(of_ref, or_ref, st_ref, rf_ref, rr_ref, wide_ref, w_ref, c_ref)

    carried, nx, ny, nz = adj_ref.shape
    species = conc_ref.shape[0]
    pitch = nx * ny
    adj_rows = adj_ref.reshape(carried * pitch, nz)
    out_rows = out_ref.reshape(carried * pitch, nz)
    sub = iota((8, nz), 0)

    @pl.loop(0, nx // XB)
    def _(step):
        gap, mass_first, mass = run_ref[0], run_ref[1], run_ref[2]
        for q in range(1, XB + 1):
            p = step * XB + q
            after = cond_ref[jnp.minimum(p, nx - 1)] - THIRD
            inv = 1.0 / (gap + after + mass)
            alpha, beta = gap * inv, after * inv
            coef_ref[0, p], coef_ref[1, p], coef_ref[2, p] = alpha, beta, inv
            mass_first = mass_first + alpha * mass
            mass = BODY + beta * mass
            gap = alpha * after
            tail_ref[p, 0], tail_ref[p, 1], tail_ref[p, 2] = gap, mass_first, mass
        run_ref[0], run_ref[1], run_ref[2] = gap, mass_first, mass

        conc32_ref[...] = conc_ref[:, pl.ds(step * XB, XB)].astype(F32).reshape(species * XB * ny, nz)
        base = step * XB * ny
        for x in range(XB):
            for y in range(ny):
                row = x * ny + y
                cols = slice(row * nz, (row + 1) * nz)
                conc = jnp.concatenate(
                    [conc32_ref[pl.ds(row + 8 * q * XB * ny, 8, stride=XB * ny), :] for q in range(4)], axis=0
                ).astype(BF16)
                x_ref[0:32, cols] = conc
                x_ref[32:64, cols] = conc
                lam = [
                    adj_rows[pl.ds(base + row + first * pitch, 8, stride=pitch), :] for first in (0, 8, carried - 8)
                ]
                level = jnp.broadcast_to(lev_ref[step * XB + x, y : y + 1, :], (8, nz))
                marks = jnp.where(level <= sub, 1.0, 0.0)
                x_ref[64:96, cols] = jnp.concatenate(lam + [marks], axis=0).astype(BF16)
        every = dot(w_ref[...], x_ref[...])
        for start, size in CHUNKS:
            got = every[3 * start : 3 * (start + size)]
            weight = got[2 * size :]
            act_ref[0, start : start + size, :] = (jnp.exp2(got[:size]) * weight).astype(BF16)
            act_ref[1, start : start + size, :] = (jnp.exp2(got[size : 2 * size]) * weight).astype(BF16)
        chem = dot(c_ref[0], act_ref[0]) + dot(c_ref[1], act_ref[1])
        for row in range(XB * ny):
            for q, first in enumerate((0, 8, carried - 8)):
                out_rows[pl.ds(base + row + first * pitch, 8, stride=pitch), :] = chem[
                    8 * q : 8 * q + 8, row * nz : (row + 1) * nz
                ]


def chemistry(adjoint, log_conc, levels, conduct, orders_fwd, orders_rev, stoich, rate_fwd, rate_rev):
    carried, nx, ny, nz = adjoint.shape
    species, react = log_conc.shape[0], orders_fwd.shape[0]
    small = [orders_fwd.T, orders_rev.T, stoich.T, rate_fwd.reshape(1, react), rate_rev.reshape(1, react)]
    return pl.pallas_call(
        chem_kernel,
        in_specs=[WHOLE] * 9,
        out_specs=[WHOLE] * 3,
        out_shape=[
            pltpu.VMEM(adjoint.shape, F32),
            pltpu.VMEM((3, nx + 1, ny, nz), F32),
            pltpu.VMEM((nx + 1, 3, ny, nz), F32),
        ],
        scratch_shapes=[
            pltpu.VMEM((K_ROWS, 256), F32),
            pltpu.VMEM((3 * R_PAD, K_ROWS), BF16),
            pltpu.VMEM((2, 32, R_PAD), BF16),
            pltpu.VMEM((species * XB * ny, nz), F32),
            pltpu.VMEM((K_ROWS, XB * ny * nz), BF16),
            pltpu.VMEM((2, R_PAD, XB * ny * nz), BF16),
            pltpu.VMEM((3, ny, nz), F32),
        ],
        compiler_params=SMALL,
        cost_estimate=pl.CostEstimate(flops=12 * 10**9, bytes_accessed=4 * 10**6, transcendentals=6_750_000),
        name="chem",
    )(adjoint, log_conc, levels, conduct, *small)


GROUP = 6
GROUPS = 4
ROWS = 16
SB = 1
LB = 22
def place(s):
    return s // GROUP * ROWS + s % GROUP


def crossing(adj_ref, s):
    carried, nx, ny, nz = adj_ref.shape
    rows = adj_ref.reshape(carried * nx * ny, nz)
    f0, f1, f6, f7 = [rows[pl.ds(s * nx * ny + r, nx, stride=ny), :] for r in (0, 1, ny - 2, ny - 1)]
    return (16.0 * f7 - f6, -f7), (-f0, 16.0 * f0 - f1)


def edges_kernel(adj_ref, low_ref, high_ref):
    carried, nx, ny, nz = adj_ref.shape
    mine = lax.axis_index("gy")
    to_high = jnp.where(mine == lax.axis_size("gy") - 1, 0.0, 1.0)
    to_low = jnp.where(mine == 0, 0.0, 1.0)

    @pl.loop(0, carried)
    def _(s):
        down, up = crossing(adj_ref, s)
        for k in range(2):
            low_ref[s, k] = down[k] * to_high
            high_ref[s, k] = up[k] * to_low


def edges(adjoint):
    carried, nx, ny, nz = adjoint.shape
    shape = pltpu.VMEM((carried, 2, nx, nz), F32)
    return pl.pallas_call(
        edges_kernel,
        in_specs=[WHOLE],
        out_specs=[WHOLE, WHOLE],
        out_shape=[shape, shape],
        compiler_params=SMALL,
        cost_estimate=pl.CostEstimate(flops=0, bytes_accessed=2 * 10**6, transcendentals=0),
        name="edges",
    )(adjoint)


def local_kernel(
    diff_ref, cond_ref, adj_ref, chem_ref, near_ref, low_ref, high_ref, coef_ref, tail_ref,
    part_ref, msg_ref, add_ref,
):
    nx, ny, nz = cond_ref.shape
    carried = adj_ref.shape[0]
    stride = GROUPS * ROWS
    msg_ref[...] = jnp.zeros(msg_ref.shape, F32)
    at = nx - 2
    face = cond_ref[nx - 1] - THIRD
    for group in range(GROUPS):
        for r, value in ((6, tail_ref[at, 0]), (7, tail_ref[at, 1]), (14, face), (15, tail_ref[at, 2])):
            msg_ref[pl.ds(group * ROWS + r, ny, stride=stride), :] = value

    add_ref[...] = jnp.zeros(add_ref.shape, F32)
    lane = iota((ny, nz), 1)
    keep_low = jnp.where(lax.axis_index("gz") == 0, 1.0, 0.0)
    keep_high = 1.0 - keep_low

    @pl.loop(0, carried // LB)
    def _(g):
        for t in range(LB):
            s = g * LB + t
            down, up = crossing(adj_ref, s)
            for r, own_term, got in (
                (0, down[0], low_ref[s, 0]),
                (1, down[1], low_ref[s, 1]),
                (ny - 2, up[0], high_ref[s, 0]),
                (ny - 1, up[1], high_ref[s, 1]),
            ):
                add_ref[pl.ds(t * nx * ny + r, nx, stride=ny), :] = got - own_term
        for t in range(LB):
            s = g * LB + t
            scale = diff_ref[s] * (SECTION * STEP / 12.0)
            b_first, carry = None, None
            for p in range(nx):
                own, near = adj_ref[s, p], near_ref[s, p]
                above, below = near * keep_low, near * keep_high
                close = pltpu.roll(own, ny - 1, 0) + pltpu.roll(own, 1, 0)
                close = close + pltpu.roll(jnp.where(lane < 1, above, own), nz - 1, 1)
                close = close + pltpu.roll(jnp.where(lane >= nz - 1, below, own), 1, 1)
                far = pltpu.roll(own, ny - 2, 0) + pltpu.roll(own, 2, 0)
                far = far + pltpu.roll(jnp.where(lane < 2, above, own), nz - 2, 1)
                far = far + pltpu.roll(jnp.where(lane >= nz - 2, below, own), 2, 1)
                at = (t * nx + p) * ny
                spread = 16.0 * close - far - 60.0 * own + add_ref[at : at + ny, :]
                b = SECTION * own + (SECTION * STEP) * chem_ref[s, p] + scale * spread
                if p == 0:
                    b_first = b
                elif p < nx - 1:
                    full = b if carry is None else b + carry
                    part_ref[s, p] = full * coef_ref[2, p]
                    b_first = b_first + coef_ref[0, p] * full
                    carry = coef_ref[1, p] * full
                else:
                    b_last = b + carry
            msg_ref[pl.ds(place(s), ny, stride=stride), :] = b_first
            msg_ref[pl.ds(place(s) + 8, ny, stride=stride), :] = b_last


def local_part(diffusivity, adjoint, chem, near, low, high, conduct, coef, ends):
    carried, nx, ny, nz = adjoint.shape
    smem = pl.BlockSpec(memory_space=pltpu.SMEM)
    return pl.pallas_call(
        local_kernel,
        in_specs=[smem] + [WHOLE] * 8,
        out_specs=[WHOLE] * 2,
        out_shape=[
            pltpu.VMEM(adjoint.shape, F32),
            pltpu.VMEM((GROUPS * ny * ROWS, nz), F32),
        ],
        scratch_shapes=[pltpu.VMEM((LB * nx * ny, nz), F32)],
        compiler_params=SMALL,
        cost_estimate=pl.CostEstimate(flops=20 * 10**6, bytes_accessed=7 * 10**6, transcendentals=0),
        name="local",
    )(diffusivity, conduct, adjoint, chem, near, low, high, coef, ends)


def chain_kernel(in_ref, out_ref):
    count, _, nz = in_ref.shape
    h, mass, rhs, ends = [], [], [], []
    passed_m = passed_b = None
    for i in range(count):
        low, high = in_ref[i, 0:8, :], in_ref[i, 8:16, :]
        g = jnp.broadcast_to(in_ref[i, 6:7, :], (8, nz))
        m_f = jnp.broadcast_to(in_ref[i, 7:8, :], (8, nz))
        face = jnp.broadcast_to(in_ref[i, 14:15, :], (8, nz))
        m_l = jnp.broadcast_to(in_ref[i, 15:16, :], (8, nz))
        inv = 1.0 / (g + face + m_l)
        a, c = g * inv, face * inv
        m, b = m_f + a * m_l, low + a * high
        if i > 0:
            m, b = m + passed_m, b + passed_b
        passed_m, passed_b = c * m_l, c * high
        h.append(a * face)
        mass.append(m)
        rhs.append(b)
        ends.append((a, c, high * inv))
    half = count // 2
    scale, ratio = [None] * count, [None] * count
    for i in range(half - 1):
        inv = 1.0 / (mass[i] + h[i])
        q = h[i] * inv
        scale[i], ratio[i] = rhs[i] * inv, q
        mass[i + 1] = mass[i + 1] + q * mass[i]
        rhs[i + 1] = rhs[i + 1] + q * rhs[i]
    mass[count - 1] = mass[count - 1] + h[count - 1]
    for i in range(count - 1, half, -1):
        inv = 1.0 / (mass[i] + h[i - 1])
        q = h[i - 1] * inv
        scale[i], ratio[i] = rhs[i] * inv, q
        mass[i - 1] = mass[i - 1] + q * mass[i]
        rhs[i - 1] = rhs[i - 1] + q * rhs[i]
    inv = 1.0 / (mass[half - 1] + h[half - 1])
    q = h[half - 1] * inv
    first = [None] * (count + 1)
    first[half] = (rhs[half] + q * rhs[half - 1]) / (mass[half] + q * mass[half - 1])
    first[half - 1] = rhs[half - 1] * inv + q * first[half]
    for i in range(half - 2, -1, -1):
        first[i] = scale[i] + ratio[i] * first[i + 1]
    for i in range(half + 1, count):
        first[i] = scale[i] + ratio[i] * first[i - 1]
    for i in range(count):
        a, c, part = ends[i]
        last = part + a * first[i]
        if i < count - 1:
            last = last + c * first[i + 1]
        out_ref[i, 0] = first[i][0:4]
        out_ref[i, 1, 0:2] = first[i][4:6]
        out_ref[i, 1, 2:4] = last[0:2]
        out_ref[i, 2] = last[2:6]


def chain(message):
    return pl.pallas_call(
        chain_kernel,
        in_specs=[WHOLE],
        out_specs=WHOLE,
        out_shape=pltpu.VMEM((message.shape[0], 3, 4, message.shape[2]), F32),
        compiler_params=SMALL,
        cost_estimate=pl.CostEstimate(flops=10**6, bytes_accessed=10**6, transcendentals=0),
        name="chain",
    )(message)


def back_kernel(coef_ref, got_ref, part_ref, out_hbm, ends_ref, out_ref, out_sem):
    carried, nx, ny, _ = part_ref.shape
    groups = carried // SB
    for i in range(got_ref.shape[0]):
        top = i * ROWS
        ends_ref[top : top + 4, :] = got_ref[i, 0]
        ends_ref[top + 4 : top + 6, :] = got_ref[i, 1, 0:2]
        ends_ref[top + 8 : top + 10, :] = got_ref[i, 1, 2:4]
        ends_ref[top + 10 : top + 14, :] = got_ref[i, 2]

    def put(g):
        return pltpu.make_async_copy(out_ref.at[pl.ds(g * SB, SB)], out_hbm.at[pl.ds(g * SB, SB)], out_sem.at[g])

    @pl.loop(0, groups)
    def _(g):
        for t in range(SB):
            s = g * SB + t
            first = ends_ref[pl.ds(place(s), ny, stride=GROUPS * ROWS), :]
            value = ends_ref[pl.ds(place(s) + 8, ny, stride=GROUPS * ROWS), :]
            out_ref[s, 0] = first
            out_ref[s, nx - 1] = value
            for p in range(nx - 2, 0, -1):
                value = part_ref[s, p] + coef_ref[0, p] * first + coef_ref[1, p] * value
                out_ref[s, p] = value
        @pl.when(g % 2 == 0)
        def _():
            put(g).start(priority=0)

        @pl.when(g % 2 == 1)
        def _():
            put(g).start(priority=1)

    @pl.loop(0, groups)
    def _(g):
        put(g).wait()


def back(part, coef, ends):
    groups = part.shape[0] // SB
    return pl.pallas_call(
        back_kernel,
        in_specs=[WHOLE, WHOLE, WHOLE],
        out_specs=ANY,
        out_shape=jax.ShapeDtypeStruct(part.shape, F32),
        scratch_shapes=[
            pltpu.VMEM((ends.shape[0] * ROWS, part.shape[3]), F32),
            pltpu.VMEM(part.shape, F32),
            pltpu.SemaphoreType.DMA((groups,)),
        ],
        compiler_params=SMALL,
        cost_estimate=pl.CostEstimate(flops=2 * 10**6, bytes_accessed=3 * 10**6, transcendentals=0),
        name="back",
    )(coef, ends, part)


def resident(value):
    return pltpu.with_memory_space_constraint(value, pltpu.VMEM)


def shards(
    adjoint, log_conc, levels, conduct, orders_fwd, orders_rev, stoich, rate_fwd, rate_rev, diffusivity
):
    carried, nx, ny, nz = adjoint.shape
    rows_y, blocks = lax.axis_size("gy"), lax.axis_size("gx")
    near = lax.ppermute(adjoint, "gz", [(0, 1), (1, 0)])
    tail, head = edges(adjoint)
    low = lax.ppermute(tail, "gy", [(i, (i + 1) % rows_y) for i in range(rows_y)])
    high = lax.ppermute(head, "gy", [((i + 1) % rows_y, i) for i in range(rows_y)])
    chem, coef, ends_m = chemistry(adjoint, log_conc, levels, conduct, orders_fwd, orders_rev, stoich, rate_fwd, rate_rev)
    part, message = local_part(diffusivity, adjoint, chem, near, low, high, conduct, coef, ends_m)
    message = lax.all_to_all(message.reshape(blocks, ROWS, nz), "gx", 0, 0, tiled=True)
    ends = lax.all_to_all(chain(message), "gx", 0, 0, tiled=True)
    return back(part, coef, ends)


def solution(mesh):
    cells = P(None, "gx", "gy", "gz")
    planes = P("gx", "gy", "gz")
    in_specs = (cells, cells, planes, planes, P(), P(), P(), P(), P(), P())
    return jax.shard_map(shards, mesh=mesh, in_specs=in_specs, out_specs=cells, check_vma=False)
```
